32 devices in a mesh: ctx: 16 (over z, y, x), head: 2 (over core).
Axes of the slice: x: 2, y: 2, z: 4, core: 2. Of those that a mesh axis runs over, the one named last changes fastest.
Arguments:
- queries: bfloat16 [4096, 8192], P(('ctx', 'head')), may hold values from -64 to 64
- keys: bfloat16 [4096, 1024], P(('ctx', 'head')), may hold values from -64 to 64
- values: bfloat16 [4096, 1024], P(('ctx', 'head')), may hold values from -6 to 6
- doc_lengths: int32 [12], replicated, may hold values from 1 to 1024, as said below
Outputs:
- attended: bfloat16 [4096, 8192], P(('ctx', 'head'))
The draws below stay inside these ranges and needn't reach their ends.
Inputs may be any that keep to these rules, and one draw needn't show every extreme that they name: `doc_lengths`: the lengths sum to 4096; the first document has one token, the second exactly 1024, and no other more than 1024.
All inputs are finite; a program needn't handle non-finite values.
Results may differ from the reference program's by a relative error of at most 0.004.
Values may be sent and summed in bfloat16 or wider, within the bound.
No kernel may reach another device: no remote copies, remote signals or barrier semaphores. Data moves between devices by JAX's collectives and lax.ppermute only.
A program may use at most 64 MiB of HBM per device.

```python
import jax
import jax.numpy as jnp
from jax import lax

H = 64
KVH = 8
HD = 128
REACH = 4
SPAN = 256
SEQ = 4096
DOCS = 12
MOST = 1024


def draw_queries(key, part):
    drawn = jnp.clip(jax.random.normal(jax.random.fold_in(key, 1), (SEQ, H * HD), jnp.float32), -6.0, 6.0)
    return drawn.astype(jnp.bfloat16)


def draw_keys(key, part):
    drawn = jnp.clip(jax.random.normal(jax.random.fold_in(key, 2), (SEQ, KVH * HD), jnp.float32), -6.0, 6.0)
    return drawn.astype(jnp.bfloat16)


def draw_doc_lengths(key, part):
    count = DOCS - 2
    remaining = SEQ - MOST - 1
    index_list = jnp.arange(count, dtype=jnp.int32)
    lengths = (remaining // count + (index_list < remaining % count).astype(jnp.int32)).astype(jnp.int32)
    half = count // 2
    for round_number in range(8):
        round_key = jax.random.fold_in(key, 100 + round_number)
        order = jax.random.permutation(jax.random.fold_in(round_key, 1), count)
        left = order[:half]
        right = order[half:2 * half]
        room = jnp.minimum(MOST - lengths[left], lengths[right] - 1)
        fraction = jax.random.randint(jax.random.fold_in(round_key, 2), (half,), 0, 1001, dtype=jnp.int32)
        moved = room * fraction // 1000
        lengths = lengths.at[left].add(moved).at[right].add(-moved)
    head_part = jnp.array([1, MOST], dtype=jnp.int32)
    return jnp.concatenate([head_part, lengths.astype(jnp.int32)]).astype(jnp.int32)


def level_of(stream_key, dims, pieces, least, top_value):
    gain, own = 1.0, jax.random.fold_in(stream_key, 6)
    for axis_at, parts in pieces:
        draws = jnp.exp(jax.random.uniform(jax.random.fold_in(own, axis_at), (parts,), jnp.float32, least / len(pieces), top_value / len(pieces)))
        gain = gain * jnp.repeat(draws, dims[axis_at] // parts).reshape([-1 if axis == axis_at else 1 for axis in range(len(dims))])
    return gain


def centred(own_key, extent, scale, bound, pieces=(), kind=jnp.bfloat16):
    entries = scale * jax.random.normal(own_key, extent, jnp.float32)
    if pieces:
        entries = entries * level_of(own_key, extent, pieces, -0.22, 0.18)
    return jnp.clip(entries, -bound, bound).astype(kind)


def setup_inputs(seed: int = 0) -> dict:
    key_of = jax.random.split(jax.random.key(seed), 5)
    return {
        "queries": draw_queries(jax.random.fold_in(key_of[4], 71), 0),
        "keys": draw_keys(jax.random.fold_in(key_of[4], 71), 0),
        "values": centred(key_of[2], (SEQ, KVH * HD), 1.0, 6.0, ((0, 32),)),
        "doc_lengths": draw_doc_lengths(jax.random.fold_in(key_of[4], 71), 0),
    }


def doc_index(positions, doc_ends):
    return jnp.sum((doc_ends[None, :] <= positions[:, None]).astype(jnp.int32), axis=1)


def reference(queries, keys, values, doc_lengths):
    doc_ends = jnp.cumsum(doc_lengths).astype(jnp.int32)
    group_size = H // KVH
    query_rows = min(256, SPAN)
    padding = REACH * SPAN
    window = padding + query_rows
    score_scale = HD ** -0.5
    keys_padded = jnp.concatenate([jnp.zeros((padding, KVH * HD), keys.dtype), keys], axis=0)
    values_padded = jnp.concatenate([jnp.zeros((padding, KVH * HD), values.dtype), values], axis=0)

    def one_block(block_index):
        offset = (block_index * query_rows).astype(jnp.int32)
        query_block = lax.dynamic_slice_in_dim(queries, offset, query_rows, 0)
        query_block = query_block.reshape(query_rows, KVH, group_size, HD).astype(jnp.float32)
        key_block = lax.dynamic_slice_in_dim(keys_padded, offset, window, 0)
        key_block = key_block.reshape(window, KVH, HD).astype(jnp.float32)
        value_block = lax.dynamic_slice_in_dim(values_padded, offset, window, 0)
        value_block = value_block.reshape(window, KVH, HD).astype(jnp.float32)
        query_pos = offset + jnp.arange(query_rows, dtype=jnp.int32)
        key_pos = offset - padding + jnp.arange(window, dtype=jnp.int32)
        allowed = (doc_index(query_pos, doc_ends)[:, None] == doc_index(key_pos, doc_ends)[None, :])
        allowed = allowed & (key_pos[None, :] <= query_pos[:, None]) & (key_pos[None, :] >= 0)
        wide = allowed[:, None, None, :]
        scores = jnp.einsum('qkgd,skd->qkgs', query_block, key_block) * score_scale
        row_max = jnp.max(jnp.where(wide, scores, jnp.float32(-1e30)), axis=-1, keepdims=True)
        weights = jnp.where(wide, jnp.exp(scores - row_max), jnp.float32(0.0))
        row_sum = jnp.sum(weights, axis=-1)
        rounded = lax.optimization_barrier(weights.astype(jnp.bfloat16)).astype(jnp.float32)
        output = jnp.einsum('qkgs,skd->qkgd', rounded, value_block) / row_sum[..., None]
        return output.reshape(query_rows, H * HD).astype(jnp.bfloat16)

    blocks = lax.map(one_block, jnp.arange(SEQ // query_rows, dtype=jnp.int32))
    return blocks.reshape(SEQ, H * HD)
```

```python
import functools
import math

import jax
import jax.numpy as jnp
from jax import lax
from jax.experimental import pallas as pl
from jax.experimental.pallas import tpu as pltpu
from jax.sharding import PartitionSpec as P

HD = 128
REACH = 4
NEVER = -1e30


def from_behind(block, axis, distance):
    devices = range(lax.axis_size(axis))
    route = [(i - distance, i) for i in devices if i - distance in devices]
    return lax.ppermute(block, axis, route)


def attend_kernel(place_ref, lengths_ref, q_ref, *refs, group_size, heads_per_chunk):
    kv_refs, (out_ref, lo_ref, max_ref, acc_ref) = refs[:-4], refs[-4:]
    rows = q_ref.shape[0]
    span_rows = kv_refs[0].shape[0]
    chunk_rows = heads_per_chunk * rows
    first_query = place_ref[0]
    half = place_ref[1]
    own_start = first_query - half * rows
    score_scale = HD ** (-0.5) * math.log2(math.e)

    @pl.when(pl.program_id(0) == 0)
    def _():
        pos = first_query + lax.broadcasted_iota(jnp.int32, (rows, HD), 0)

        def later_doc(i, carry):
            start, lo = carry
            start = start + lengths_ref[i]
            return start, jnp.where(start <= pos, start, lo)

        _, lo = lax.fori_loop(
            0, lengths_ref.shape[0], later_doc, (jnp.int32(0), jnp.zeros((rows, HD), jnp.int32))
        )
        lo_ref[...] = lo

    def first_doc(i, carry):
        start, lo = carry
        start = start + lengths_ref[i]
        return start, jnp.where(start <= first_query, start, lo)

    _, lo_first = lax.fori_loop(0, lengths_ref.shape[0], first_doc, (jnp.int32(0), jnp.int32(0)))

    def absorb(key_block, value_block, key_start, causal, initial):
        keys = key_block.shape[0]
        key_pos = key_start + lax.broadcasted_iota(jnp.int32, (rows, keys), 1)
        lo = jnp.concatenate([lo_ref[...]] * (keys // HD), axis=1)
        allowed = key_pos >= lo
        if causal:
            query_pos = first_query + lax.broadcasted_iota(jnp.int32, (rows, keys), 0)
            allowed = allowed & (key_pos <= query_pos)
        allowed = jnp.concatenate([allowed] * heads_per_chunk, axis=0)
        widened = jnp.concatenate([value_block, jnp.ones_like(value_block)], axis=1)
        for chunk in range(group_size // heads_per_chunk):
            at = pl.ds(chunk * chunk_rows, chunk_rows)
            q = jnp.concatenate(
                [
                    q_ref[:, (chunk * heads_per_chunk + h) * HD : (chunk * heads_per_chunk + h + 1) * HD]
                    for h in range(heads_per_chunk)
                ],
                axis=0,
            )
            scores = lax.dot_general(
                q, key_block, (((1,), (1,)), ((), ())), preferred_element_type=jnp.float32
            )
            scores = jnp.where(allowed, scores * score_scale, NEVER)
            block_max = jnp.max(scores, axis=1, keepdims=True)
            if initial:
                max_new = block_max
            else:
                max_old = max_ref[at, :]
                max_new = jnp.maximum(max_old, block_max)
            weights = jnp.exp2(scores - max_new[:, :1]).astype(jnp.bfloat16)
            added = jnp.dot(weights, widened, preferred_element_type=jnp.float32)
            if initial:
                acc_ref[at, :] = added
                max_ref[at, :] = jnp.broadcast_to(max_new, (chunk_rows, HD))
            else:
                rescale = jnp.exp2(max_old - max_new)
                acc_ref[at, :] = acc_ref[at, :] * jnp.concatenate([rescale] * 2, axis=1) + added
                max_ref[at, :] = max_new

    mine = pl.ds(pl.multiple_of(half * rows, rows), rows)
    absorb(kv_refs[0][mine, :], kv_refs[1][mine, :], first_query, True, True)

    @pl.when((half == 1) & (own_start + rows > lo_first))
    def _():
        absorb(kv_refs[0][:rows, :], kv_refs[1][:rows, :], own_start, False, False)

    for distance in range(1, len(kv_refs) // 2):
        start = own_start - distance * span_rows

        @pl.when(start + span_rows > lo_first)
        def _():
            absorb(kv_refs[2 * distance][...], kv_refs[2 * distance + 1][...], start, False, False)

    for h in range(group_size):
        acc = acc_ref[h * rows : (h + 1) * rows, :]
        out_ref[:, h * HD : (h + 1) * HD] = (acc[:, :HD] / acc[:, HD:]).astype(jnp.bfloat16)


def per_device(queries, keys, values, doc_lengths):
    rows = queries.shape[0]
    kv_heads = keys.shape[1] // HD
    group_size = queries.shape[1] // keys.shape[1]
    half = lax.axis_index("head")
    span = lax.axis_index("ctx")
    place = jnp.stack([(span * lax.axis_size("head") + half) * rows, half]).astype(jnp.int32)

    own = jnp.concatenate([keys, values], axis=1)
    arrived = [own] + [from_behind(own, "ctx", d) for d in range(1, REACH + 1)]
    spans = [lax.all_gather(block, "head", axis=0, tiled=True) for block in arrived]

    smem = pl.BlockSpec(memory_space=pltpu.SMEM)
    kv_specs, kv_args = [], []
    for block in spans:
        kv_specs.append(pl.BlockSpec((block.shape[0], HD), lambda g: (0, g)))
        kv_specs.append(pl.BlockSpec((block.shape[0], HD), lambda g: (0, kv_heads + g)))
        kv_args += [block, block]
    head_rows = group_size * rows
    return pl.pallas_call(
        functools.partial(attend_kernel, group_size=group_size, heads_per_chunk=2),
        grid=(kv_heads,),
        in_specs=[smem, smem, pl.BlockSpec((rows, group_size * HD), lambda g: (0, g))] + kv_specs,
        out_specs=pl.BlockSpec((rows, group_size * HD), lambda g: (0, g)),
        out_shape=jax.ShapeDtypeStruct(queries.shape, queries.dtype),
        scratch_shapes=[
            pltpu.VMEM((rows, HD), jnp.int32),
            pltpu.VMEM((head_rows, HD), jnp.float32),
            pltpu.VMEM((head_rows, 2 * HD), jnp.float32),
        ],
        compiler_params=pltpu.CompilerParams(
            dimension_semantics=("arbitrary",), vmem_limit_bytes=32 * 1024 * 1024
        ),
        name="attend",
    )(place, doc_lengths, queries, *kv_args)


def solution(mesh):
    placed = P(("ctx", "head"), None)
    return jax.shard_map(
        per_device, mesh=mesh, in_specs=(placed, placed, placed, P()), out_specs=placed, check_vma=False
    )
```

```python
import functools
import math

import jax
import jax.numpy as jnp
from jax import lax
from jax.experimental import pallas as pl
from jax.experimental.pallas import tpu as pltpu
from jax.sharding import PartitionSpec as P

HD = 128
REACH = 4
NEVER = -1e30
SUM_ROWS = 16


def from_behind(block, axis, distance):
    devices = range(lax.axis_size(axis))
    route = [(i - distance, i) for i in devices if i - distance in devices]
    return lax.ppermute(block, axis, route)


def swapped(block):
    return lax.ppermute(block, "head", [(0, 1), (1, 0)])


def attend_kernel(place_ref, lengths_ref, q_ref, *refs, group_size, chunk_heads):
    kv_refs, (out_ref, lo_ref, qt_ref, max_ref, acc_ref) = refs[:-5], refs[-5:]
    rows = q_ref.shape[0]
    span_rows = 2 * rows
    chunk = chunk_heads * rows
    first_query = place_ref[0]
    half = place_ref[1]
    own_start = first_query - half * rows
    last_query = first_query + rows - 1
    score_scale = HD ** (-0.5) * math.log2(math.e)

    @pl.when(pl.program_id(0) == 0)
    def _():
        pos = first_query + lax.broadcasted_iota(jnp.int32, (8, rows), 1)

        def later_doc(i, carry):
            start, lo = carry
            start = start + lengths_ref[i]
            return start, jnp.where(start <= pos, start, lo)

        _, lo = lax.fori_loop(
            0, lengths_ref.shape[0], later_doc, (jnp.int32(0), jnp.zeros((8, rows), jnp.int32))
        )
        lo_ref[...] = lo

    def doc_start(i, carry):
        start, lo_first, lo_last = carry
        start = start + lengths_ref[i]
        lo_first = jnp.where(start <= first_query, start, lo_first)
        lo_last = jnp.where(start <= last_query, start, lo_last)
        return start, lo_first, lo_last

    zero = jnp.int32(0)
    _, lo_first, lo_last = lax.fori_loop(0, lengths_ref.shape[0], doc_start, (zero, zero, zero))

    for h in range(group_size):
        qt_ref[:, h * rows : (h + 1) * rows] = q_ref[:, h * HD : (h + 1) * HD].T

    def absorb(key_block, value_block, allowed, initial):
        keys = key_block.shape[0]
        widened = jnp.concatenate([value_block.T, jnp.ones((SUM_ROWS, keys), value_block.dtype)], axis=0)
        if allowed is not None:
            allowed = jnp.concatenate([allowed] * chunk_heads, axis=1)
        for i in range(group_size // chunk_heads):
            at = slice(i * chunk, (i + 1) * chunk)
            scores = jnp.dot(key_block, qt_ref[:, at], preferred_element_type=jnp.float32)
            if allowed is not None:
                scores = jnp.where(allowed, scores, NEVER)
            max_new = jnp.max(scores, axis=0, keepdims=True)
            if not initial:
                max_old = max_ref[:, at]
                max_new = jnp.maximum(max_old, max_new)
            weights = jnp.exp2((scores - max_new) * score_scale).astype(jnp.bfloat16)
            added = jnp.dot(widened, weights, preferred_element_type=jnp.float32)
            if not initial:
                added = acc_ref[:, at] * jnp.exp2((max_old - max_new) * score_scale) + added
            acc_ref[:, at] = added
            max_ref[:, at] = max_new

    def positions(start, keys):
        return start + lax.broadcasted_iota(jnp.int32, (keys, rows), 0)

    def lows(keys):
        return jnp.concatenate([lo_ref[...]] * (keys // 8), axis=0)

    query_pos = first_query + lax.broadcasted_iota(jnp.int32, (rows, rows), 1)
    key_pos = positions(first_query, rows)
    absorb(kv_refs[0][...], kv_refs[1][...], (key_pos >= lows(rows)) & (key_pos <= query_pos), True)

    @pl.when((half == 1) & (own_start + rows > lo_first))
    def _():
        absorb(kv_refs[2][...], kv_refs[3][...], positions(own_start, rows) >= lows(rows), False)

    for distance in range(1, len(kv_refs) // 4):
        start = own_start - distance * span_rows
        k_near, v_near, k_far, v_far = kv_refs[4 * distance : 4 * distance + 4]

        def span(masked, k_near=k_near, v_near=v_near, k_far=k_far, v_far=v_far, start=start):
            allowed = None
            if masked:
                allowed = (
                    jnp.concatenate(
                        [positions(start + half * rows, rows), positions(start + (1 - half) * rows, rows)], axis=0
                    )
                    >= lows(span_rows)
                )
            absorb(
                jnp.concatenate([k_near[...], k_far[...]], axis=0),
                jnp.concatenate([v_near[...], v_far[...]], axis=0),
                allowed,
                False,
            )

        @pl.when((start + span_rows > lo_first) & (start < lo_last))
        def _():
            span(True)

        @pl.when(start >= lo_last)
        def _():
            span(False)

    for h in range(group_size):
        at = slice(h * rows, (h + 1) * rows)
        finished = acc_ref[:HD, at] * (1.0 / acc_ref[HD : HD + 1, at])
        out_ref[:, h * HD : (h + 1) * HD] = finished.astype(jnp.bfloat16).T


def per_device(queries, keys, values, doc_lengths):
    rows = queries.shape[0]
    kv_heads = keys.shape[1] // HD
    group_size = queries.shape[1] // keys.shape[1]
    half = lax.axis_index("head")
    span = lax.axis_index("ctx")
    place = jnp.stack([(span * lax.axis_size("head") + half) * rows, half]).astype(jnp.int32)

    own = jnp.concatenate([keys, values], axis=1)
    near = [own] + [from_behind(own, "ctx", d) for d in range(REACH, 0, -1)][::-1]
    far = [swapped(block) for block in near]

    smem = pl.BlockSpec(memory_space=pltpu.SMEM)
    kv_specs, kv_args = [], []
    for pair in zip(near, far):
        for block in pair:
            kv_specs.append(pl.BlockSpec((rows, HD), lambda g: (0, g)))
            kv_specs.append(pl.BlockSpec((rows, HD), lambda g: (0, kv_heads + g)))
            kv_args += [block, block]
    head_rows = group_size * rows
    return pl.pallas_call(
        functools.partial(attend_kernel, group_size=group_size, chunk_heads=2),
        grid=(kv_heads,),
        in_specs=[smem, smem, pl.BlockSpec((rows, group_size * HD), lambda g: (0, g))] + kv_specs,
        out_specs=pl.BlockSpec((rows, group_size * HD), lambda g: (0, g)),
        out_shape=jax.ShapeDtypeStruct(queries.shape, queries.dtype),
        scratch_shapes=[
            pltpu.VMEM((8, rows), jnp.int32),
            pltpu.VMEM((HD, head_rows), jnp.bfloat16),
            pltpu.VMEM((1, head_rows), jnp.float32),
            pltpu.VMEM((HD + SUM_ROWS, head_rows), jnp.float32),
        ],
        compiler_params=pltpu.CompilerParams(
            dimension_semantics=("arbitrary",), vmem_limit_bytes=32 * 1024 * 1024
        ),
        name="attend",
    )(place, doc_lengths, queries, *kv_args)


def solution(mesh):
    placed = P(("ctx", "head"), None)
    return jax.shard_map(
        per_device, mesh=mesh, in_specs=(placed, placed, placed, P()), out_specs=placed, check_vma=False
    )
```

```python
import functools
import math

import jax
import jax.numpy as jnp
from jax import lax
from jax.experimental import pallas as pl
from jax.experimental.pallas import tpu as pltpu
from jax.sharding import PartitionSpec as P

HD = 128
REACH = 4
NEVER = -1e30
SUM_ROWS = 16
AXES = ("ctx", "head")
PARTNER = ((1, 2, 3), (2, 1, 3))


def to_next_group(block):
    spans, cores = lax.axis_size("ctx"), lax.axis_size("head")
    pairs = [(s * cores + h, (s + REACH) * cores + h) for s in range(spans - REACH) for h in range(cores)]
    return lax.ppermute(block, AXES, pairs)


def in_group(block, turn):
    spans, cores = lax.axis_size("ctx"), lax.axis_size("head")
    pairs = []
    for s in range(spans):
        for h in range(cores):
            pairs.append((s * cores + h, (s ^ PARTNER[h][turn]) * cores + h))
    return lax.ppermute(block, AXES, pairs)


def to_other_core(block):
    cores = lax.axis_size("head")
    return lax.ppermute(block, "head", [(h, cores - 1 - h) for h in range(cores)])


def doc_starts(lengths_ref, first, last):
    def one_doc(i, carry):
        start, lo_first, lo_last = carry
        start = start + lengths_ref[i]
        return start, jnp.where(start <= first, start, lo_first), jnp.where(start <= last, start, lo_last)

    zero = jnp.int32(0)
    _, lo_first, lo_last = lax.fori_loop(0, lengths_ref.shape[0], one_doc, (zero, zero, zero))
    return lo_first, lo_last


def doc_start_rows(lengths_ref, first_query, rows):
    pos = first_query + lax.broadcasted_iota(jnp.int32, (8, rows), 1)

    def one_doc(i, carry):
        start, lo = carry
        start = start + lengths_ref[i]
        return start, jnp.where(start <= pos, start, lo)

    zero = jnp.zeros((8, rows), jnp.int32)
    return lax.fori_loop(0, lengths_ref.shape[0], one_doc, (jnp.int32(0), zero))[1]


def head_group(g, width):
    return pl.ds(pl.multiple_of(g * width, width), width)


def absorb(key_block, value_block, allowed, state, at, initial, group_size):
    qt_ref, max_ref, acc_ref = state
    keys = key_block.shape[0]
    widened = jnp.concatenate([value_block.T, jnp.ones((SUM_ROWS, keys), value_block.dtype)], axis=0)
    scores = jnp.dot(key_block, qt_ref[:, at], preferred_element_type=jnp.float32)
    if allowed is not None:
        scores = jnp.where(jnp.concatenate([allowed] * group_size, axis=1), scores, NEVER)
    max_new = jnp.max(scores, axis=0, keepdims=True)
    score_scale = HD ** (-0.5) * math.log2(math.e)
    if not initial:
        max_old = max_ref[:1, at]
        max_new = jnp.maximum(max_old, max_new)
    weights = jnp.exp2((scores - max_new) * score_scale).astype(jnp.bfloat16)
    added = jnp.dot(widened, weights, preferred_element_type=jnp.float32)
    if not initial:
        added = acc_ref[:, at] * jnp.exp2((max_old - max_new) * score_scale) + added
    acc_ref[:, at] = added
    max_ref[:, at] = jnp.broadcast_to(max_new, (8, max_new.shape[1]))


def positions(start, keys, queries):
    return start + lax.broadcasted_iota(jnp.int32, (keys, queries), 0)


def own_kernel(place_ref, lengths_ref, q_ref, near_ref, far_ref, qt_ref, max_ref, acc_ref, *, group_size):
    rows = q_ref.shape[0]
    width = group_size * rows
    first_query, half = place_ref[0], place_ref[1]
    own_start = first_query - half * rows
    lo_first, _ = doc_starts(lengths_ref, first_query, first_query)
    lo = doc_start_rows(lengths_ref, first_query, rows)
    lo = jnp.concatenate([lo] * (rows // 8), axis=0)
    query_pos = first_query + lax.broadcasted_iota(jnp.int32, (rows, rows), 1)
    key_pos = positions(first_query, rows, rows)
    own_allowed = (key_pos >= lo) & (key_pos <= query_pos)
    far_allowed = positions(own_start, rows, rows) >= lo
    state = (qt_ref, max_ref, acc_ref)

    def one_group(g, _):
        at = head_group(g, width)
        kv = head_group(g, HD)
        q = q_ref[:, head_group(g, group_size * HD)]
        qt_ref[:, at] = jnp.concatenate([q[:, h * HD : (h + 1) * HD].T for h in range(group_size)], axis=1)
        absorb(near_ref[0, :, kv], near_ref[1, :, kv], own_allowed, state, at, True, group_size)

        @pl.when((half == 1) & (own_start + rows > lo_first))
        def _():
            absorb(far_ref[0, :, kv], far_ref[1, :, kv], far_allowed, state, at, False, group_size)

        return 0

    lax.fori_loop(0, near_ref.shape[2] // HD, one_group, 0)


def span_kernel(place_ref, lengths_ref, near_ref, far_ref, qt_ref, max_in, acc_in, *refs, group_size, last):
    del max_in, acc_in
    out_ref = refs[0] if last else None
    max_ref, acc_ref = refs[-2:]
    rows = near_ref.shape[1]
    width = group_size * rows
    kv_heads = near_ref.shape[2] // HD
    first_query, half, near_start, far_start = place_ref[0], place_ref[1], place_ref[2], place_ref[3]
    lo_first, lo_last = doc_starts(lengths_ref, first_query, first_query + rows - 1)
    state = (qt_ref, max_ref, acc_ref)

    def span(masked):
        allowed = None
        if masked:
            lo = jnp.concatenate([doc_start_rows(lengths_ref, first_query, rows)] * (rows // 4), axis=0)
            key_pos = jnp.concatenate([positions(near_start, rows, rows), positions(far_start, rows, rows)], axis=0)
            allowed = key_pos >= lo

        def one_group(g, _):
            kv = head_group(g, HD)
            absorb(
                jnp.concatenate([near_ref[0, :, kv], far_ref[0, :, kv]], axis=0),
                jnp.concatenate([near_ref[1, :, kv], far_ref[1, :, kv]], axis=0),
                allowed,
                state,
                head_group(g, width),
                False,
                group_size,
            )
            return 0

        lax.fori_loop(0, kv_heads, one_group, 0)

    needed = jnp.maximum(near_start, far_start) + rows > lo_first
    whole = jnp.minimum(near_start, far_start) >= lo_last

    @pl.when(needed & jnp.logical_not(whole))
    def _():
        span(True)

    @pl.when(whole)
    def _():
        span(False)

    if last:

        def finish(g, _):
            acc = acc_ref[:, head_group(g, width)]
            finished = (acc[:HD] * (1.0 / acc[HD : HD + 1])).astype(jnp.bfloat16)
            out_ref[:, head_group(g, group_size * HD)] = jnp.concatenate(
                [finished[:, h * rows : (h + 1) * rows].T for h in range(group_size)], axis=1
            )
            return 0

        lax.fori_loop(0, kv_heads, finish, 0)


def per_device(queries, keys, values, doc_lengths):
    rows = queries.shape[0]
    group_size = queries.shape[1] // keys.shape[1]
    head_rows = (queries.shape[1] // HD) * rows
    half, span = lax.axis_index("head"), lax.axis_index("ctx")
    cores = lax.axis_size("head")
    place_in_group = lax.rem(span, REACH)
    first_query = (span * cores + half) * rows

    vmem = pl.BlockSpec(memory_space=pltpu.VMEM)
    smem = pl.BlockSpec(memory_space=pltpu.SMEM)
    qt_shape = jax.ShapeDtypeStruct((HD, head_rows), queries.dtype)
    max_shape = jax.ShapeDtypeStruct((8, head_rows), jnp.float32)
    acc_shape = jax.ShapeDtypeStruct((HD + SUM_ROWS, head_rows), jnp.float32)
    params = pltpu.CompilerParams(vmem_limit_bytes=24 * 1024 * 1024)

    cost = pl.CostEstimate(flops=0, bytes_accessed=0, transcendentals=0)

    own = jnp.stack([keys, values])
    behind = to_next_group(own)
    own_far = to_other_core(own)

    def place(near_span, far_span):
        near_start = (near_span * cores + half) * rows
        far_start = (far_span * cores + 1 - half) * rows
        return jnp.stack([first_query, half, near_start, far_start]).astype(jnp.int32)

    qt, row_max, acc = pl.pallas_call(
        functools.partial(own_kernel, group_size=group_size),
        in_specs=[smem, smem, vmem, vmem, vmem],
        out_specs=(vmem, vmem, vmem),
        out_shape=(qt_shape, max_shape, acc_shape),
        compiler_params=params,
        cost_estimate=cost,
        name="attend_own",
    )(place(span, span), doc_lengths, queries, own, own_far)

    behind, acc = lax.optimization_barrier((behind, acc))
    arrivals = [(span - REACH, span - REACH, behind)]
    for turn in range(REACH - 1):
        mine = jnp.where(half == 0, PARTNER[0][turn], PARTNER[1][turn])
        other = jnp.where(half == 0, PARTNER[1][turn], PARTNER[0][turn])
        send = jnp.where((place_in_group ^ mine) > place_in_group, own, behind)

        def source(partner):
            from_place = place_in_group ^ partner
            return span - place_in_group + from_place - jnp.where(from_place > place_in_group, REACH, 0)

        arrivals.append((source(mine), source(other), in_group(send, turn)))

    for number, (near_span, far_span, near) in enumerate(arrivals):
        last = number == len(arrivals) - 1
        if number > 0:
            near, acc = lax.optimization_barrier((near, acc))
        out_shapes = (max_shape, acc_shape)
        if last:
            out_shapes = (jax.ShapeDtypeStruct(queries.shape, queries.dtype),) + out_shapes
        *out, row_max, acc = pl.pallas_call(
            functools.partial(span_kernel, group_size=group_size, last=last),
            in_specs=[smem, smem] + [vmem] * 5,
            out_specs=(vmem,) * len(out_shapes),
            out_shape=out_shapes,
            input_output_aliases={5: len(out_shapes) - 2, 6: len(out_shapes) - 1},
            compiler_params=params,
            cost_estimate=cost,
            name="attend_last" if last else "attend_span",
        )(place(near_span, far_span), doc_lengths, near, to_other_core(near), qt, row_max, acc)
    return out[0]


def solution(mesh):
    placed = P(AXES, None)
    return jax.shard_map(
        per_device, mesh=mesh, in_specs=(placed, placed, placed, P()), out_specs=placed, check_vma=False
    )
```

```python
import functools
import math

import jax
import jax.numpy as jnp
from jax import lax
from jax.experimental import pallas as pl
from jax.experimental.pallas import tpu as pltpu
from jax.sharding import PartitionSpec as P

HD = 128
REACH = 4
NEVER = -1e30
SCORE_SCALE = HD ** (-0.5) * math.log2(math.e)
SUM_ROWS = 16
AXES = ("ctx", "head")
PARTNER = ((1, 2), (2, 1))
SAFE = 100.0


def to_next_group(block):
    spans, cores = lax.axis_size("ctx"), lax.axis_size("head")
    pairs = [(s * cores + h, (s + REACH) * cores + h) for s in range(spans - REACH) for h in range(cores)]
    return lax.ppermute(block, AXES, pairs)


def to_opposite(block):
    spans, cores = lax.axis_size("ctx"), lax.axis_size("head")
    pairs = []
    for s in range(spans):
        place = s % REACH
        target = s - place + REACH - 1 - place
        target += 0 if target > s else REACH
        if target < spans:
            pairs += [(s * cores + h, target * cores + h) for h in range(cores)]
    return lax.ppermute(block, AXES, pairs)


def in_group(block, turn):
    spans, cores = lax.axis_size("ctx"), lax.axis_size("head")
    pairs = []
    for s in range(spans):
        for h in range(cores):
            pairs.append((s * cores + h, (s ^ PARTNER[h][turn]) * cores + h))
    return lax.ppermute(block, AXES, pairs)


def to_other_core(block):
    cores = lax.axis_size("head")
    return lax.ppermute(block, "head", [(h, cores - 1 - h) for h in range(cores)])


def doc_starts(lengths_ref, first, last):
    def one_doc(i, carry):
        start, lo_first, lo_last = carry
        start = start + lengths_ref[i]
        return start, jnp.where(start <= first, start, lo_first), jnp.where(start <= last, start, lo_last)

    zero = jnp.int32(0)
    _, lo_first, lo_last = lax.fori_loop(0, lengths_ref.shape[0], one_doc, (zero, zero, zero))
    return lo_first, lo_last


def doc_start_rows(lengths_ref, first_query, rows):
    pos = first_query + lax.broadcasted_iota(jnp.int32, (8, rows), 1)

    def one_doc(i, carry):
        start, lo = carry
        start = start + lengths_ref[i]
        return start, jnp.where(start <= pos, start, lo)

    zero = jnp.zeros((8, rows), jnp.int32)
    return lax.fori_loop(0, lengths_ref.shape[0], one_doc, (jnp.int32(0), zero))[1]


def head_group(g, width):
    return pl.ds(pl.multiple_of(g * width, width), width)


def positions(start, keys, queries):
    return start + lax.broadcasted_iota(jnp.int32, (keys, queries), 0)


def score_bound(blocks, q_square):
    largest = None
    for block in blocks:
        top = jnp.max(jnp.abs(block[0].astype(jnp.float32)), axis=0, keepdims=True)
        largest = top if largest is None else jnp.maximum(largest, top)
    square = largest * largest
    kv_heads = square.shape[1] // HD
    by_head = jnp.concatenate([square[:, g * HD : (g + 1) * HD] for g in range(kv_heads)], axis=0)
    return jnp.max(jnp.sum(by_head, axis=1, keepdims=True) * q_square)


def is_safe(bound):
    return bound * (SCORE_SCALE * SCORE_SCALE) <= SAFE * SAFE


def absorb(key_block, value_block, allowed, state, at, initial, shifted, group_size):
    qt_ref, max_ref, acc_ref = state
    keys = key_block.shape[0]
    widened = jnp.concatenate([value_block.T, jnp.ones((SUM_ROWS, keys), value_block.dtype)], axis=0)
    scores = jnp.dot(key_block, qt_ref[:, at], preferred_element_type=jnp.float32)
    if allowed is not None:
        allowed = jnp.concatenate([allowed] * group_size, axis=1)
    if shifted:
        if allowed is not None:
            scores = jnp.where(allowed, scores, NEVER)
        max_new = jnp.max(scores, axis=0, keepdims=True)
        if not initial:
            max_old = max_ref[:1, at]
            max_new = jnp.maximum(max_old, max_new)
        weights = jnp.exp2((scores - max_new) * SCORE_SCALE)
        max_ref[:, at] = jnp.broadcast_to(max_new, (8, max_new.shape[1]))
    else:
        weights = jnp.exp2(scores * SCORE_SCALE)
        if allowed is not None:
            weights = jnp.where(allowed, weights, 0.0)
        if initial:
            max_ref[:, at] = jnp.zeros((8, scores.shape[1]), jnp.float32)
    added = jnp.dot(widened, weights.astype(jnp.bfloat16), preferred_element_type=jnp.float32)
    if initial:
        acc_ref[:, at] = added
    elif shifted:
        acc_ref[:, at] = acc_ref[:, at] * jnp.exp2((max_old - max_new) * SCORE_SCALE) + added
    else:
        acc_ref[:, at] += added


def own_kernel(
    place_ref, lengths_ref, q_ref, near_ref, far_ref, qt_ref, max_ref, acc_ref, square_ref, safe_ref, *, group_size
):
    rows = q_ref.shape[0]
    width = group_size * rows
    kv_heads = near_ref.shape[2] // HD
    first_query, half = place_ref[0], place_ref[1]
    own_start = first_query - half * rows
    lo_first, _ = doc_starts(lengths_ref, first_query, first_query)
    lo = doc_start_rows(lengths_ref, first_query, rows)
    lo = jnp.concatenate([lo] * (rows // 8), axis=0)
    query_pos = first_query + lax.broadcasted_iota(jnp.int32, (rows, rows), 1)
    key_pos = positions(first_query, rows, rows)
    own_allowed = (key_pos >= lo) & (key_pos <= query_pos)
    far_allowed = positions(own_start, rows, rows) >= lo
    state = (qt_ref, max_ref, acc_ref)

    def turn_queries(g, _):
        q = q_ref[:, head_group(g, group_size * HD)]
        qt = jnp.concatenate([q[:, h * HD : (h + 1) * HD].T for h in range(group_size)], axis=1)
        qt_ref[:, head_group(g, width)] = qt
        wide = qt.astype(jnp.float32)
        square = jnp.max(jnp.sum(wide * wide, axis=0, keepdims=True), axis=1, keepdims=True)
        square_ref[pl.ds(g, 1), :] = jnp.broadcast_to(square, (1, HD))
        return 0

    lax.fori_loop(0, kv_heads, turn_queries, 0)
    safe = is_safe(score_bound([near_ref, far_ref], square_ref[:, :1]))
    safe_ref[0] = safe.astype(jnp.int32)

    def work(shifted):
        def one_group(g, _):
            at = head_group(g, width)
            kv = head_group(g, HD)
            absorb(near_ref[0, :, kv], near_ref[1, :, kv], own_allowed, state, at, True, shifted, group_size)

            @pl.when((half == 1) & (own_start + rows > lo_first))
            def _():
                absorb(far_ref[0, :, kv], far_ref[1, :, kv], far_allowed, state, at, False, shifted, group_size)

            return 0

        lax.fori_loop(0, kv_heads, one_group, 0)

    pl.when(safe)(lambda: work(False))
    pl.when(jnp.logical_not(safe))(lambda: work(True))


def span_kernel(place_ref, lengths_ref, safe_in, square_ref, *refs, spans, group_size, last):
    blocks, (qt_ref, max_in, acc_in), refs = refs[: 2 * spans], refs[2 * spans : 2 * spans + 3], refs[2 * spans + 3 :]
    del max_in, acc_in
    out_ref = refs[0] if last else None
    max_ref, acc_ref, safe_ref = refs[-3:]
    rows = blocks[0].shape[1]
    width = group_size * rows
    kv_heads = blocks[0].shape[2] // HD
    first_query = place_ref[0]
    lo_first, lo_last = doc_starts(lengths_ref, first_query, first_query + rows - 1)
    state = (qt_ref, max_ref, acc_ref)
    safe_ref[0] = safe_in[0]

    def span(near_ref, far_ref, near_start, far_start, masked, shifted):
        allowed = None
        if masked:
            lo = jnp.concatenate([doc_start_rows(lengths_ref, first_query, rows)] * (rows // 4), axis=0)
            key_pos = jnp.concatenate([positions(near_start, rows, rows), positions(far_start, rows, rows)], axis=0)
            allowed = key_pos >= lo

        def one_group(g, _):
            kv = head_group(g, HD)
            absorb(
                jnp.concatenate([near_ref[0, :, kv], far_ref[0, :, kv]], axis=0),
                jnp.concatenate([near_ref[1, :, kv], far_ref[1, :, kv]], axis=0),
                allowed,
                state,
                head_group(g, width),
                False,
                shifted,
                group_size,
            )
            return 0

        lax.fori_loop(0, kv_heads, one_group, 0)

    for number in range(spans):
        near_ref, far_ref = blocks[2 * number : 2 * number + 2]
        near_start, far_start = place_ref[2 + 2 * number], place_ref[3 + 2 * number]
        work = functools.partial(span, near_ref, far_ref, near_start, far_start)
        needed = jnp.maximum(near_start, far_start) + rows > lo_first
        whole = jnp.minimum(near_start, far_start) >= lo_last

        @pl.when(needed)
        def _():
            safe = (safe_ref[0] == 1) & is_safe(score_bound([near_ref, far_ref], square_ref[:, :1]))
            safe_ref[0] = safe.astype(jnp.int32)
            pl.when(safe & whole)(lambda: work(False, False))
            pl.when(safe & jnp.logical_not(whole))(lambda: work(True, False))
            pl.when(jnp.logical_not(safe))(lambda: work(True, True))

    if last:

        def finish(g, _):
            acc = acc_ref[:, head_group(g, width)]
            finished = (acc[:HD] * (1.0 / acc[HD : HD + 1])).astype(jnp.bfloat16)
            out_ref[:, head_group(g, group_size * HD)] = jnp.concatenate(
                [finished[:, h * rows : (h + 1) * rows].T for h in range(group_size)], axis=1
            )
            return 0

        lax.fori_loop(0, kv_heads, finish, 0)


def per_device(queries, keys, values, doc_lengths):
    rows = queries.shape[0]
    kv_heads = keys.shape[1] // HD
    group_size = queries.shape[1] // keys.shape[1]
    head_rows = (queries.shape[1] // HD) * rows
    half, span = lax.axis_index("head"), lax.axis_index("ctx")
    cores = lax.axis_size("head")
    place_in_group = lax.rem(span, REACH)
    first_query = (span * cores + half) * rows

    vmem = pl.BlockSpec(memory_space=pltpu.VMEM)
    smem = pl.BlockSpec(memory_space=pltpu.SMEM)
    qt_shape = jax.ShapeDtypeStruct((HD, head_rows), queries.dtype)
    max_shape = jax.ShapeDtypeStruct((8, head_rows), jnp.float32)
    acc_shape = jax.ShapeDtypeStruct((HD + SUM_ROWS, head_rows), jnp.float32)
    square_shape = jax.ShapeDtypeStruct((kv_heads, HD), jnp.float32)
    safe_shape = jax.ShapeDtypeStruct((1,), jnp.int32)
    params = pltpu.CompilerParams(vmem_limit_bytes=24 * 1024 * 1024)
    cost = pl.CostEstimate(flops=0, bytes_accessed=0, transcendentals=0)

    def place(*spans_of):
        parts = [first_query, half]
        for near_span, far_span in spans_of:
            parts += [(near_span * cores + half) * rows, (far_span * cores + 1 - half) * rows]
        return jnp.stack(parts).astype(jnp.int32)

    own = jnp.stack([keys, values])
    behind = to_next_group(own)
    opposite = to_opposite(own)
    own_far = to_other_core(own)

    qt, row_max, acc, square, safe = pl.pallas_call(
        functools.partial(own_kernel, group_size=group_size),
        in_specs=[smem, smem, vmem, vmem, vmem],
        out_specs=(vmem, vmem, vmem, vmem, smem),
        out_shape=(qt_shape, max_shape, acc_shape, square_shape, safe_shape),
        compiler_params=params,
        cost_estimate=cost,
        name="attend_own",
    )(place(), doc_lengths, queries, own, own_far)

    def source(partner):
        from_place = place_in_group ^ partner
        return span - place_in_group + from_place - jnp.where(from_place > place_in_group, REACH, 0)

    def attend(state, arrivals, last):
        safe, row_max, acc = state
        out_shapes = (max_shape, acc_shape, safe_shape)
        if last:
            out_shapes = (jax.ShapeDtypeStruct(queries.shape, queries.dtype),) + out_shapes
        blocks = []
        for _, _, near in arrivals:
            blocks += [near, to_other_core(near)]
        at = 4 + len(blocks)
        *out, row_max, acc, safe = pl.pallas_call(
            functools.partial(span_kernel, spans=len(arrivals), group_size=group_size, last=last),
            in_specs=[smem, smem, smem] + [vmem] * at,
            out_specs=(vmem,) * (len(out_shapes) - 1) + (smem,),
            out_shape=out_shapes,
            input_output_aliases={at + 1: len(out_shapes) - 3, at + 2: len(out_shapes) - 2},
            compiler_params=params,
            cost_estimate=cost,
            name="attend_last" if last else "attend_spans",
        )(place(*[a[:2] for a in arrivals]), doc_lengths, safe, square, *blocks, qt, row_max, acc)
        return out, (safe, row_max, acc)

    behind, opposite, acc = lax.optimization_barrier((behind, opposite, acc))
    exchanged = []
    for turn in range(2):
        mine = jnp.where(half == 0, PARTNER[0][turn], PARTNER[1][turn])
        other = jnp.where(half == 0, PARTNER[1][turn], PARTNER[0][turn])
        send = jnp.where((place_in_group ^ mine) > place_in_group, own, behind)
        exchanged.append((source(mine), source(other), in_group(send, turn)))
    arrivals = [
        (span - REACH, span - REACH, behind),
        (source(REACH - 1), source(REACH - 1), opposite),
    ]
    _, (safe, row_max, acc) = attend((safe, row_max, acc), arrivals, False)
    first, second, acc = lax.optimization_barrier((exchanged[0][2], exchanged[1][2], acc))
    arrivals = [exchanged[0][:2] + (first,), exchanged[1][:2] + (second,)]
    (out,), _ = attend((safe, row_max, acc), arrivals, True)
    return out


def solution(mesh):
    placed = P(AXES, None)
    return jax.shard_map(
        per_device, mesh=mesh, in_specs=(placed, placed, placed, P()), out_specs=placed, check_vma=False
    )
```

```python
import functools
import math

import jax
import jax.numpy as jnp
from jax import lax
from jax.experimental import pallas as pl
from jax.experimental.pallas import tpu as pltpu
from jax.sharding import PartitionSpec as P

HD = 128
REACH = 4
NEVER = -1e30
SCORE_SCALE = HD ** (-0.5) * math.log2(math.e)
SUM_ROWS = 16
AXES = ("ctx", "head")
PARTNER = ((1, 2), (2, 1))


def to_next_group(block):
    spans, cores = lax.axis_size("ctx"), lax.axis_size("head")
    pairs = [(s * cores + h, (s + REACH) * cores + h) for s in range(spans - REACH) for h in range(cores)]
    return lax.ppermute(block, AXES, pairs)


def to_opposite(block):
    spans, cores = lax.axis_size("ctx"), lax.axis_size("head")
    pairs = []
    for s in range(spans):
        place = s % REACH
        target = s - place + REACH - 1 - place
        target += 0 if target > s else REACH
        if target < spans:
            pairs += [(s * cores + h, target * cores + h) for h in range(cores)]
    return lax.ppermute(block, AXES, pairs)


def in_group(block, turn):
    spans, cores = lax.axis_size("ctx"), lax.axis_size("head")
    pairs = []
    for s in range(spans):
        for h in range(cores):
            pairs.append((s * cores + h, (s ^ PARTNER[h][turn]) * cores + h))
    return lax.ppermute(block, AXES, pairs)


def to_other_core(block):
    cores = lax.axis_size("head")
    return lax.ppermute(block, "head", [(h, cores - 1 - h) for h in range(cores)])


def doc_starts(lengths_ref, first, last):
    def one_doc(i, carry):
        start, lo_first, lo_last = carry
        start = start + lengths_ref[i]
        return start, jnp.where(start <= first, start, lo_first), jnp.where(start <= last, start, lo_last)

    zero = jnp.int32(0)
    _, lo_first, lo_last = lax.fori_loop(0, lengths_ref.shape[0], one_doc, (zero, zero, zero))
    return lo_first, lo_last


def doc_start_rows(lengths_ref, first_query, keys, rows):
    pos = first_query + lax.broadcasted_iota(jnp.int32, (8, rows), 1)

    def one_doc(i, carry):
        start, lo = carry
        start = start + lengths_ref[i]
        return start, jnp.where(start <= pos, start, lo)

    zero = jnp.zeros((8, rows), jnp.int32)
    lo = lax.fori_loop(0, lengths_ref.shape[0], one_doc, (jnp.int32(0), zero))[1]
    return jnp.concatenate([lo] * (keys // 8), axis=0)


def lanes(at, width):
    return pl.ds(pl.multiple_of(at * width, width), width)


def positions(starts, rows):
    return jnp.concatenate([start + lax.broadcasted_iota(jnp.int32, (rows, rows), 0) for start in starts], axis=0)


def turned(block, count):
    width = block.shape[1] // count
    return jnp.concatenate([block[:, i * width : (i + 1) * width].T for i in range(count)], axis=1)


def absorb(keys, values, allowed, qt, before):
    widened = jnp.concatenate([values.T, jnp.ones((SUM_ROWS, values.shape[0]), values.dtype)], axis=0)
    scores = jnp.dot(keys, qt, preferred_element_type=jnp.float32)
    if allowed is not None:
        allowed = jnp.concatenate([allowed] * (scores.shape[1] // allowed.shape[1]), axis=1)
        scores = jnp.where(allowed, scores, NEVER)
    row_max = jnp.max(scores, axis=0, keepdims=True)
    if before is not None:
        row_max = jnp.maximum(before[0], row_max)
    weights = jnp.exp2((scores - row_max) * SCORE_SCALE).astype(jnp.bfloat16)
    acc = jnp.dot(widened, weights, preferred_element_type=jnp.float32)
    if before is not None:
        acc = before[1] * jnp.exp2((before[0] - row_max) * SCORE_SCALE) + acc
    return row_max, acc


def own_kernel(place_ref, lengths_ref, q_ref, q_far_ref, kv_ref, qt_ref, max_ref, acc_ref, q_near_ref, sem):
    rows, wide = q_far_ref.shape
    kv_heads = kv_ref.shape[3] // HD
    group_size = wide // (kv_heads * HD)
    width = group_size * rows
    half = place_ref[2]
    fetch = pltpu.make_async_copy(q_ref.at[:, lanes(half, wide)], q_near_ref, sem)
    fetch.start()
    starts = place_ref[0], place_ref[1]

    def tokens(side, q_side_ref):
        first = starts[side]
        query_pos = first + lax.broadcasted_iota(jnp.int32, (rows, rows), 1)
        key_pos = positions([first], rows)
        diagonal = (key_pos >= doc_start_rows(lengths_ref, first, rows, rows)) & (key_pos <= query_pos)
        earlier = positions([starts[1 - side]], rows) >= doc_start_rows(lengths_ref, first, rows, rows)

        def one_group(g, _):
            at = lanes(side * kv_heads + g, width)
            kv = lanes(g, HD)
            qt = turned(q_side_ref[:, lanes(g, group_size * HD)], group_size)
            qt_ref[:, at] = qt

            def store(state):
                max_ref[:, at] = jnp.broadcast_to(state[0], (8, width))
                acc_ref[:, at] = state[1]

            @pl.when(half == side)
            def _():
                store(absorb(kv_ref[side, 0, :, kv], kv_ref[side, 1, :, kv], diagonal, qt, None))

            @pl.when(half != side)
            def _():
                both = [jnp.concatenate([kv_ref[1 - side, i, :, kv], kv_ref[side, i, :, kv]], axis=0) for i in range(2)]
                store(absorb(both[0], both[1], jnp.concatenate([earlier, diagonal], axis=0), qt, None))

            return 0

        lax.fori_loop(0, kv_heads, one_group, 0)

    tokens(1, q_far_ref)
    fetch.wait()
    tokens(0, q_near_ref)


def span_steps(place_ref, lengths_ref, kv_ref, qt_ref, number, side, load, store):
    rows = kv_ref.shape[2]
    kv_heads = kv_ref.shape[3] // HD
    width = qt_ref.shape[1] // (2 * kv_heads)
    first = place_ref[side]
    key_starts = place_ref[3 + 2 * number], place_ref[4 + 2 * number]
    lo_first, lo_last = doc_starts(lengths_ref, first, first + rows - 1)
    needed = jnp.maximum(key_starts[0], key_starts[1]) + rows > lo_first
    whole = jnp.minimum(key_starts[0], key_starts[1]) >= lo_last

    def work(masked):
        allowed = None
        if masked:
            allowed = positions(key_starts, rows) >= doc_start_rows(lengths_ref, first, 2 * rows, rows)

        def one_group(g, _):
            kv = lanes(g, HD)
            keys, values = (jnp.concatenate([kv_ref[0, i, :, kv], kv_ref[1, i, :, kv]], axis=0) for i in range(2))
            qt = qt_ref[:, lanes(side * kv_heads + g, width)]
            store(g, absorb(keys, values, allowed, qt, load(g)))
            return 0

        lax.fori_loop(0, kv_heads, one_group, 0)

    pl.when(whole)(lambda: work(False))
    pl.when(needed & jnp.logical_not(whole))(lambda: work(True))
    return needed


def span_kernel(place_ref, lengths_ref, kv_ref, qt_ref, max_in, acc_in, max_ref, acc_ref, *, number):
    del max_in, acc_in
    kv_heads = kv_ref.shape[3] // HD
    width = qt_ref.shape[1] // (2 * kv_heads)
    for side in range(2):

        def load(g):
            at = lanes(side * kv_heads + g, width)
            return max_ref[:1, at], acc_ref[:, at]

        def store(g, state):
            at = lanes(side * kv_heads + g, width)
            max_ref[:, at] = jnp.broadcast_to(state[0], (8, width))
            acc_ref[:, at] = state[1]

        span_steps(place_ref, lengths_ref, kv_ref, qt_ref, number, side, load, store)


def last_kernel(place_ref, lengths_ref, kv_ref, qt_ref, max_ref, acc_ref, out_ref, *refs, number, side):
    rows = kv_ref.shape[2]
    kv_heads = kv_ref.shape[3] // HD
    width = qt_ref.shape[1] // (2 * kv_heads)
    group_size = width // rows
    out = out_ref
    if refs:
        out, sem = refs

    def load(g):
        at = lanes(side * kv_heads + g, width)
        return max_ref[:1, at], acc_ref[:, at]

    def finish(g, state):
        acc = state[1]
        finished = (acc[:HD] * (1.0 / acc[HD : HD + 1])).astype(out.dtype)
        out[:, lanes(g, group_size * HD)] = turned(finished, group_size)

    needed = span_steps(place_ref, lengths_ref, kv_ref, qt_ref, number, side, load, finish)

    @pl.when(jnp.logical_not(needed))
    def _():
        def one_group(g, _):
            finish(g, load(g))
            return 0

        lax.fori_loop(0, kv_heads, one_group, 0)

    if refs:
        copy = pltpu.make_async_copy(out, out_ref.at[:, lanes(place_ref[2], out.shape[1])], sem)
        copy.start()
        copy.wait()


def join_kernel(place_ref, far_ref, out_in, out_ref, sem):
    del out_in
    copy = pltpu.make_async_copy(far_ref, out_ref.at[:, lanes(1 - place_ref[2], far_ref.shape[1])], sem)
    copy.start()
    copy.wait()


def per_device(queries, keys, values, doc_lengths):
    rows, all_heads = queries.shape
    half_heads = all_heads // 2
    head_rows = (all_heads // HD) * rows
    half, span = lax.axis_index("head"), lax.axis_index("ctx")
    cores = lax.axis_size("head")
    place_in_group = lax.rem(span, REACH)

    def source(partner):
        from_place = place_in_group ^ partner
        return span - place_in_group + from_place - jnp.where(from_place > place_in_group, REACH, 0)

    mine = [jnp.where(half == 0, PARTNER[0][turn], PARTNER[1][turn]) for turn in range(2)]
    parts = [(span * cores + half) * rows, (span * cores + 1 - half) * rows, half]
    for origin in (span - REACH, source(REACH - 1), source(mine[0]), source(mine[1])):
        parts += [(origin * cores + half) * rows, (origin * cores + 1 - half) * rows]
    place = jnp.stack(parts).astype(jnp.int32)

    vmem = pl.BlockSpec(memory_space=pltpu.VMEM)
    smem = pl.BlockSpec(memory_space=pltpu.SMEM)
    anywhere = pl.BlockSpec(memory_space=pl.ANY)
    qt_shape = jax.ShapeDtypeStruct((HD, head_rows), queries.dtype)
    max_shape = jax.ShapeDtypeStruct((8, head_rows), jnp.float32)
    acc_shape = jax.ShapeDtypeStruct((HD + SUM_ROWS, head_rows), jnp.float32)
    side_shape = jax.ShapeDtypeStruct((rows, half_heads), queries.dtype)
    common = dict(
        compiler_params=pltpu.CompilerParams(vmem_limit_bytes=24 * 1024 * 1024),
        cost_estimate=pl.CostEstimate(flops=0, bytes_accessed=0, transcendentals=0),
    )

    def heads_of(array, core):
        width = array.shape[1] // 2
        return lax.dynamic_slice_in_dim(array, core * width, width, 1)

    given = to_other_core(jnp.stack([heads_of(keys, 1 - half), heads_of(values, 1 - half)]))
    own = jnp.stack([jnp.stack([heads_of(keys, half), heads_of(values, half)]), given])
    behind = to_next_group(own)
    opposite = to_opposite(own)
    q_far = to_other_core(heads_of(queries, 1 - half))

    qt, row_max, acc = pl.pallas_call(
        own_kernel,
        in_specs=[smem, smem, anywhere, vmem, vmem],
        out_specs=(vmem, vmem, vmem),
        out_shape=(qt_shape, max_shape, acc_shape),
        scratch_shapes=[pltpu.VMEM((rows, half_heads), queries.dtype), pltpu.SemaphoreType.DMA],
        name="attend_own",
        **common,
    )(place, doc_lengths, queries, q_far, own)

    def attend(kv, row_max, acc, number):
        return pl.pallas_call(
            functools.partial(span_kernel, number=number),
            in_specs=[smem, smem] + [vmem] * 4,
            out_specs=(vmem, vmem),
            out_shape=(max_shape, acc_shape),
            input_output_aliases={4: 0, 5: 1},
            name="attend_span",
            **common,
        )(place, doc_lengths, kv, qt, row_max, acc)

    behind, acc = lax.optimization_barrier((behind, acc))
    exchanged = []
    for turn in range(2):
        send = jnp.where((place_in_group ^ mine[turn]) > place_in_group, own, behind)
        exchanged.append(in_group(send, turn))
    row_max, acc = attend(behind, row_max, acc, 0)
    row_max, acc = attend(opposite, row_max, acc, 1)
    row_max, acc = attend(exchanged[0], row_max, acc, 2)

    last_args = (place, doc_lengths, exchanged[1], qt, row_max, acc)
    out_far = pl.pallas_call(
        functools.partial(last_kernel, number=3, side=1),
        in_specs=[smem, smem] + [vmem] * 4,
        out_specs=vmem,
        out_shape=side_shape,
        name="attend_last_far",
        **common,
    )(*last_args)
    out = pl.pallas_call(
        functools.partial(last_kernel, number=3, side=0),
        in_specs=[smem, smem] + [vmem] * 4,
        out_specs=anywhere,
        out_shape=jax.ShapeDtypeStruct(queries.shape, queries.dtype),
        scratch_shapes=[pltpu.VMEM((rows, half_heads), queries.dtype), pltpu.SemaphoreType.DMA],
        name="attend_last_near",
        **common,
    )(*last_args)
    return pl.pallas_call(
        join_kernel,
        in_specs=[smem, vmem, anywhere],
        out_specs=anywhere,
        out_shape=jax.ShapeDtypeStruct(queries.shape, queries.dtype),
        input_output_aliases={2: 0},
        scratch_shapes=[pltpu.SemaphoreType.DMA],
        name="join_heads",
        **common,
    )(place, to_other_core(out_far), out)


def solution(mesh):
    placed = P(AXES, None)
    return jax.shard_map(
        per_device, mesh=mesh, in_specs=(placed, placed, placed, P()), out_specs=placed, check_vma=False
    )
```

```python
import functools
import math

import jax
import jax.numpy as jnp
from jax import lax
from jax.experimental import pallas as pl
from jax.experimental.pallas import tpu as pltpu
from jax.sharding import PartitionSpec as P

HD = 128
REACH = 4
NEVER = -1e30
SCORE_SCALE = HD ** (-0.5) * math.log2(math.e)
SUM_ROWS = 16
PARTS = 2
AXES = ("ctx", "head")
PARTNER = ((1, 2), (2, 1))


def to_next_group(block):
    spans, cores = lax.axis_size("ctx"), lax.axis_size("head")
    pairs = [(s * cores + h, (s + REACH) * cores + h) for s in range(spans - REACH) for h in range(cores)]
    return lax.ppermute(block, AXES, pairs)


def to_opposite(block):
    spans, cores = lax.axis_size("ctx"), lax.axis_size("head")
    pairs = []
    for s in range(spans):
        place = s % REACH
        target = s - place + REACH - 1 - place
        target += 0 if target > s else REACH
        if target < spans:
            pairs += [(s * cores + h, target * cores + h) for h in range(cores)]
    return lax.ppermute(block, AXES, pairs)


def in_group(block, turn):
    spans, cores = lax.axis_size("ctx"), lax.axis_size("head")
    pairs = []
    for s in range(spans):
        for h in range(cores):
            pairs.append((s * cores + h, (s ^ PARTNER[h][turn]) * cores + h))
    return lax.ppermute(block, AXES, pairs)


def to_other_core(block):
    cores = lax.axis_size("head")
    return lax.ppermute(block, "head", [(h, cores - 1 - h) for h in range(cores)])


def doc_starts(lengths_ref, first, last):
    def one_doc(i, carry):
        start, lo_first, lo_last = carry
        start = start + lengths_ref[i]
        return start, jnp.where(start <= first, start, lo_first), jnp.where(start <= last, start, lo_last)

    zero = jnp.int32(0)
    _, lo_first, lo_last = lax.fori_loop(0, lengths_ref.shape[0], one_doc, (zero, zero, zero))
    return lo_first, lo_last


def doc_start_rows(lengths_ref, first_query, keys, rows):
    pos = first_query + lax.broadcasted_iota(jnp.int32, (8, rows), 1)

    def one_doc(i, carry):
        start, lo = carry
        start = start + lengths_ref[i]
        return start, jnp.where(start <= pos, start, lo)

    zero = jnp.zeros((8, rows), jnp.int32)
    lo = lax.fori_loop(0, lengths_ref.shape[0], one_doc, (jnp.int32(0), zero))[1]
    return jnp.concatenate([lo] * (keys // 8), axis=0)


def lanes(at, width):
    return pl.ds(pl.multiple_of(at * width, width), width)


def positions(starts, rows):
    return jnp.concatenate([start + lax.broadcasted_iota(jnp.int32, (rows, rows), 0) for start in starts], axis=0)


def turned(block, count):
    width = block.shape[1] // count
    return jnp.concatenate([block[:, i * width : (i + 1) * width].T for i in range(count)], axis=1)


def softmax_step(scores, allowed, max_before):
    if allowed is not None:
        allowed = jnp.concatenate([allowed] * (scores.shape[1] // allowed.shape[1]), axis=1)
        scores = jnp.where(allowed, scores, NEVER)
    row_max = jnp.max(scores, axis=0, keepdims=True)
    rescale = None
    if max_before is not None:
        row_max = jnp.maximum(max_before, row_max)
        rescale = jnp.exp2((max_before - row_max) * SCORE_SCALE)
    return jnp.exp2((scores - row_max) * SCORE_SCALE).astype(jnp.bfloat16), row_max, rescale


def pipeline(chunks, allowed, queries_of, keys_of, values_of, before_of, store):
    def scores_of(chunk):
        return jnp.dot(keys_of(chunk), queries_of(chunk), preferred_element_type=jnp.float32)

    ahead = scores_of(chunks[0])
    for number, chunk in enumerate(chunks):
        scores = ahead
        if number + 1 < len(chunks):
            ahead = scores_of(chunks[number + 1])
        max_before, acc_before = before_of(chunk)
        weights, row_max, rescale = softmax_step(scores, allowed, max_before)
        values = values_of(chunk)
        widened = jnp.concatenate([values.T, jnp.ones((SUM_ROWS, values.shape[0]), values.dtype)], axis=0)
        acc = jnp.dot(widened, weights, preferred_element_type=jnp.float32)
        if rescale is not None:
            acc = acc_before * rescale + acc
        store(chunk, row_max, acc)


def chunks_of(kv_heads):
    return [(g, part) for g in range(kv_heads) for part in range(PARTS)]


def pick_kernel(place_ref, q_ref, out_ref, sem):
    copy = pltpu.make_async_copy(q_ref.at[:, lanes(1 - place_ref[2], out_ref.shape[1])], out_ref, sem)
    copy.start()
    copy.wait()


def own_kernel(place_ref, lengths_ref, q_ref, q_far_ref, kv_ref, qt_ref, max_ref, acc_ref, q_near_ref, sem):
    rows, wide = q_far_ref.shape
    kv_heads = kv_ref.shape[3] // HD
    group_size = wide // (kv_heads * HD)
    width = group_size * rows // PARTS
    half = place_ref[2]
    fetch = pltpu.make_async_copy(q_ref.at[:, lanes(half, wide)], q_near_ref, sem)
    fetch.start()
    starts = place_ref[0], place_ref[1]

    def tokens(side, q_side_ref):
        first = starts[side]
        query_pos = first + lax.broadcasted_iota(jnp.int32, (rows, rows), 1)
        key_pos = positions([first], rows)
        diagonal = (key_pos >= doc_start_rows(lengths_ref, first, rows, rows)) & (key_pos <= query_pos)
        earlier = positions([starts[1 - side]], rows) >= doc_start_rows(lengths_ref, first, rows, rows)

        def at(chunk):
            begin = ((side * kv_heads + chunk[0]) * PARTS + chunk[1]) * width
            return slice(begin, begin + width)

        for chunk in chunks_of(kv_heads):
            begin = (chunk[0] * PARTS + chunk[1]) * (group_size // PARTS) * HD
            qt_ref[:, at(chunk)] = turned(
                q_side_ref[:, begin : begin + group_size // PARTS * HD], group_size // PARTS
            )

        def store(chunk, row_max, acc):
            max_ref[:, at(chunk)] = jnp.broadcast_to(row_max, (8, width))
            acc_ref[:, at(chunk)] = acc

        def work(blocks, allowed):
            def of(i):
                return lambda chunk: jnp.concatenate(
                    [kv_ref[block, i, :, chunk[0] * HD : (chunk[0] + 1) * HD] for block in blocks], axis=0
                )

            pipeline(
                chunks_of(kv_heads),
                allowed,
                lambda chunk: qt_ref[:, at(chunk)],
                of(0),
                of(1),
                lambda chunk: (None, None),
                store,
            )

        pl.when(half == side)(lambda: work([side], diagonal))
        pl.when(half != side)(lambda: work([1 - side, side], jnp.concatenate([earlier, diagonal], axis=0)))

    tokens(1, q_far_ref)
    fetch.wait()
    tokens(0, q_near_ref)


def span_steps(place_ref, lengths_ref, kv_ref, qt_ref, number, side, load, store):
    rows = kv_ref.shape[2]
    kv_heads = kv_ref.shape[3] // HD
    width = qt_ref.shape[1] // (2 * kv_heads * PARTS)
    first = place_ref[side]
    key_starts = place_ref[3 + 2 * number], place_ref[4 + 2 * number]
    lo_first, lo_last = doc_starts(lengths_ref, first, first + rows - 1)
    needed = jnp.maximum(key_starts[0], key_starts[1]) + rows > lo_first
    whole = jnp.minimum(key_starts[0], key_starts[1]) >= lo_last

    def at(chunk):
        begin = ((side * kv_heads + chunk[0]) * PARTS + chunk[1]) * width
        return slice(begin, begin + width)

    def of(i):
        return lambda chunk: jnp.concatenate(
            [kv_ref[block, i, :, chunk[0] * HD : (chunk[0] + 1) * HD] for block in range(2)], axis=0
        )

    def work(masked):
        allowed = None
        if masked:
            allowed = positions(key_starts, rows) >= doc_start_rows(lengths_ref, first, 2 * rows, rows)
        pipeline(
            chunks_of(kv_heads),
            allowed,
            lambda chunk: qt_ref[:, at(chunk)],
            of(0),
            of(1),
            lambda chunk: load(at(chunk)),
            lambda chunk, row_max, acc: store(chunk, at(chunk), row_max, acc),
        )

    pl.when(whole)(lambda: work(False))
    pl.when(needed & jnp.logical_not(whole))(lambda: work(True))
    return needed


def span_kernel(place_ref, lengths_ref, kv_ref, qt_ref, max_in, acc_in, max_ref, acc_ref, *, number):
    del max_in, acc_in

    def load(at):
        return max_ref[:1, at], acc_ref[:, at]

    def store(chunk, at, row_max, acc):
        max_ref[:, at] = jnp.broadcast_to(row_max, (8, acc.shape[1]))
        acc_ref[:, at] = acc

    for side in range(2):
        span_steps(place_ref, lengths_ref, kv_ref, qt_ref, number, side, load, store)


def last_kernel(place_ref, lengths_ref, kv_ref, qt_ref, max_ref, acc_ref, out_ref, *refs, number, side):
    rows = kv_ref.shape[2]
    kv_heads = kv_ref.shape[3] // HD
    width = qt_ref.shape[1] // (2 * kv_heads * PARTS)
    out = out_ref
    if refs:
        out, sem = refs

    def load(at):
        return max_ref[:1, at], acc_ref[:, at]

    def finish(chunk, at, row_max, acc):
        begin = (chunk[0] * PARTS + chunk[1]) * width
        finished = (acc[:HD] * (1.0 / acc[HD : HD + 1])).astype(out.dtype)
        out[:, begin : begin + width] = turned(finished, width // rows)

    needed = span_steps(place_ref, lengths_ref, kv_ref, qt_ref, number, side, load, finish)

    @pl.when(jnp.logical_not(needed))
    def _():
        for chunk in chunks_of(kv_heads):
            begin = ((side * kv_heads + chunk[0]) * PARTS + chunk[1]) * width
            finish(chunk, None, *load(slice(begin, begin + width)))

    if refs:
        copy = pltpu.make_async_copy(out, out_ref.at[:, lanes(place_ref[2], out.shape[1])], sem)
        copy.start()
        copy.wait()


def join_kernel(place_ref, far_ref, out_in, out_ref, sem):
    del out_in
    copy = pltpu.make_async_copy(far_ref, out_ref.at[:, lanes(1 - place_ref[2], far_ref.shape[1])], sem)
    copy.start()
    copy.wait()


def per_device(queries, keys, values, doc_lengths):
    rows, all_heads = queries.shape
    half_heads = all_heads // 2
    head_rows = (all_heads // HD) * rows
    half, span = lax.axis_index("head"), lax.axis_index("ctx")
    cores = lax.axis_size("head")
    place_in_group = lax.rem(span, REACH)

    def source(partner):
        from_place = place_in_group ^ partner
        return span - place_in_group + from_place - jnp.where(from_place > place_in_group, REACH, 0)

    mine = [jnp.where(half == 0, PARTNER[0][turn], PARTNER[1][turn]) for turn in range(2)]
    parts = [(span * cores + half) * rows, (span * cores + 1 - half) * rows, half]
    for origin in (span - REACH, source(REACH - 1), source(mine[0]), source(mine[1])):
        parts += [(origin * cores + half) * rows, (origin * cores + 1 - half) * rows]
    place = jnp.stack(parts).astype(jnp.int32)

    vmem = pl.BlockSpec(memory_space=pltpu.VMEM)
    smem = pl.BlockSpec(memory_space=pltpu.SMEM)
    anywhere = pl.BlockSpec(memory_space=pl.ANY)
    qt_shape = jax.ShapeDtypeStruct((HD, head_rows), queries.dtype)
    max_shape = jax.ShapeDtypeStruct((8, head_rows), jnp.float32)
    acc_shape = jax.ShapeDtypeStruct((HD + SUM_ROWS, head_rows), jnp.float32)
    side_shape = jax.ShapeDtypeStruct((rows, half_heads), queries.dtype)
    common = dict(
        compiler_params=pltpu.CompilerParams(vmem_limit_bytes=24 * 1024 * 1024),
        cost_estimate=pl.CostEstimate(flops=0, bytes_accessed=0, transcendentals=0),
    )

    def heads_of(array, core):
        width = array.shape[1] // 2
        return lax.dynamic_slice_in_dim(array, core * width, width, 1)

    to_give = jnp.stack([heads_of(keys, 1 - half), heads_of(values, 1 - half)])
    given = to_other_core(to_give)
    given, queries = lax.optimization_barrier((given, queries))
    own = jnp.stack([jnp.stack([heads_of(keys, half), heads_of(values, half)]), given])
    behind = to_next_group(own)
    opposite = to_opposite(own)
    q_far = to_other_core(
        pl.pallas_call(
            pick_kernel,
            in_specs=[smem, anywhere],
            out_specs=vmem,
            out_shape=side_shape,
            scratch_shapes=[pltpu.SemaphoreType.DMA],
            name="pick_queries",
            **common,
        )(place, queries)
    )

    qt, row_max, acc = pl.pallas_call(
        own_kernel,
        in_specs=[smem, smem, anywhere, vmem, vmem],
        out_specs=(vmem, vmem, vmem),
        out_shape=(qt_shape, max_shape, acc_shape),
        scratch_shapes=[pltpu.VMEM((rows, half_heads), queries.dtype), pltpu.SemaphoreType.DMA],
        name="attend_own",
        **common,
    )(place, doc_lengths, queries, q_far, own)

    def attend(kv, row_max, acc, number):
        return pl.pallas_call(
            functools.partial(span_kernel, number=number),
            in_specs=[smem, smem] + [vmem] * 4,
            out_specs=(vmem, vmem),
            out_shape=(max_shape, acc_shape),
            input_output_aliases={4: 0, 5: 1},
            name="attend_span",
            **common,
        )(place, doc_lengths, kv, qt, row_max, acc)

    behind, acc = lax.optimization_barrier((behind, acc))
    exchanged = []
    for turn in range(2):
        send = jnp.where((place_in_group ^ mine[turn]) > place_in_group, own, behind)
        exchanged.append(in_group(send, turn))
    row_max, acc = attend(behind, row_max, acc, 0)
    row_max, acc = attend(opposite, row_max, acc, 1)
    row_max, acc = attend(exchanged[0], row_max, acc, 2)

    last_args = (place, doc_lengths, exchanged[1], qt, row_max, acc)
    out_far = pl.pallas_call(
        functools.partial(last_kernel, number=3, side=1),
        in_specs=[smem, smem] + [vmem] * 4,
        out_specs=vmem,
        out_shape=side_shape,
        name="attend_last_far",
        **common,
    )(*last_args)
    out = pl.pallas_call(
        functools.partial(last_kernel, number=3, side=0),
        in_specs=[smem, smem] + [vmem] * 4,
        out_specs=anywhere,
        out_shape=jax.ShapeDtypeStruct(queries.shape, queries.dtype),
        scratch_shapes=[pltpu.VMEM((rows, half_heads), queries.dtype), pltpu.SemaphoreType.DMA],
        name="attend_last_near",
        **common,
    )(*last_args)
    return pl.pallas_call(
        join_kernel,
        in_specs=[smem, vmem, anywhere],
        out_specs=anywhere,
        out_shape=jax.ShapeDtypeStruct(queries.shape, queries.dtype),
        input_output_aliases={2: 0},
        scratch_shapes=[pltpu.SemaphoreType.DMA],
        name="join_heads",
        **common,
    )(place, to_other_core(out_far), out)


def solution(mesh):
    placed = P(AXES, None)
    return jax.shard_map(
        per_device, mesh=mesh, in_specs=(placed, placed, placed, P()), out_specs=placed, check_vma=False
    )
```

```python
import functools
import math

import jax
import jax.numpy as jnp
from jax import lax
from jax.experimental import pallas as pl
from jax.experimental.pallas import tpu as pltpu
from jax.sharding import PartitionSpec as P

HD = 128
REACH = 4
NEVER = -1e30
SCORE_SCALE = HD ** (-0.5) * math.log2(math.e)
SUM_ROWS = 16
PARTS = 2
AXES = ("ctx", "head")
SHIFT, SHIFT_OPPOSITE, OPPOSITE = "shift", "shift opposite", REACH - 1
ROUNDS = ((SHIFT, OPPOSITE), (OPPOSITE, SHIFT), (1, 2), (2, SHIFT_OPPOSITE), (SHIFT_OPPOSITE, 1))


def send_round(block, kinds):
    spans, cores = lax.axis_size("ctx"), lax.axis_size("head")
    pairs = []
    for s in range(spans):
        for core, kind in enumerate(kinds):
            if kind in (SHIFT, SHIFT_OPPOSITE):
                target = s + REACH
                if target >= spans or (kind == SHIFT_OPPOSITE and s % REACH >= REACH // 2):
                    continue
            else:
                target = s ^ kind
            pairs.append((s * cores + core, target * cores + core))
    return lax.ppermute(block, AXES, pairs)


def to_other_core(block):
    cores = lax.axis_size("head")
    return lax.ppermute(block, "head", [(h, cores - 1 - h) for h in range(cores)])


def doc_starts(lengths_ref, first, last):
    def one_doc(i, carry):
        start, lo_first, lo_last = carry
        start = start + lengths_ref[i]
        return start, jnp.where(start <= first, start, lo_first), jnp.where(start <= last, start, lo_last)

    zero = jnp.int32(0)
    _, lo_first, lo_last = lax.fori_loop(0, lengths_ref.shape[0], one_doc, (zero, zero, zero))
    return lo_first, lo_last


def doc_start_rows(lengths_ref, first_query, keys, rows):
    pos = first_query + lax.broadcasted_iota(jnp.int32, (8, rows), 1)

    def one_doc(i, carry):
        start, lo = carry
        start = start + lengths_ref[i]
        return start, jnp.where(start <= pos, start, lo)

    zero = jnp.zeros((8, rows), jnp.int32)
    lo = lax.fori_loop(0, lengths_ref.shape[0], one_doc, (jnp.int32(0), zero))[1]
    return jnp.concatenate([lo] * (keys // 8), axis=0)


def lanes(at, width):
    return pl.ds(pl.multiple_of(at * width, width), width)


def positions(starts, rows):
    return jnp.concatenate([start + lax.broadcasted_iota(jnp.int32, (rows, rows), 0) for start in starts], axis=0)


def turned(block, count):
    width = block.shape[1] // count
    return jnp.concatenate([block[:, i * width : (i + 1) * width].T for i in range(count)], axis=1)


def softmax_step(scores, allowed, max_before):
    if allowed is not None:
        allowed = jnp.concatenate([allowed] * (scores.shape[1] // allowed.shape[1]), axis=1)
        scores = jnp.where(allowed, scores, NEVER)
    row_max = jnp.max(scores, axis=0, keepdims=True)
    rescale = None
    if max_before is not None:
        row_max = jnp.maximum(max_before, row_max)
        rescale = jnp.exp2((max_before - row_max) * SCORE_SCALE)
    return jnp.exp2((scores - row_max) * SCORE_SCALE).astype(jnp.bfloat16), row_max, rescale


def pipeline(chunks, allowed, queries_of, keys_of, values_of, before_of, store):
    def scores_of(chunk):
        return jnp.dot(keys_of(chunk), queries_of(chunk), preferred_element_type=jnp.float32)

    ahead = scores_of(chunks[0])
    for number, chunk in enumerate(chunks):
        scores = ahead
        if number + 1 < len(chunks):
            ahead = scores_of(chunks[number + 1])
        max_before, acc_before = before_of(chunk)
        weights, row_max, rescale = softmax_step(scores, allowed, max_before)
        values = values_of(chunk)
        widened = jnp.concatenate([values.T, jnp.ones((SUM_ROWS, values.shape[0]), values.dtype)], axis=0)
        acc = jnp.dot(widened, weights, preferred_element_type=jnp.float32)
        if rescale is not None:
            acc = acc_before * rescale + acc
        store(chunk, row_max, acc)


def chunks_of(kv_heads):
    return [(g, part) for g in range(kv_heads) for part in range(PARTS)]


def pick_kernel(place_ref, q_ref, out_ref, sem):
    copy = pltpu.make_async_copy(q_ref.at[:, lanes(1 - place_ref[2], out_ref.shape[1])], out_ref, sem)
    copy.start()
    copy.wait()


def own_kernel(place_ref, lengths_ref, q_ref, q_far_ref, kv_ref, qt_ref, max_ref, acc_ref, q_near_ref, sem):
    rows, wide = q_far_ref.shape
    kv_heads = kv_ref.shape[3] // HD
    group_size = wide // (kv_heads * HD)
    width = group_size * rows // PARTS
    half = place_ref[2]
    fetch = pltpu.make_async_copy(q_ref.at[:, lanes(half, wide)], q_near_ref, sem)
    fetch.start()
    starts = place_ref[0], place_ref[1]

    def tokens(side, q_side_ref):
        first = starts[side]
        query_pos = first + lax.broadcasted_iota(jnp.int32, (rows, rows), 1)
        key_pos = positions([first], rows)
        diagonal = (key_pos >= doc_start_rows(lengths_ref, first, rows, rows)) & (key_pos <= query_pos)
        earlier = positions([starts[1 - side]], rows) >= doc_start_rows(lengths_ref, first, rows, rows)

        def at(chunk):
            begin = ((side * kv_heads + chunk[0]) * PARTS + chunk[1]) * width
            return slice(begin, begin + width)

        for chunk in chunks_of(kv_heads):
            begin = (chunk[0] * PARTS + chunk[1]) * (group_size // PARTS) * HD
            qt_ref[:, at(chunk)] = turned(
                q_side_ref[:, begin : begin + group_size // PARTS * HD], group_size // PARTS
            )

        def store(chunk, row_max, acc):
            max_ref[:, at(chunk)] = jnp.broadcast_to(row_max, (8, width))
            acc_ref[:, at(chunk)] = acc

        def work(blocks, allowed):
            def of(i):
                return lambda chunk: jnp.concatenate(
                    [kv_ref[block, i, :, chunk[0] * HD : (chunk[0] + 1) * HD] for block in blocks], axis=0
                )

            pipeline(
                chunks_of(kv_heads),
                allowed,
                lambda chunk: qt_ref[:, at(chunk)],
                of(0),
                of(1),
                lambda chunk: (None, None),
                store,
            )

        pl.when(half == side)(lambda: work([side], diagonal))
        pl.when(half != side)(lambda: work([1 - side, side], jnp.concatenate([earlier, diagonal], axis=0)))

    tokens(1, q_far_ref)
    fetch.wait()
    tokens(0, q_near_ref)


def span_steps(place_ref, lengths_ref, kv_ref, qt_ref, number, side, load, store):
    rows = kv_ref.shape[2]
    kv_heads = kv_ref.shape[3] // HD
    width = qt_ref.shape[1] // (2 * kv_heads * PARTS)
    first = place_ref[side]
    key_starts = place_ref[3 + 2 * number], place_ref[4 + 2 * number]
    lo_first, lo_last = doc_starts(lengths_ref, first, first + rows - 1)
    needed = jnp.maximum(key_starts[0], key_starts[1]) + rows > lo_first
    whole = jnp.minimum(key_starts[0], key_starts[1]) >= lo_last

    def at(chunk):
        begin = ((side * kv_heads + chunk[0]) * PARTS + chunk[1]) * width
        return slice(begin, begin + width)

    def of(i):
        return lambda chunk: jnp.concatenate(
            [kv_ref[block, i, :, chunk[0] * HD : (chunk[0] + 1) * HD] for block in range(2)], axis=0
        )

    def work(masked):
        allowed = None
        if masked:
            allowed = positions(key_starts, rows) >= doc_start_rows(lengths_ref, first, 2 * rows, rows)
        pipeline(
            chunks_of(kv_heads),
            allowed,
            lambda chunk: qt_ref[:, at(chunk)],
            of(0),
            of(1),
            lambda chunk: load(at(chunk)),
            lambda chunk, row_max, acc: store(chunk, at(chunk), row_max, acc),
        )

    pl.when(whole)(lambda: work(False))
    pl.when(needed & jnp.logical_not(whole))(lambda: work(True))
    return needed


def span_kernel(place_ref, lengths_ref, *refs, numbers):
    kv_refs, (qt_ref, _, _, max_ref, acc_ref) = refs[: len(numbers)], refs[len(numbers) :]

    def load(at):
        return max_ref[:1, at], acc_ref[:, at]

    def store(chunk, at, row_max, acc):
        max_ref[:, at] = jnp.broadcast_to(row_max, (8, acc.shape[1]))
        acc_ref[:, at] = acc

    for number, kv_ref in zip(numbers, kv_refs):
        for side in range(2):
            span_steps(place_ref, lengths_ref, kv_ref, qt_ref, number, side, load, store)


def last_kernel(place_ref, lengths_ref, kv_ref, qt_ref, max_ref, acc_ref, out_ref, *refs, number, side):
    rows = kv_ref.shape[2]
    kv_heads = kv_ref.shape[3] // HD
    width = qt_ref.shape[1] // (2 * kv_heads * PARTS)
    out = out_ref
    if refs:
        out, sem = refs

    def load(at):
        return max_ref[:1, at], acc_ref[:, at]

    def finish(chunk, at, row_max, acc):
        begin = (chunk[0] * PARTS + chunk[1]) * width
        finished = (acc[:HD] * (1.0 / acc[HD : HD + 1])).astype(out.dtype)
        out[:, begin : begin + width] = turned(finished, width // rows)

    needed = span_steps(place_ref, lengths_ref, kv_ref, qt_ref, number, side, load, finish)

    @pl.when(jnp.logical_not(needed))
    def _():
        for chunk in chunks_of(kv_heads):
            begin = ((side * kv_heads + chunk[0]) * PARTS + chunk[1]) * width
            finish(chunk, None, *load(slice(begin, begin + width)))

    if refs:
        copy = pltpu.make_async_copy(out, out_ref.at[:, lanes(place_ref[2], out.shape[1])], sem)
        copy.start()
        copy.wait()


def join_kernel(place_ref, far_ref, out_in, out_ref, sem):
    del out_in
    copy = pltpu.make_async_copy(far_ref, out_ref.at[:, lanes(1 - place_ref[2], far_ref.shape[1])], sem)
    copy.start()
    copy.wait()


def per_device(queries, keys, values, doc_lengths):
    rows, all_heads = queries.shape
    half_heads = all_heads // 2
    head_rows = (all_heads // HD) * rows
    half, span = lax.axis_index("head"), lax.axis_index("ctx")
    cores = lax.axis_size("head")
    place_in_group = lax.rem(span, REACH)

    nowhere = -2 * REACH

    def origin(kind):
        if kind == SHIFT:
            return span - REACH
        late = place_in_group >= REACH // 2
        from_place = place_in_group ^ (OPPOSITE if kind == SHIFT_OPPOSITE else kind)
        here = span - place_in_group + from_place
        if kind == SHIFT_OPPOSITE:
            return jnp.where(late, nowhere, here - REACH)
        if kind == OPPOSITE:
            return jnp.where(late, here, nowhere)
        return here - jnp.where(from_place > place_in_group, REACH, 0)

    parts = [(span * cores + half) * rows, (span * cores + 1 - half) * rows, half]
    for kinds in ROUNDS:
        start = jnp.where(half == 0, origin(kinds[0]), origin(kinds[1]))
        parts += [(start * cores + half) * rows, (start * cores + 1 - half) * rows]
    place = jnp.stack(parts).astype(jnp.int32)

    vmem = pl.BlockSpec(memory_space=pltpu.VMEM)
    smem = pl.BlockSpec(memory_space=pltpu.SMEM)
    anywhere = pl.BlockSpec(memory_space=pl.ANY)
    hbm = pl.BlockSpec(memory_space=pltpu.MemorySpace.HBM)
    qt_shape = jax.ShapeDtypeStruct((HD, head_rows), queries.dtype)
    max_shape = jax.ShapeDtypeStruct((8, head_rows), jnp.float32)
    acc_shape = jax.ShapeDtypeStruct((HD + SUM_ROWS, head_rows), jnp.float32)
    side_shape = jax.ShapeDtypeStruct((rows, half_heads), queries.dtype)
    common = dict(
        compiler_params=pltpu.CompilerParams(vmem_limit_bytes=24 * 1024 * 1024),
        cost_estimate=pl.CostEstimate(flops=0, bytes_accessed=0, transcendentals=0),
    )

    def heads_of(array, core):
        width = array.shape[1] // 2
        return lax.dynamic_slice_in_dim(array, core * width, width, 1)

    to_give = jnp.stack([heads_of(keys, 1 - half), heads_of(values, 1 - half)])
    given = to_other_core(to_give)
    given, queries = lax.optimization_barrier((given, queries))
    own = jnp.stack([jnp.stack([heads_of(keys, half), heads_of(values, half)]), given])
    arrived = [send_round(own, kinds) for kinds in ROUNDS[:2]]
    q_far = to_other_core(
        pl.pallas_call(
            pick_kernel,
            in_specs=[smem, hbm],
            out_specs=vmem,
            out_shape=side_shape,
            scratch_shapes=[pltpu.SemaphoreType.DMA],
            name="pick_queries",
            **common,
        )(place, queries)
    )

    qt, row_max, acc = pl.pallas_call(
        own_kernel,
        in_specs=[smem, smem, hbm, vmem, vmem],
        out_specs=(vmem, vmem, vmem),
        out_shape=(qt_shape, max_shape, acc_shape),
        scratch_shapes=[pltpu.VMEM((rows, half_heads), queries.dtype), pltpu.SemaphoreType.DMA],
        name="attend_own",
        **common,
    )(place, doc_lengths, queries, q_far, own)

    def attend(kv, row_max, acc, number):
        return pl.pallas_call(
            functools.partial(span_kernel, numbers=tuple(range(number, number + len(kv)))),
            in_specs=[smem, smem] + [vmem] * (len(kv) + 3),
            out_specs=(vmem, vmem),
            out_shape=(max_shape, acc_shape),
            input_output_aliases={len(kv) + 3: 0, len(kv) + 4: 1},
            name="attend_spans",
            **common,
        )(place, doc_lengths, *kv, qt, row_max, acc)

    arrived[0], arrived[1], acc = lax.optimization_barrier((arrived[0], arrived[1], acc))
    behind = jnp.where(half == 0, arrived[0], arrived[1])
    opposite = jnp.where(half == 0, arrived[1], arrived[0])

    def to_send(kind):
        if kind == SHIFT_OPPOSITE:
            return opposite
        return jnp.where((place_in_group ^ kind) > place_in_group, own, behind)

    for kinds in ROUNDS[2:]:
        arrived.append(send_round(jnp.where(half == 0, to_send(kinds[0]), to_send(kinds[1])), kinds))
    row_max, acc = attend(arrived[:2], row_max, acc, 0)
    row_max, acc = attend(arrived[2:3], row_max, acc, 2)
    row_max, acc = attend(arrived[3:4], row_max, acc, 3)

    last_args = (place, doc_lengths, arrived[4], qt, row_max, acc)
    out_far = pl.pallas_call(
        functools.partial(last_kernel, number=4, side=1),
        in_specs=[smem, smem] + [vmem] * 4,
        out_specs=vmem,
        out_shape=side_shape,
        name="attend_last_far",
        **common,
    )(*last_args)
    out = pl.pallas_call(
        functools.partial(last_kernel, number=4, side=0),
        in_specs=[smem, smem] + [vmem] * 4,
        out_specs=anywhere,
        out_shape=jax.ShapeDtypeStruct(queries.shape, queries.dtype),
        scratch_shapes=[pltpu.VMEM((rows, half_heads), queries.dtype), pltpu.SemaphoreType.DMA],
        name="attend_last_near",
        **common,
    )(*last_args)
    return pl.pallas_call(
        join_kernel,
        in_specs=[smem, vmem, anywhere],
        out_specs=anywhere,
        out_shape=jax.ShapeDtypeStruct(queries.shape, queries.dtype),
        input_output_aliases={2: 0},
        scratch_shapes=[pltpu.SemaphoreType.DMA],
        name="join_heads",
        **common,
    )(place, to_other_core(out_far), out)


def solution(mesh):
    placed = P(AXES, None)
    return jax.shard_map(
        per_device, mesh=mesh, in_specs=(placed, placed, placed, P()), out_specs=placed, check_vma=False
    )
```

```python
import functools
import math

import jax
import jax.numpy as jnp
from jax import lax
from jax.experimental import pallas as pl
from jax.experimental.pallas import tpu as pltpu
from jax.sharding import PartitionSpec as P

HD = 128
REACH = 4
NEVER = -1e30
SCORE_SCALE = HD ** (-0.5) * math.log2(math.e)
SUM_ROWS = 16
PARTS = 2
AXES = ("ctx", "head")
SHIFT, SHIFT_OPPOSITE, OPPOSITE = "shift", "shift opposite", REACH - 1
ROUNDS = ((SHIFT, OPPOSITE), (OPPOSITE, SHIFT), (1, 2), (2, SHIFT_OPPOSITE), (SHIFT_OPPOSITE, 1))


def send_round(block, kinds):
    spans, cores = lax.axis_size("ctx"), lax.axis_size("head")
    pairs = []
    for s in range(spans):
        for core, kind in enumerate(kinds):
            if kind in (SHIFT, SHIFT_OPPOSITE):
                target = s + REACH
                if target >= spans or (kind == SHIFT_OPPOSITE and s % REACH >= REACH // 2):
                    continue
            else:
                target = s ^ kind
            pairs.append((s * cores + core, target * cores + core))
    return lax.ppermute(block, AXES, pairs)


def to_other_core(block):
    cores = lax.axis_size("head")
    return lax.ppermute(block, "head", [(h, cores - 1 - h) for h in range(cores)])


def doc_starts(lengths_ref, first, last):
    def one_doc(i, carry):
        start, lo_first, lo_last = carry
        start = start + lengths_ref[i]
        return start, jnp.where(start <= first, start, lo_first), jnp.where(start <= last, start, lo_last)

    zero = jnp.int32(0)
    _, lo_first, lo_last = lax.fori_loop(0, lengths_ref.shape[0], one_doc, (zero, zero, zero))
    return lo_first, lo_last


def doc_start_rows(lengths_ref, first_query, keys, rows):
    pos = first_query + lax.broadcasted_iota(jnp.int32, (8, rows), 1)

    def one_doc(i, carry):
        start, lo = carry
        start = start + lengths_ref[i]
        return start, jnp.where(start <= pos, start, lo)

    zero = jnp.zeros((8, rows), jnp.int32)
    lo = lax.fori_loop(0, lengths_ref.shape[0], one_doc, (jnp.int32(0), zero))[1]
    return jnp.concatenate([lo] * (keys // 8), axis=0)


def lanes(at, width):
    return pl.ds(pl.multiple_of(at * width, width), width)


def positions(starts, rows):
    return jnp.concatenate([start + lax.broadcasted_iota(jnp.int32, (rows, rows), 0) for start in starts], axis=0)


def turned(block, count):
    width = block.shape[1] // count
    return jnp.concatenate([block[:, i * width : (i + 1) * width].T for i in range(count)], axis=1)


def softmax_step(scores, allowed, max_before):
    if allowed is not None:
        allowed = jnp.concatenate([allowed] * (scores.shape[1] // allowed.shape[1]), axis=1)
        scores = jnp.where(allowed, scores, NEVER)
    row_max = jnp.max(scores, axis=0, keepdims=True)
    rescale = None
    if max_before is not None:
        row_max = jnp.maximum(max_before, row_max)
        rescale = jnp.exp2((max_before - row_max) * SCORE_SCALE)
    return jnp.exp2((scores - row_max) * SCORE_SCALE).astype(jnp.bfloat16), row_max, rescale


def pipeline(kv_heads, ahead_ref, allowed, scores_of, values_of, before_of, store):
    def finish(g, part, scores):
        max_before, acc_before = before_of(g, part)
        weights, row_max, rescale = softmax_step(scores, allowed, max_before)
        values = values_of(g)
        widened = jnp.concatenate([values.T, jnp.ones((SUM_ROWS, values.shape[0]), values.dtype)], axis=0)
        acc = jnp.dot(widened, weights, preferred_element_type=jnp.float32)
        if rescale is not None:
            acc = acc_before * rescale + acc
        store(g, part, row_max, acc)

    ahead_ref[...] = scores_of(0, 0)

    def one_head(g, _):
        scores = ahead_ref[...]
        for part in range(PARTS):
            if part + 1 < PARTS:
                later = scores_of(g, part + 1)
            else:
                later = scores_of(jnp.minimum(g + 1, kv_heads - 1), 0)
            finish(g, part, scores)
            scores = later
        ahead_ref[...] = scores
        return 0

    lax.fori_loop(0, kv_heads, one_head, 0)


def pick_kernel(place_ref, q_ref, out_ref, sem):
    copy = pltpu.make_async_copy(q_ref.at[:, lanes(1 - place_ref[2], out_ref.shape[1])], out_ref, sem)
    copy.start()
    copy.wait()


def own_kernel(place_ref, lengths_ref, q_ref, kv_ref, *refs, side):
    if side == 0:
        qt_ref, max_ref, acc_ref, ahead_ref, q_side_ref, sem = refs
        fetch = pltpu.make_async_copy(q_ref.at[:, lanes(place_ref[2], q_side_ref.shape[1])], q_side_ref, sem)
        fetch.start()
    else:
        _, _, _, qt_ref, max_ref, acc_ref, ahead_ref = refs
        q_side_ref = q_ref
    rows, wide = q_side_ref.shape
    kv_heads = kv_ref.shape[3] // HD
    group_size = wide // (kv_heads * HD)
    width = group_size * rows // PARTS
    half = place_ref[2]
    first, other = place_ref[side], place_ref[1 - side]
    query_pos = first + lax.broadcasted_iota(jnp.int32, (rows, rows), 1)
    lows = doc_start_rows(lengths_ref, first, rows, rows)
    key_pos = positions([first], rows)
    diagonal = (key_pos >= lows) & (key_pos <= query_pos)
    earlier = positions([other], rows) >= lows
    if side == 0:
        fetch.wait()

    def at(g, part):
        return lanes((side * kv_heads + g) * PARTS + part, width)

    def turn_queries(g, _):
        for part in range(PARTS):
            q = q_side_ref[:, lanes(g * PARTS + part, group_size // PARTS * HD)]
            qt_ref[:, at(g, part)] = turned(q, group_size // PARTS)
        return 0

    lax.fori_loop(0, kv_heads, turn_queries, 0)

    def store(g, part, row_max, acc):
        max_ref[:, at(g, part)] = jnp.broadcast_to(row_max, (8, width))
        acc_ref[:, at(g, part)] = acc

    def work(blocks, allowed):
        def of(i, g):
            return jnp.concatenate([kv_ref[block, i, :, lanes(g, HD)] for block in blocks], axis=0)

        pipeline(
            kv_heads,
            ahead_ref.at[: len(blocks) * rows],
            allowed,
            lambda g, part: jnp.dot(of(0, g), qt_ref[:, at(g, part)], preferred_element_type=jnp.float32),
            lambda g: of(1, g),
            lambda g, part: (None, None),
            store,
        )

    pl.when(half == side)(lambda: work([side], diagonal))
    pl.when(half != side)(lambda: work([1 - side, side], jnp.concatenate([earlier, diagonal], axis=0)))


def span_steps(place_ref, lengths_ref, kv_ref, qt_ref, ahead_ref, number, side, load, store):
    rows = kv_ref.shape[2]
    kv_heads = kv_ref.shape[3] // HD
    width = qt_ref.shape[1] // (2 * kv_heads * PARTS)
    first = place_ref[side]
    key_starts = place_ref[3 + 2 * number], place_ref[4 + 2 * number]
    lo_first, lo_last = doc_starts(lengths_ref, first, first + rows - 1)
    needed = jnp.maximum(key_starts[0], key_starts[1]) + rows > lo_first
    whole = jnp.minimum(key_starts[0], key_starts[1]) >= lo_last

    def at(g, part):
        return lanes((side * kv_heads + g) * PARTS + part, width)

    def of(i, g):
        return jnp.concatenate([kv_ref[block, i, :, lanes(g, HD)] for block in range(2)], axis=0)

    def work(masked):
        allowed = None
        if masked:
            allowed = positions(key_starts, rows) >= doc_start_rows(lengths_ref, first, 2 * rows, rows)
        pipeline(
            kv_heads,
            ahead_ref,
            allowed,
            lambda g, part: jnp.dot(of(0, g), qt_ref[:, at(g, part)], preferred_element_type=jnp.float32),
            lambda g: of(1, g),
            lambda g, part: load(at(g, part)),
            lambda g, part, row_max, acc: store(g, part, at(g, part), row_max, acc),
        )

    pl.when(whole)(lambda: work(False))
    pl.when(needed & jnp.logical_not(whole))(lambda: work(True))
    return needed


def span_kernel(place_ref, lengths_ref, *refs, numbers):
    kv_refs, (qt_ref, _, _, max_ref, acc_ref, ahead_ref) = refs[: len(numbers)], refs[len(numbers) :]

    def load(at):
        return max_ref[:1, at], acc_ref[:, at]

    def store(g, part, at, row_max, acc):
        max_ref[:, at] = jnp.broadcast_to(row_max, (8, acc.shape[1]))
        acc_ref[:, at] = acc

    for number, kv_ref in zip(numbers, kv_refs):

        def one_side(side, _):
            span_steps(place_ref, lengths_ref, kv_ref, qt_ref, ahead_ref, number, side, load, store)
            return 0

        lax.fori_loop(0, 2, one_side, 0)


def last_kernel(place_ref, lengths_ref, kv_ref, qt_ref, max_ref, acc_ref, out_ref, ahead_ref, *refs, number, side):
    rows = kv_ref.shape[2]
    kv_heads = kv_ref.shape[3] // HD
    width = qt_ref.shape[1] // (2 * kv_heads * PARTS)
    out = out_ref
    if refs:
        out, sem = refs

    def load(at):
        return max_ref[:1, at], acc_ref[:, at]

    def finish(g, part, at, row_max, acc):
        finished = (acc[:HD] * (1.0 / acc[HD : HD + 1])).astype(out.dtype)
        out[:, lanes(g * PARTS + part, width)] = turned(finished, width // rows)

    needed = span_steps(place_ref, lengths_ref, kv_ref, qt_ref, ahead_ref, number, side, load, finish)

    @pl.when(jnp.logical_not(needed))
    def _():
        def one_head(g, _):
            for part in range(PARTS):
                finish(g, part, None, *load(lanes((side * kv_heads + g) * PARTS + part, width)))
            return 0

        lax.fori_loop(0, kv_heads, one_head, 0)

    if refs:
        copy = pltpu.make_async_copy(out, out_ref.at[:, lanes(place_ref[2], out.shape[1])], sem)
        copy.start()
        copy.wait()


def join_kernel(place_ref, far_ref, out_in, out_ref, sem):
    del out_in
    copy = pltpu.make_async_copy(far_ref, out_ref.at[:, lanes(1 - place_ref[2], far_ref.shape[1])], sem)
    copy.start()
    copy.wait()


def per_device(queries, keys, values, doc_lengths):
    rows, all_heads = queries.shape
    half_heads = all_heads // 2
    head_rows = (all_heads // HD) * rows
    half, span = lax.axis_index("head"), lax.axis_index("ctx")
    cores = lax.axis_size("head")
    place_in_group = lax.rem(span, REACH)

    nowhere = -2 * REACH

    def origin(kind):
        if kind == SHIFT:
            return span - REACH
        late = place_in_group >= REACH // 2
        from_place = place_in_group ^ (OPPOSITE if kind == SHIFT_OPPOSITE else kind)
        here = span - place_in_group + from_place
        if kind == SHIFT_OPPOSITE:
            return jnp.where(late, nowhere, here - REACH)
        if kind == OPPOSITE:
            return jnp.where(late, here, nowhere)
        return here - jnp.where(from_place > place_in_group, REACH, 0)

    parts = [(span * cores + half) * rows, (span * cores + 1 - half) * rows, half]
    for kinds in ROUNDS:
        start = jnp.where(half == 0, origin(kinds[0]), origin(kinds[1]))
        parts += [(start * cores + half) * rows, (start * cores + 1 - half) * rows]
    place = jnp.stack(parts).astype(jnp.int32)

    vmem = pl.BlockSpec(memory_space=pltpu.VMEM)
    smem = pl.BlockSpec(memory_space=pltpu.SMEM)
    anywhere = pl.BlockSpec(memory_space=pl.ANY)
    hbm = pl.BlockSpec(memory_space=pltpu.MemorySpace.HBM)
    qt_shape = jax.ShapeDtypeStruct((HD, head_rows), queries.dtype)
    max_shape = jax.ShapeDtypeStruct((8, head_rows), jnp.float32)
    acc_shape = jax.ShapeDtypeStruct((HD + SUM_ROWS, head_rows), jnp.float32)
    side_shape = jax.ShapeDtypeStruct((rows, half_heads), queries.dtype)
    common = dict(
        compiler_params=pltpu.CompilerParams(vmem_limit_bytes=24 * 1024 * 1024),
        cost_estimate=pl.CostEstimate(flops=0, bytes_accessed=0, transcendentals=0),
    )

    def heads_of(array, core):
        width = array.shape[1] // 2
        return lax.dynamic_slice_in_dim(array, core * width, width, 1)

    to_give = jnp.stack([heads_of(keys, 1 - half), heads_of(values, 1 - half)])
    given = to_other_core(to_give)
    given, queries = lax.optimization_barrier((given, queries))
    own = jnp.stack([jnp.stack([heads_of(keys, half), heads_of(values, half)]), given])
    arrived = [send_round(own, kinds) for kinds in ROUNDS[:2]]
    q_far = to_other_core(
        pl.pallas_call(
            pick_kernel,
            in_specs=[smem, hbm],
            out_specs=vmem,
            out_shape=side_shape,
            scratch_shapes=[pltpu.SemaphoreType.DMA],
            name="pick_queries",
            **common,
        )(place, queries)
    )

    group_columns = half_heads // (keys.shape[1] // 2) * rows // PARTS
    ahead = pltpu.VMEM((2 * rows, group_columns), jnp.float32)
    state_shapes = (qt_shape, max_shape, acc_shape)
    state = pl.pallas_call(
        functools.partial(own_kernel, side=0),
        in_specs=[smem, smem, hbm, vmem],
        out_specs=(vmem, vmem, vmem),
        out_shape=state_shapes,
        scratch_shapes=[ahead, pltpu.VMEM((rows, half_heads), queries.dtype), pltpu.SemaphoreType.DMA],
        name="attend_own_near",
        **{**common, "cost_estimate": pl.CostEstimate(flops=10**11, bytes_accessed=0, transcendentals=0)},
    )(place, doc_lengths, queries, own)
    qt, row_max, acc = pl.pallas_call(
        functools.partial(own_kernel, side=1),
        in_specs=[smem, smem] + [vmem] * 5,
        out_specs=(vmem, vmem, vmem),
        out_shape=state_shapes,
        input_output_aliases={4: 0, 5: 1, 6: 2},
        scratch_shapes=[ahead],
        name="attend_own_far",
        **common,
    )(place, doc_lengths, q_far, own, *state)

    def attend(kv, row_max, acc, number):
        return pl.pallas_call(
            functools.partial(span_kernel, numbers=tuple(range(number, number + len(kv)))),
            in_specs=[smem, smem] + [vmem] * (len(kv) + 3),
            out_specs=(vmem, vmem),
            out_shape=(max_shape, acc_shape),
            input_output_aliases={len(kv) + 3: 0, len(kv) + 4: 1},
            scratch_shapes=[ahead],
            name="attend_spans",
            **common,
        )(place, doc_lengths, *kv, qt, row_max, acc)

    arrived[0], arrived[1], acc = lax.optimization_barrier((arrived[0], arrived[1], acc))
    behind = jnp.where(half == 0, arrived[0], arrived[1])
    opposite = jnp.where(half == 0, arrived[1], arrived[0])

    def to_send(kind):
        if kind == SHIFT_OPPOSITE:
            return opposite
        return jnp.where((place_in_group ^ kind) > place_in_group, own, behind)

    for kinds in ROUNDS[2:]:
        arrived.append(send_round(jnp.where(half == 0, to_send(kinds[0]), to_send(kinds[1])), kinds))
    row_max, acc = attend(arrived[:2], row_max, acc, 0)
    row_max, acc = attend(arrived[2:3], row_max, acc, 2)
    row_max, acc = attend(arrived[3:4], row_max, acc, 3)

    last_args = (place, doc_lengths, arrived[4], qt, row_max, acc)
    out_far = pl.pallas_call(
        functools.partial(last_kernel, number=4, side=1),
        in_specs=[smem, smem] + [vmem] * 4,
        out_specs=vmem,
        out_shape=side_shape,
        scratch_shapes=[ahead],
        name="attend_last_far",
        **common,
    )(*last_args)
    out = pl.pallas_call(
        functools.partial(last_kernel, number=4, side=0),
        in_specs=[smem, smem] + [vmem] * 4,
        out_specs=anywhere,
        out_shape=jax.ShapeDtypeStruct(queries.shape, queries.dtype),
        scratch_shapes=[ahead, pltpu.VMEM((rows, half_heads), queries.dtype), pltpu.SemaphoreType.DMA],
        name="attend_last_near",
        **common,
    )(*last_args)
    return pl.pallas_call(
        join_kernel,
        in_specs=[smem, vmem, anywhere],
        out_specs=anywhere,
        out_shape=jax.ShapeDtypeStruct(queries.shape, queries.dtype),
        input_output_aliases={2: 0},
        scratch_shapes=[pltpu.SemaphoreType.DMA],
        name="join_heads",
        **common,
    )(place, to_other_core(out_far), out)


def solution(mesh):
    placed = P(AXES, None)
    return jax.shard_map(
        per_device, mesh=mesh, in_specs=(placed, placed, placed, P()), out_specs=placed, check_vma=False
    )
```

```python
import functools
import math

import jax
import jax.numpy as jnp
from jax import lax
from jax.experimental import pallas as pl
from jax.experimental.pallas import tpu as pltpu
from jax.sharding import PartitionSpec as P

HD = 128
REACH = 4
NEVER = -1e30
SCORE_SCALE = HD ** (-0.5) * math.log2(math.e)
SUM_ROWS = 16
PARTS = 2
AXES = ("ctx", "head")
SHIFT, SHIFT_OPPOSITE, OPPOSITE = "shift", "shift opposite", REACH - 1
ROUNDS = ((SHIFT, SHIFT), (OPPOSITE, OPPOSITE), (1, 2), (SHIFT_OPPOSITE, SHIFT_OPPOSITE), (2, 1))


def send_round(block, kinds):
    spans, cores = lax.axis_size("ctx"), lax.axis_size("head")
    pairs = []
    for s in range(spans):
        for core, kind in enumerate(kinds):
            if kind in (SHIFT, SHIFT_OPPOSITE):
                target = s + REACH
                if target >= spans or (kind == SHIFT_OPPOSITE and s % REACH >= REACH // 2):
                    continue
            else:
                target = s ^ kind
            pairs.append((s * cores + core, target * cores + core))
    return lax.ppermute(block, AXES, pairs)


def to_other_core(block):
    cores = lax.axis_size("head")
    return lax.ppermute(block, "head", [(h, cores - 1 - h) for h in range(cores)])


def doc_starts(lengths_ref, first, last):
    def one_doc(i, carry):
        start, lo_first, lo_last = carry
        start = start + lengths_ref[i]
        return start, jnp.where(start <= first, start, lo_first), jnp.where(start <= last, start, lo_last)

    zero = jnp.int32(0)
    _, lo_first, lo_last = lax.fori_loop(0, lengths_ref.shape[0], one_doc, (zero, zero, zero))
    return lo_first, lo_last


def doc_start_rows(lengths_ref, first_query, keys, rows):
    pos = first_query + lax.broadcasted_iota(jnp.int32, (8, rows), 1)

    def one_doc(i, carry):
        start, lo = carry
        start = start + lengths_ref[i]
        return start, jnp.where(start <= pos, start, lo)

    zero = jnp.zeros((8, rows), jnp.int32)
    lo = lax.fori_loop(0, lengths_ref.shape[0], one_doc, (jnp.int32(0), zero))[1]
    return jnp.concatenate([lo] * (keys // 8), axis=0)


def lanes(at, width):
    return pl.ds(pl.multiple_of(at * width, width), width)


def positions(starts, rows):
    return jnp.concatenate([start + lax.broadcasted_iota(jnp.int32, (rows, rows), 0) for start in starts], axis=0)


def turned(block, count):
    width = block.shape[1] // count
    return jnp.concatenate([block[:, i * width : (i + 1) * width].T for i in range(count)], axis=1)


def softmax_step(scores, allowed, max_before):
    if allowed is not None:
        allowed = jnp.concatenate([allowed] * (scores.shape[1] // allowed.shape[1]), axis=1)
        scores = jnp.where(allowed, scores, NEVER)
    row_max = jnp.max(scores, axis=0, keepdims=True)
    rescale = None
    if max_before is not None:
        row_max = jnp.maximum(max_before, row_max)
        rescale = jnp.exp2((max_before - row_max) * SCORE_SCALE)
    return jnp.exp2((scores - row_max) * SCORE_SCALE).astype(jnp.bfloat16), row_max, rescale


def pipeline(kv_heads, ahead_ref, allowed, scores_of, values_of, before_of, store):
    def finish(g, part, scores):
        max_before, acc_before = before_of(g, part)
        weights, row_max, rescale = softmax_step(scores, allowed, max_before)
        values = values_of(g)
        widened = jnp.concatenate([values.T, jnp.ones((SUM_ROWS, values.shape[0]), values.dtype)], axis=0)
        acc = jnp.dot(widened, weights, preferred_element_type=jnp.float32)
        if rescale is not None:
            acc = acc_before * rescale + acc
        store(g, part, row_max, acc)

    ahead_ref[...] = scores_of(0, 0)
    step = 2 if kv_heads % 2 == 0 else 1

    def some_heads(i, _):
        scores = ahead_ref[...]
        for number in range(step * PARTS):
            g, part = i * step + number // PARTS, number % PARTS
            if number + 1 < step * PARTS:
                later = scores_of(i * step + (number + 1) // PARTS, (number + 1) % PARTS)
            else:
                later = scores_of(jnp.minimum((i + 1) * step, kv_heads - 1), 0)
            finish(g, part, scores)
            scores = later
        ahead_ref[...] = scores
        return 0

    lax.fori_loop(0, kv_heads // step, some_heads, 0)


def pick_kernel(place_ref, q_ref, out_ref, sem):
    copy = pltpu.make_async_copy(q_ref.at[:, lanes(1 - place_ref[2], out_ref.shape[1])], out_ref, sem)
    copy.start()
    copy.wait()


def own_kernel(place_ref, lengths_ref, q_ref, kv_ref, *refs, side):
    if side == 0:
        qt_ref, max_ref, acc_ref, ahead_ref, q_side_ref, sem = refs
        fetch = pltpu.make_async_copy(q_ref.at[:, lanes(place_ref[2], q_side_ref.shape[1])], q_side_ref, sem)
        fetch.start()
    else:
        _, _, _, qt_ref, max_ref, acc_ref, ahead_ref = refs
        q_side_ref = q_ref
    rows, wide = q_side_ref.shape
    kv_heads = kv_ref.shape[3] // HD
    group_size = wide // (kv_heads * HD)
    width = group_size * rows // PARTS
    half = place_ref[2]
    first, other = place_ref[side], place_ref[1 - side]
    query_pos = first + lax.broadcasted_iota(jnp.int32, (rows, rows), 1)
    lows = doc_start_rows(lengths_ref, first, rows, rows)
    key_pos = positions([first], rows)
    diagonal = (key_pos >= lows) & (key_pos <= query_pos)
    earlier = positions([other], rows) >= lows
    if side == 0:
        fetch.wait()

    def at(g, part):
        return lanes((side * kv_heads + g) * PARTS + part, width)

    def turn_queries(g, _):
        for part in range(PARTS):
            q = q_side_ref[:, lanes(g * PARTS + part, group_size // PARTS * HD)]
            qt_ref[:, at(g, part)] = turned(q, group_size // PARTS)
        return 0

    lax.fori_loop(0, kv_heads, turn_queries, 0)

    def store(g, part, row_max, acc):
        max_ref[:, at(g, part)] = jnp.broadcast_to(row_max, (8, width))
        acc_ref[:, at(g, part)] = acc

    def work(blocks, allowed):
        def of(i, g):
            return jnp.concatenate([kv_ref[block, i, :, lanes(g, HD)] for block in blocks], axis=0)

        pipeline(
            kv_heads,
            ahead_ref.at[: len(blocks) * rows],
            allowed,
            lambda g, part: jnp.dot(of(0, g), qt_ref[:, at(g, part)], preferred_element_type=jnp.float32),
            lambda g: of(1, g),
            lambda g, part: (None, None),
            store,
        )

    pl.when(half == side)(lambda: work([side], diagonal))
    pl.when(half != side)(lambda: work([1 - side, side], jnp.concatenate([earlier, diagonal], axis=0)))


def span_steps(place_ref, lengths_ref, kv_ref, qt_ref, ahead_ref, number, side, load, store):
    rows = kv_ref.shape[2]
    kv_heads = kv_ref.shape[3] // HD
    width = qt_ref.shape[1] // (2 * kv_heads * PARTS)
    first = place_ref[side]
    key_starts = place_ref[3 + 2 * number], place_ref[4 + 2 * number]
    lo_first, lo_last = doc_starts(lengths_ref, first, first + rows - 1)
    needed = jnp.maximum(key_starts[0], key_starts[1]) + rows > lo_first
    whole = jnp.minimum(key_starts[0], key_starts[1]) >= lo_last

    def at(g, part):
        return lanes((side * kv_heads + g) * PARTS + part, width)

    def of(i, g):
        return jnp.concatenate([kv_ref[block, i, :, lanes(g, HD)] for block in range(2)], axis=0)

    def work(masked):
        allowed = None
        if masked:
            allowed = positions(key_starts, rows) >= doc_start_rows(lengths_ref, first, 2 * rows, rows)
        pipeline(
            kv_heads,
            ahead_ref,
            allowed,
            lambda g, part: jnp.dot(of(0, g), qt_ref[:, at(g, part)], preferred_element_type=jnp.float32),
            lambda g: of(1, g),
            lambda g, part: load(at(g, part)),
            lambda g, part, row_max, acc: store(g, part, at(g, part), row_max, acc),
        )

    pl.when(whole)(lambda: work(False))
    pl.when(needed & jnp.logical_not(whole))(lambda: work(True))
    return needed


def span_kernel(place_ref, lengths_ref, *refs, numbers):
    kv_refs, (qt_ref, _, _, max_ref, acc_ref, ahead_ref) = refs[: len(numbers)], refs[len(numbers) :]

    def load(at):
        return max_ref[:1, at], acc_ref[:, at]

    def store(g, part, at, row_max, acc):
        max_ref[:, at] = jnp.broadcast_to(row_max, (8, acc.shape[1]))
        acc_ref[:, at] = acc

    for number, kv_ref in zip(numbers, kv_refs):

        def one_side(side, _):
            span_steps(place_ref, lengths_ref, kv_ref, qt_ref, ahead_ref, number, side, load, store)
            return 0

        lax.fori_loop(0, 2, one_side, 0)


def last_kernel(place_ref, lengths_ref, kv_ref, qt_ref, max_ref, acc_ref, out_ref, ahead_ref, *refs, number, side):
    rows = kv_ref.shape[2]
    kv_heads = kv_ref.shape[3] // HD
    width = qt_ref.shape[1] // (2 * kv_heads * PARTS)
    out = out_ref
    if refs:
        out, sems = refs

    def load(at):
        return max_ref[:1, at], acc_ref[:, at]

    def copy_out(piece):
        whole = place_ref[2] * (kv_heads * PARTS) + piece
        return pltpu.make_async_copy(
            out.at[:, lanes(piece, width)], out_ref.at[:, lanes(whole, width)], sems.at[piece]
        )

    def finish(g, part, at, row_max, acc):
        finished = (acc[:HD] * (1.0 / acc[HD : HD + 1])).astype(out.dtype)
        out[:, lanes(g * PARTS + part, width)] = turned(finished, width // rows)
        if refs:
            copy_out(g * PARTS + part).start()

    needed = span_steps(place_ref, lengths_ref, kv_ref, qt_ref, ahead_ref, number, side, load, finish)

    @pl.when(jnp.logical_not(needed))
    def _():
        def one_head(g, _):
            for part in range(PARTS):
                finish(g, part, None, *load(lanes((side * kv_heads + g) * PARTS + part, width)))
            return 0

        lax.fori_loop(0, kv_heads, one_head, 0)

    if refs:
        for piece in range(kv_heads * PARTS):
            copy_out(piece).wait()


def join_kernel(place_ref, far_ref, out_in, out_ref, sems):
    del out_in
    pieces = sems.shape[0]
    rows = far_ref.shape[0] // pieces
    columns = lanes(1 - place_ref[2], far_ref.shape[1])
    copies = [
        pltpu.make_async_copy(
            far_ref.at[pl.ds(i * rows, rows), :], out_ref.at[pl.ds(i * rows, rows), columns], sems.at[i]
        )
        for i in range(pieces)
    ]
    for copy in copies:
        copy.start()
    for copy in copies:
        copy.wait()


def per_device(queries, keys, values, doc_lengths):
    rows, all_heads = queries.shape
    half_heads = all_heads // 2
    head_rows = (all_heads // HD) * rows
    half, span = lax.axis_index("head"), lax.axis_index("ctx")
    cores = lax.axis_size("head")
    place_in_group = lax.rem(span, REACH)

    nowhere = -2 * REACH

    def origin(kind):
        if kind == SHIFT:
            return span - REACH
        late = place_in_group >= REACH // 2
        from_place = place_in_group ^ (OPPOSITE if kind == SHIFT_OPPOSITE else kind)
        here = span - place_in_group + from_place
        if kind == SHIFT_OPPOSITE:
            return jnp.where(late, nowhere, here - REACH)
        if kind == OPPOSITE:
            return jnp.where(late, here, nowhere)
        return here - jnp.where(from_place > place_in_group, REACH, 0)

    parts = [(span * cores + half) * rows, (span * cores + 1 - half) * rows, half]
    for kinds in ROUNDS:
        start = jnp.where(half == 0, origin(kinds[0]), origin(kinds[1]))
        parts += [(start * cores + half) * rows, (start * cores + 1 - half) * rows]
    place = jnp.stack(parts).astype(jnp.int32)

    vmem = pl.BlockSpec(memory_space=pltpu.VMEM)
    smem = pl.BlockSpec(memory_space=pltpu.SMEM)
    anywhere = pl.BlockSpec(memory_space=pl.ANY)
    hbm = pl.BlockSpec(memory_space=pltpu.MemorySpace.HBM)
    qt_shape = jax.ShapeDtypeStruct((HD, head_rows), queries.dtype)
    max_shape = jax.ShapeDtypeStruct((8, head_rows), jnp.float32)
    acc_shape = jax.ShapeDtypeStruct((HD + SUM_ROWS, head_rows), jnp.float32)
    side_shape = jax.ShapeDtypeStruct((rows, half_heads), queries.dtype)
    common = dict(
        compiler_params=pltpu.CompilerParams(vmem_limit_bytes=24 * 1024 * 1024),
        cost_estimate=pl.CostEstimate(flops=0, bytes_accessed=0, transcendentals=0),
    )

    def heads_of(array, core):
        width = array.shape[1] // 2
        return lax.dynamic_slice_in_dim(array, core * width, width, 1)

    to_give = jnp.stack([heads_of(keys, 1 - half), heads_of(values, 1 - half)])
    given = to_other_core(to_give)
    given, queries = lax.optimization_barrier((given, queries))
    own = jnp.stack([jnp.stack([heads_of(keys, half), heads_of(values, half)]), given])
    arrived = [send_round(own, kinds) for kinds in ROUNDS[:2]]
    q_far = to_other_core(
        pl.pallas_call(
            pick_kernel,
            in_specs=[smem, hbm],
            out_specs=vmem,
            out_shape=side_shape,
            scratch_shapes=[pltpu.SemaphoreType.DMA],
            name="pick_queries",
            **common,
        )(place, queries)
    )

    group_columns = half_heads // (keys.shape[1] // 2) * rows // PARTS
    ahead = pltpu.VMEM((2 * rows, group_columns), jnp.float32)
    state_shapes = (qt_shape, max_shape, acc_shape)
    state = pl.pallas_call(
        functools.partial(own_kernel, side=0),
        in_specs=[smem, smem, hbm, vmem],
        out_specs=(vmem, vmem, vmem),
        out_shape=state_shapes,
        scratch_shapes=[ahead, pltpu.VMEM((rows, half_heads), queries.dtype), pltpu.SemaphoreType.DMA],
        name="attend_own_near",
        **{**common, "cost_estimate": pl.CostEstimate(flops=10**11, bytes_accessed=0, transcendentals=0)},
    )(place, doc_lengths, queries, own)
    qt, row_max, acc = pl.pallas_call(
        functools.partial(own_kernel, side=1),
        in_specs=[smem, smem] + [vmem] * 5,
        out_specs=(vmem, vmem, vmem),
        out_shape=state_shapes,
        input_output_aliases={4: 0, 5: 1, 6: 2},
        scratch_shapes=[ahead],
        name="attend_own_far",
        **common,
    )(place, doc_lengths, q_far, own, *state)

    def attend(kv, row_max, acc, number):
        return pl.pallas_call(
            functools.partial(span_kernel, numbers=tuple(range(number, number + len(kv)))),
            in_specs=[smem, smem] + [vmem] * (len(kv) + 3),
            out_specs=(vmem, vmem),
            out_shape=(max_shape, acc_shape),
            input_output_aliases={len(kv) + 3: 0, len(kv) + 4: 1},
            scratch_shapes=[ahead],
            name="attend_spans",
            **common,
        )(place, doc_lengths, *kv, qt, row_max, acc)

    behind, opposite, acc = lax.optimization_barrier((arrived[0], arrived[1], acc))

    def plane_round(number):
        sends = [jnp.where((place_in_group ^ kind) > place_in_group, own, behind) for kind in ROUNDS[number]]
        return jnp.where(half == 0, *sends)

    first = send_round(plane_round(2), ROUNDS[2])
    relayed = send_round(opposite, ROUNDS[3])
    row_max, acc = attend([behind, opposite], row_max, acc, 0)
    to_second, acc = lax.optimization_barrier((plane_round(4), acc))
    second = send_round(to_second, ROUNDS[4])
    row_max, acc = attend([first], row_max, acc, 2)
    row_max, acc = attend([relayed], row_max, acc, 3)

    last_args = (place, doc_lengths, second, qt, row_max, acc)
    out_far = pl.pallas_call(
        functools.partial(last_kernel, number=4, side=1),
        in_specs=[smem, smem] + [vmem] * 4,
        out_specs=vmem,
        out_shape=side_shape,
        scratch_shapes=[ahead],
        name="attend_last_far",
        **common,
    )(*last_args)
    out = pl.pallas_call(
        functools.partial(last_kernel, number=4, side=0),
        in_specs=[smem, smem] + [vmem] * 4,
        out_specs=anywhere,
        out_shape=jax.ShapeDtypeStruct(queries.shape, queries.dtype),
        scratch_shapes=[
            ahead,
            pltpu.VMEM((rows, half_heads), queries.dtype),
            pltpu.SemaphoreType.DMA((half_heads // group_columns,)),
        ],
        name="attend_last_near",
        **common,
    )(*last_args)
    return pl.pallas_call(
        join_kernel,
        in_specs=[smem, vmem, anywhere],
        out_specs=anywhere,
        out_shape=jax.ShapeDtypeStruct(queries.shape, queries.dtype),
        input_output_aliases={2: 0},
        scratch_shapes=[pltpu.SemaphoreType.DMA((rows // 16,))],
        name="join_heads",
        **common,
    )(place, to_other_core(out_far), out)


def solution(mesh):
    placed = P(AXES, None)
    return jax.shard_map(
        per_device, mesh=mesh, in_specs=(placed, placed, placed, P()), out_specs=placed, check_vma=False
    )
```

```python
import functools
import math

import jax
import jax.numpy as jnp
from jax import lax
from jax.experimental import pallas as pl
from jax.experimental.pallas import tpu as pltpu
from jax.sharding import PartitionSpec as P

HD = 128
REACH = 4
NEVER = -1e30
SCORE_SCALE = HD ** (-0.5) * math.log2(math.e)
PARTS = 2
AXES = ("ctx", "head")
SHIFT, SHIFT_OPPOSITE, OPPOSITE = "shift", "shift opposite", REACH - 1
ROUNDS = ((SHIFT, SHIFT), (OPPOSITE, OPPOSITE), (1, 2), (SHIFT_OPPOSITE, SHIFT_OPPOSITE), (2, 1))


def send_round(block, kinds):
    spans, cores = lax.axis_size("ctx"), lax.axis_size("head")
    pairs = []
    for s in range(spans):
        for core, kind in enumerate(kinds):
            if kind in (SHIFT, SHIFT_OPPOSITE):
                target = s + REACH
                if target >= spans or (kind == SHIFT_OPPOSITE and s % REACH >= REACH // 2):
                    continue
            else:
                target = s ^ kind
            pairs.append((s * cores + core, target * cores + core))
    return lax.ppermute(block, AXES, pairs)


def to_other_core(block):
    cores = lax.axis_size("head")
    return lax.ppermute(block, "head", [(h, cores - 1 - h) for h in range(cores)])


def doc_starts(lengths_ref, first, last):
    def one_doc(i, carry):
        start, lo_first, lo_last = carry
        start = start + lengths_ref[i]
        return start, jnp.where(start <= first, start, lo_first), jnp.where(start <= last, start, lo_last)

    zero = jnp.int32(0)
    _, lo_first, lo_last = lax.fori_loop(0, lengths_ref.shape[0], one_doc, (zero, zero, zero))
    return lo_first, lo_last


def doc_start_rows(lengths_ref, first_query, rows):
    pos = first_query + lax.broadcasted_iota(jnp.int32, (rows, rows), 0)

    def one_doc(i, carry):
        start, lo = carry
        start = start + lengths_ref[i]
        return start, jnp.where(start <= pos, start, lo)

    zero = jnp.zeros((rows, rows), jnp.int32)
    return lax.fori_loop(0, lengths_ref.shape[0], one_doc, (jnp.int32(0), zero))[1]


def block_of(at, size):
    return pl.ds(pl.multiple_of(at * size, size), size)


def positions(start, rows):
    return start + lax.broadcasted_iota(jnp.int32, (rows, rows), 1)


def softmax_step(scores, allowed, max_before):
    if allowed is not None:
        allowed = jnp.concatenate([allowed] * (scores.shape[0] // allowed.shape[0]), axis=0)
        scores = jnp.where(allowed, scores, NEVER)
    row_max = jnp.broadcast_to(jnp.max(scores, axis=1, keepdims=True), (scores.shape[0], HD))
    rescale = None
    if max_before is not None:
        row_max = jnp.maximum(max_before, row_max)
        rescale = jnp.exp2((max_before - row_max) * SCORE_SCALE)
    shift = jnp.concatenate([row_max] * (scores.shape[1] // HD), axis=1)
    return jnp.exp2((scores - shift) * SCORE_SCALE).astype(jnp.bfloat16), row_max, rescale


def scores_for(queries, keys):
    return lax.dot_general(queries, keys, (((1,), (1,)), ((), ())), preferred_element_type=jnp.float32)


def pipeline(kv_heads, ahead_ref, allowed, scores_of, values_of, before_of, store):
    def finish(g, part, scores):
        max_before, acc_before = before_of(g, part)
        weights, row_max, rescale = softmax_step(scores, allowed, max_before)
        values = values_of(g)
        widened = jnp.concatenate([values, jnp.ones_like(values)], axis=1)
        acc = jnp.dot(weights, widened, preferred_element_type=jnp.float32)
        if rescale is not None:
            acc = acc_before * jnp.concatenate([rescale] * 2, axis=1) + acc
        store(g, part, row_max, acc)

    ahead_ref[...] = scores_of(0, 0)

    def one_head(g, _):
        scores = ahead_ref[...]
        for part in range(PARTS):
            if part + 1 < PARTS:
                later = scores_of(g, part + 1)
            else:
                later = scores_of(jnp.minimum(g + 1, kv_heads - 1), 0)
            finish(g, part, scores)
            scores = later
        ahead_ref[...] = scores
        return 0

    lax.fori_loop(0, kv_heads, one_head, 0)


def pick_kernel(place_ref, q_ref, out_ref, sem):
    copy = pltpu.make_async_copy(q_ref.at[:, block_of(1 - place_ref[2], out_ref.shape[1])], out_ref, sem)
    copy.start()
    copy.wait()


def own_kernel(place_ref, lengths_ref, q_ref, kv_ref, *refs, side):
    if side == 0:
        queries_ref, max_ref, acc_ref, ahead_ref, q_side_ref, sem = refs
        fetch = pltpu.make_async_copy(q_ref.at[:, block_of(place_ref[2], q_side_ref.shape[1])], q_side_ref, sem)
        fetch.start()
    else:
        _, _, _, queries_ref, max_ref, acc_ref, ahead_ref = refs
        q_side_ref = q_ref
    rows, wide = q_side_ref.shape
    kv_heads = kv_ref.shape[3] // HD
    heads = wide // (kv_heads * PARTS * HD)
    half = place_ref[2]
    first, other = place_ref[side], place_ref[1 - side]
    query_pos = first + lax.broadcasted_iota(jnp.int32, (rows, rows), 0)
    lows = doc_start_rows(lengths_ref, first, rows)
    key_pos = positions(first, rows)
    diagonal = (key_pos >= lows) & (key_pos <= query_pos)
    earlier = positions(other, rows) >= lows
    if side == 0:
        fetch.wait()

    def at(g, part):
        return block_of((side * kv_heads + g) * PARTS + part, heads * rows)

    def place_queries(i, _):
        q = q_side_ref[:, block_of(i, heads * HD)]
        queries_ref[block_of(side * kv_heads * PARTS + i, heads * rows), :] = jnp.concatenate(
            [q[:, h * HD : (h + 1) * HD] for h in range(heads)], axis=0
        )
        return 0

    lax.fori_loop(0, kv_heads * PARTS, place_queries, 0)

    def store(g, part, row_max, acc):
        max_ref[at(g, part), :] = row_max
        acc_ref[at(g, part), :] = acc

    def work(blocks, allowed):
        def of(i, g):
            return jnp.concatenate([kv_ref[block, i, :, block_of(g, HD)] for block in blocks], axis=0)

        pipeline(
            kv_heads,
            ahead_ref.at[:, : len(blocks) * rows],
            allowed,
            lambda g, part: scores_for(queries_ref[at(g, part), :], of(0, g)),
            lambda g: of(1, g),
            lambda g, part: (None, None),
            store,
        )

    pl.when(half == side)(lambda: work([side], diagonal))
    pl.when(half != side)(lambda: work([1 - side, side], jnp.concatenate([earlier, diagonal], axis=1)))


def span_steps(place_ref, lengths_ref, kv_ref, queries_ref, ahead_ref, number, side, load, store):
    rows = kv_ref.shape[2]
    kv_heads = kv_ref.shape[3] // HD
    first = place_ref[side]
    key_starts = place_ref[3 + 2 * number], place_ref[4 + 2 * number]
    lo_first, lo_last = doc_starts(lengths_ref, first, first + rows - 1)
    needed = jnp.maximum(key_starts[0], key_starts[1]) + rows > lo_first
    whole = jnp.minimum(key_starts[0], key_starts[1]) >= lo_last

    def at(g, part):
        return block_of((side * kv_heads + g) * PARTS + part, ahead_ref.shape[0])

    def of(i, g):
        return jnp.concatenate([kv_ref[block, i, :, block_of(g, HD)] for block in range(2)], axis=0)

    def work(masked):
        allowed = None
        if masked:
            lows = doc_start_rows(lengths_ref, first, rows)
            allowed = jnp.concatenate([positions(start, rows) >= lows for start in key_starts], axis=1)
        pipeline(
            kv_heads,
            ahead_ref,
            allowed,
            lambda g, part: scores_for(queries_ref[at(g, part), :], of(0, g)),
            lambda g: of(1, g),
            lambda g, part: load(at(g, part)),
            lambda g, part, row_max, acc: store(g, part, at(g, part), row_max, acc),
        )

    pl.when(whole)(lambda: work(False))
    pl.when(needed & jnp.logical_not(whole))(lambda: work(True))
    return needed


def span_kernel(place_ref, lengths_ref, *refs, numbers):
    kv_refs, (queries_ref, _, _, max_ref, acc_ref, ahead_ref) = refs[: len(numbers)], refs[len(numbers) :]

    def load(at):
        return max_ref[at, :], acc_ref[at, :]

    def store(g, part, at, row_max, acc):
        max_ref[at, :] = row_max
        acc_ref[at, :] = acc

    for number, kv_ref in zip(numbers, kv_refs):

        def one_side(side, _):
            span_steps(place_ref, lengths_ref, kv_ref, queries_ref, ahead_ref, number, side, load, store)
            return 0

        lax.fori_loop(0, 2, one_side, 0)


def last_kernel(place_ref, lengths_ref, kv_ref, queries_ref, max_ref, acc_ref, out_ref, ahead_ref, *refs, number, side):
    rows = kv_ref.shape[2]
    kv_heads = kv_ref.shape[3] // HD
    chunk = ahead_ref.shape[0]
    heads = chunk // rows
    out = out_ref
    if refs:
        out, sems = refs

    def load(at):
        return max_ref[at, :], acc_ref[at, :]

    def copy_out(piece):
        whole = place_ref[2] * (kv_heads * PARTS) + piece
        return pltpu.make_async_copy(
            out.at[:, block_of(piece, heads * HD)], out_ref.at[:, block_of(whole, heads * HD)], sems.at[piece]
        )

    def finish(g, part, at, row_max, acc):
        finished = (acc[:, :HD] * (1.0 / acc[:, HD:])).astype(out.dtype)
        out[:, block_of(g * PARTS + part, heads * HD)] = jnp.concatenate(
            [finished[h * rows : (h + 1) * rows] for h in range(heads)], axis=1
        )
        if refs:
            copy_out(g * PARTS + part).start()

    needed = span_steps(place_ref, lengths_ref, kv_ref, queries_ref, ahead_ref, number, side, load, finish)

    @pl.when(jnp.logical_not(needed))
    def _():
        def one_head(g, _):
            for part in range(PARTS):
                finish(g, part, None, *load(block_of((side * kv_heads + g) * PARTS + part, chunk)))
            return 0

        lax.fori_loop(0, kv_heads, one_head, 0)

    if refs:
        for piece in range(kv_heads * PARTS):
            copy_out(piece).wait()


def join_kernel(place_ref, far_ref, out_in, out_ref, sems):
    del out_in
    pieces = sems.shape[0]
    rows = far_ref.shape[0] // pieces
    columns = block_of(1 - place_ref[2], far_ref.shape[1])
    copies = [
        pltpu.make_async_copy(
            far_ref.at[pl.ds(i * rows, rows), :], out_ref.at[pl.ds(i * rows, rows), columns], sems.at[i]
        )
        for i in range(pieces)
    ]
    for copy in copies:
        copy.start()
    for copy in copies:
        copy.wait()


def per_device(queries, keys, values, doc_lengths):
    rows, all_heads = queries.shape
    half_heads = all_heads // 2
    head_rows = (all_heads // HD) * rows
    half, span = lax.axis_index("head"), lax.axis_index("ctx")
    cores = lax.axis_size("head")
    place_in_group = lax.rem(span, REACH)

    nowhere = -2 * REACH

    def origin(kind):
        if kind == SHIFT:
            return span - REACH
        late = place_in_group >= REACH // 2
        from_place = place_in_group ^ (OPPOSITE if kind == SHIFT_OPPOSITE else kind)
        here = span - place_in_group + from_place
        if kind == SHIFT_OPPOSITE:
            return jnp.where(late, nowhere, here - REACH)
        if kind == OPPOSITE:
            return jnp.where(late, here, nowhere)
        return here - jnp.where(from_place > place_in_group, REACH, 0)

    parts = [(span * cores + half) * rows, (span * cores + 1 - half) * rows, half]
    for kinds in ROUNDS:
        start = jnp.where(half == 0, origin(kinds[0]), origin(kinds[1]))
        parts += [(start * cores + half) * rows, (start * cores + 1 - half) * rows]
    place = jnp.stack(parts).astype(jnp.int32)

    vmem = pl.BlockSpec(memory_space=pltpu.VMEM)
    smem = pl.BlockSpec(memory_space=pltpu.SMEM)
    anywhere = pl.BlockSpec(memory_space=pl.ANY)
    hbm = pl.BlockSpec(memory_space=pltpu.MemorySpace.HBM)
    placed_shape = jax.ShapeDtypeStruct((head_rows, HD), queries.dtype)
    max_shape = jax.ShapeDtypeStruct((head_rows, HD), jnp.float32)
    acc_shape = jax.ShapeDtypeStruct((head_rows, 2 * HD), jnp.float32)
    side_shape = jax.ShapeDtypeStruct((rows, half_heads), queries.dtype)
    common = dict(
        compiler_params=pltpu.CompilerParams(vmem_limit_bytes=24 * 1024 * 1024),
        cost_estimate=pl.CostEstimate(flops=0, bytes_accessed=0, transcendentals=0),
    )

    def heads_of(array, core):
        width = array.shape[1] // 2
        return lax.dynamic_slice_in_dim(array, core * width, width, 1)

    to_give = jnp.stack([heads_of(keys, 1 - half), heads_of(values, 1 - half)])
    given = to_other_core(to_give)
    given, queries = lax.optimization_barrier((given, queries))
    own = jnp.stack([jnp.stack([heads_of(keys, half), heads_of(values, half)]), given])
    arrived = [send_round(own, kinds) for kinds in ROUNDS[:2]]
    q_far = to_other_core(
        pl.pallas_call(
            pick_kernel,
            in_specs=[smem, hbm],
            out_specs=vmem,
            out_shape=side_shape,
            scratch_shapes=[pltpu.SemaphoreType.DMA],
            name="pick_queries",
            **common,
        )(place, queries)
    )

    chunk_heads = queries.shape[1] // keys.shape[1] // PARTS
    ahead = pltpu.VMEM((chunk_heads * rows, 2 * rows), jnp.float32)
    state_shapes = (placed_shape, max_shape, acc_shape)
    state = pl.pallas_call(
        functools.partial(own_kernel, side=0),
        in_specs=[smem, smem, hbm, vmem],
        out_specs=(vmem, vmem, vmem),
        out_shape=state_shapes,
        scratch_shapes=[ahead, pltpu.VMEM((rows, half_heads), queries.dtype), pltpu.SemaphoreType.DMA],
        name="attend_own_near",
        **{**common, "cost_estimate": pl.CostEstimate(flops=10**11, bytes_accessed=0, transcendentals=0)},
    )(place, doc_lengths, queries, own)
    placed, row_max, acc = pl.pallas_call(
        functools.partial(own_kernel, side=1),
        in_specs=[smem, smem] + [vmem] * 5,
        out_specs=(vmem, vmem, vmem),
        out_shape=state_shapes,
        input_output_aliases={4: 0, 5: 1, 6: 2},
        scratch_shapes=[ahead],
        name="attend_own_far",
        **common,
    )(place, doc_lengths, q_far, own, *state)

    def attend(kv, row_max, acc, number):
        return pl.pallas_call(
            functools.partial(span_kernel, numbers=tuple(range(number, number + len(kv)))),
            in_specs=[smem, smem] + [vmem] * (len(kv) + 3),
            out_specs=(vmem, vmem),
            out_shape=(max_shape, acc_shape),
            input_output_aliases={len(kv) + 3: 0, len(kv) + 4: 1},
            scratch_shapes=[ahead],
            name="attend_spans",
            **common,
        )(place, doc_lengths, *kv, placed, row_max, acc)

    behind, acc = lax.optimization_barrier((arrived[0], acc))
    opposite, acc = lax.optimization_barrier((arrived[1], acc))

    def plane_round(number):
        sends = [jnp.where((place_in_group ^ kind) > place_in_group, own, behind) for kind in ROUNDS[number]]
        return jnp.where(half == 0, *sends)

    first = send_round(plane_round(2), ROUNDS[2])
    relayed = send_round(opposite, ROUNDS[3])
    row_max, acc = attend([behind, opposite], row_max, acc, 0)
    to_second, acc = lax.optimization_barrier((plane_round(4), acc))
    second = send_round(to_second, ROUNDS[4])
    row_max, acc = attend([first], row_max, acc, 2)
    row_max, acc = attend([relayed], row_max, acc, 3)

    last_args = (place, doc_lengths, second, placed, row_max, acc)
    out_far = pl.pallas_call(
        functools.partial(last_kernel, number=4, side=1),
        in_specs=[smem, smem] + [vmem] * 4,
        out_specs=vmem,
        out_shape=side_shape,
        scratch_shapes=[ahead],
        name="attend_last_far",
        **common,
    )(*last_args)
    out = pl.pallas_call(
        functools.partial(last_kernel, number=4, side=0),
        in_specs=[smem, smem] + [vmem] * 4,
        out_specs=anywhere,
        out_shape=jax.ShapeDtypeStruct(queries.shape, queries.dtype),
        scratch_shapes=[
            ahead,
            pltpu.VMEM((rows, half_heads), queries.dtype),
            pltpu.SemaphoreType.DMA((half_heads // (chunk_heads * HD),)),
        ],
        name="attend_last_near",
        **common,
    )(*last_args)
    return pl.pallas_call(
        join_kernel,
        in_specs=[smem, vmem, anywhere],
        out_specs=anywhere,
        out_shape=jax.ShapeDtypeStruct(queries.shape, queries.dtype),
        input_output_aliases={2: 0},
        scratch_shapes=[pltpu.SemaphoreType.DMA((rows // 16,))],
        name="join_heads",
        **common,
    )(place, to_other_core(out_far), out)


def solution(mesh):
    placed = P(AXES, None)
    return jax.shard_map(
        per_device, mesh=mesh, in_specs=(placed, placed, placed, P()), out_specs=placed, check_vma=False
    )
```

```python
import functools
import math

import jax
import jax.numpy as jnp
from jax import lax
from jax.experimental import pallas as pl
from jax.experimental.pallas import tpu as pltpu
from jax.sharding import PartitionSpec as P

HD = 128
REACH = 4
NEVER = -1e30
SCORE_SCALE = HD ** (-0.5) * math.log2(math.e)
PARTS = 2
AXES = ("ctx", "head")
SHIFT, SHIFT_OPPOSITE, OPPOSITE = "shift", "shift opposite", REACH - 1
ROUNDS = ((SHIFT, SHIFT), (OPPOSITE, OPPOSITE), (1, 2), (SHIFT_OPPOSITE, SHIFT_OPPOSITE), (2, 1))


def send_round(block, kinds):
    spans, cores = lax.axis_size("ctx"), lax.axis_size("head")
    pairs = []
    for s in range(spans):
        for core, kind in enumerate(kinds):
            if kind in (SHIFT, SHIFT_OPPOSITE):
                target = s + REACH
                if target >= spans or (kind == SHIFT_OPPOSITE and s % REACH >= REACH // 2):
                    continue
            else:
                target = s ^ kind
            pairs.append((s * cores + core, target * cores + core))
    return lax.ppermute(block, AXES, pairs)


def to_other_core(block):
    cores = lax.axis_size("head")
    return lax.ppermute(block, "head", [(h, cores - 1 - h) for h in range(cores)])


def doc_starts(lengths_ref, first, last):
    def one_doc(i, carry):
        start, lo_first, lo_last = carry
        start = start + lengths_ref[i]
        return start, jnp.where(start <= first, start, lo_first), jnp.where(start <= last, start, lo_last)

    zero = jnp.int32(0)
    _, lo_first, lo_last = lax.fori_loop(0, lengths_ref.shape[0], one_doc, (zero, zero, zero))
    return lo_first, lo_last


def doc_start_rows(lengths_ref, first_query, rows):
    pos = first_query + lax.broadcasted_iota(jnp.int32, (rows, rows), 0)

    def one_doc(i, carry):
        start, lo = carry
        start = start + lengths_ref[i]
        return start, jnp.where(start <= pos, start, lo)

    zero = jnp.zeros((rows, rows), jnp.int32)
    return lax.fori_loop(0, lengths_ref.shape[0], one_doc, (jnp.int32(0), zero))[1]


def block_of(at, size):
    return pl.ds(pl.multiple_of(at * size, size), size)


def positions(start, rows):
    return start + lax.broadcasted_iota(jnp.int32, (rows, rows), 1)


def softmax_step(scores, allowed, max_before):
    if allowed is not None:
        allowed = jnp.concatenate([allowed] * (scores.shape[0] // allowed.shape[0]), axis=0)
        scores = jnp.where(allowed, scores, NEVER)
    row_max = jnp.broadcast_to(jnp.max(scores, axis=1, keepdims=True), (scores.shape[0], HD))
    rescale = None
    if max_before is not None:
        row_max = jnp.maximum(max_before, row_max)
        rescale = jnp.exp2((max_before - row_max) * SCORE_SCALE)
    shift = jnp.concatenate([row_max] * (scores.shape[1] // HD), axis=1)
    return jnp.exp2((scores - shift) * SCORE_SCALE).astype(jnp.bfloat16), row_max, rescale


def scores_for(queries, keys):
    return lax.dot_general(queries, keys, (((1,), (1,)), ((), ())), preferred_element_type=jnp.float32)


def pipeline(kv_heads, ahead_ref, allowed, scores_of, values_of, before_of, store):
    def finish(g, part, scores):
        max_before, acc_before = before_of(g, part)
        weights, row_max, rescale = softmax_step(scores, allowed, max_before)
        values = values_of(g)
        widened = jnp.concatenate([values, jnp.ones_like(values)], axis=1)
        acc = jnp.dot(weights, widened, preferred_element_type=jnp.float32)
        if rescale is not None:
            acc = acc_before * jnp.concatenate([rescale] * 2, axis=1) + acc
        store(g, part, row_max, acc)

    ahead_ref[...] = scores_of(0, 0)

    def one_head(g, _):
        scores = ahead_ref[...]
        for part in range(PARTS):
            if part + 1 < PARTS:
                later = scores_of(g, part + 1)
            else:
                later = scores_of(jnp.minimum(g + 1, kv_heads - 1), 0)
            finish(g, part, scores)
            scores = later
        ahead_ref[...] = scores
        return 0

    lax.fori_loop(0, kv_heads, one_head, 0)


def pick_kernel(place_ref, q_ref, out_ref, sem):
    copy = pltpu.make_async_copy(q_ref.at[:, block_of(1 - place_ref[2], out_ref.shape[1])], out_ref, sem)
    copy.start()
    copy.wait()


def own_kernel(place_ref, lengths_ref, q_ref, kv_ref, *refs, side):
    if side == 0:
        queries_ref, max_ref, acc_ref, lows_ref, bounds_ref, ahead_ref, q_side_ref, sem = refs
        fetch = pltpu.make_async_copy(q_ref.at[:, block_of(place_ref[2], q_side_ref.shape[1])], q_side_ref, sem)
        fetch.start()
    else:
        _, _, _, lows_ref, queries_ref, max_ref, acc_ref, ahead_ref = refs
        q_side_ref = q_ref
    rows, wide = q_side_ref.shape
    kv_heads = kv_ref.shape[3] // HD
    heads = wide // (kv_heads * PARTS * HD)
    half = place_ref[2]
    first, other = place_ref[side], place_ref[1 - side]
    query_pos = first + lax.broadcasted_iota(jnp.int32, (rows, rows), 0)
    if side == 0:
        for i in range(2):
            lows_ref[i] = doc_start_rows(lengths_ref, place_ref[i], rows)
            bounds_ref[2 * i], bounds_ref[2 * i + 1] = doc_starts(lengths_ref, place_ref[i], place_ref[i] + rows - 1)
    lows = lows_ref[side]
    key_pos = positions(first, rows)
    diagonal = (key_pos >= lows) & (key_pos <= query_pos)
    earlier = positions(other, rows) >= lows
    if side == 0:
        fetch.wait()

    def at(g, part):
        return block_of((side * kv_heads + g) * PARTS + part, heads * rows)

    def place_queries(i, _):
        q = q_side_ref[:, block_of(i, heads * HD)]
        queries_ref[block_of(side * kv_heads * PARTS + i, heads * rows), :] = jnp.concatenate(
            [q[:, h * HD : (h + 1) * HD] for h in range(heads)], axis=0
        )
        return 0

    lax.fori_loop(0, kv_heads * PARTS, place_queries, 0)

    def store(g, part, row_max, acc):
        max_ref[at(g, part), :] = row_max
        acc_ref[at(g, part), :] = acc

    def work(blocks, allowed):
        def of(i, g):
            return jnp.concatenate([kv_ref[block, i, :, block_of(g, HD)] for block in blocks], axis=0)

        pipeline(
            kv_heads,
            ahead_ref.at[:, : len(blocks) * rows],
            allowed,
            lambda g, part: scores_for(queries_ref[at(g, part), :], of(0, g)),
            lambda g: of(1, g),
            lambda g, part: (None, None),
            store,
        )

    pl.when(half == side)(lambda: work([side], diagonal))
    pl.when(half != side)(lambda: work([1 - side, side], jnp.concatenate([earlier, diagonal], axis=1)))


def span_steps(place_ref, bounds_ref, lows_ref, kv_ref, queries_ref, ahead_ref, number, side, load, store):
    rows = kv_ref.shape[2]
    kv_heads = kv_ref.shape[3] // HD
    key_starts = place_ref[3 + 2 * number], place_ref[4 + 2 * number]
    lo_first, lo_last = bounds_ref[2 * side], bounds_ref[2 * side + 1]
    needed = jnp.maximum(key_starts[0], key_starts[1]) + rows > lo_first
    whole = jnp.minimum(key_starts[0], key_starts[1]) >= lo_last

    def at(g, part):
        return block_of((side * kv_heads + g) * PARTS + part, ahead_ref.shape[0])

    def of(i, g):
        return jnp.concatenate([kv_ref[block, i, :, block_of(g, HD)] for block in range(2)], axis=0)

    def work(masked):
        allowed = None
        if masked:
            lows = lows_ref[side]
            allowed = jnp.concatenate([positions(start, rows) >= lows for start in key_starts], axis=1)
        pipeline(
            kv_heads,
            ahead_ref,
            allowed,
            lambda g, part: scores_for(queries_ref[at(g, part), :], of(0, g)),
            lambda g: of(1, g),
            lambda g, part: load(at(g, part)),
            lambda g, part, row_max, acc: store(g, part, at(g, part), row_max, acc),
        )

    pl.when(whole)(lambda: work(False))
    pl.when(needed & jnp.logical_not(whole))(lambda: work(True))
    return needed


def span_kernel(place_ref, bounds_ref, lows_ref, *refs, numbers):
    kv_refs, (queries_ref, _, _, max_ref, acc_ref, ahead_ref) = refs[: len(numbers)], refs[len(numbers) :]

    def load(at):
        return max_ref[at, :], acc_ref[at, :]

    def store(g, part, at, row_max, acc):
        max_ref[at, :] = row_max
        acc_ref[at, :] = acc

    for number, kv_ref in zip(numbers, kv_refs):

        def one_side(side, _):
            span_steps(place_ref, bounds_ref, lows_ref, kv_ref, queries_ref, ahead_ref, number, side, load, store)
            return 0

        lax.fori_loop(0, 2, one_side, 0)


def last_kernel(
    place_ref, bounds_ref, lows_ref, kv_ref, queries_ref, max_ref, acc_ref, out_ref, ahead_ref, *refs, number, side
):
    rows = kv_ref.shape[2]
    kv_heads = kv_ref.shape[3] // HD
    chunk = ahead_ref.shape[0]
    heads = chunk // rows
    out = out_ref
    if refs:
        out, sems = refs

    def load(at):
        return max_ref[at, :], acc_ref[at, :]

    def copy_out(piece):
        whole = place_ref[2] * (kv_heads * PARTS) + piece
        return pltpu.make_async_copy(
            out.at[:, block_of(piece, heads * HD)], out_ref.at[:, block_of(whole, heads * HD)], sems.at[piece]
        )

    def finish(g, part, at, row_max, acc):
        finished = (acc[:, :HD] * (1.0 / acc[:, HD:])).astype(out.dtype)
        out[:, block_of(g * PARTS + part, heads * HD)] = jnp.concatenate(
            [finished[h * rows : (h + 1) * rows] for h in range(heads)], axis=1
        )
        if refs:
            copy_out(g * PARTS + part).start()

    needed = span_steps(place_ref, bounds_ref, lows_ref, kv_ref, queries_ref, ahead_ref, number, side, load, finish)

    @pl.when(jnp.logical_not(needed))
    def _():
        def one_head(g, _):
            for part in range(PARTS):
                finish(g, part, None, *load(block_of((side * kv_heads + g) * PARTS + part, chunk)))
            return 0

        lax.fori_loop(0, kv_heads, one_head, 0)

    if refs:
        for piece in range(kv_heads * PARTS):
            copy_out(piece).wait()


def join_kernel(place_ref, far_ref, out_in, out_ref, sems):
    del out_in
    pieces = sems.shape[0]
    rows = far_ref.shape[0] // pieces
    columns = block_of(1 - place_ref[2], far_ref.shape[1])
    copies = [
        pltpu.make_async_copy(
            far_ref.at[pl.ds(i * rows, rows), :], out_ref.at[pl.ds(i * rows, rows), columns], sems.at[i]
        )
        for i in range(pieces)
    ]
    for copy in copies:
        copy.start()
    for copy in copies:
        copy.wait()


def per_device(queries, keys, values, doc_lengths):
    rows, all_heads = queries.shape
    half_heads = all_heads // 2
    head_rows = (all_heads // HD) * rows
    half, span = lax.axis_index("head"), lax.axis_index("ctx")
    cores = lax.axis_size("head")
    place_in_group = lax.rem(span, REACH)

    nowhere = -2 * REACH

    def origin(kind):
        if kind == SHIFT:
            return span - REACH
        late = place_in_group >= REACH // 2
        from_place = place_in_group ^ (OPPOSITE if kind == SHIFT_OPPOSITE else kind)
        here = span - place_in_group + from_place
        if kind == SHIFT_OPPOSITE:
            return jnp.where(late, nowhere, here - REACH)
        if kind == OPPOSITE:
            return jnp.where(late, here, nowhere)
        return here - jnp.where(from_place > place_in_group, REACH, 0)

    parts = [(span * cores + half) * rows, (span * cores + 1 - half) * rows, half]
    for kinds in ROUNDS:
        start = jnp.where(half == 0, origin(kinds[0]), origin(kinds[1]))
        parts += [(start * cores + half) * rows, (start * cores + 1 - half) * rows]
    place = jnp.stack(parts).astype(jnp.int32)

    vmem = pl.BlockSpec(memory_space=pltpu.VMEM)
    smem = pl.BlockSpec(memory_space=pltpu.SMEM)
    anywhere = pl.BlockSpec(memory_space=pl.ANY)
    hbm = pl.BlockSpec(memory_space=pltpu.MemorySpace.HBM)
    placed_shape = jax.ShapeDtypeStruct((head_rows, HD), queries.dtype)
    max_shape = jax.ShapeDtypeStruct((head_rows, HD), jnp.float32)
    acc_shape = jax.ShapeDtypeStruct((head_rows, 2 * HD), jnp.float32)
    side_shape = jax.ShapeDtypeStruct((rows, half_heads), queries.dtype)
    common = dict(
        compiler_params=pltpu.CompilerParams(vmem_limit_bytes=24 * 1024 * 1024),
        cost_estimate=pl.CostEstimate(flops=0, bytes_accessed=0, transcendentals=0),
    )

    def heads_of(array, core):
        width = array.shape[1] // 2
        return lax.dynamic_slice_in_dim(array, core * width, width, 1)

    to_give = jnp.stack([heads_of(keys, 1 - half), heads_of(values, 1 - half)])
    given = to_other_core(to_give)
    given, queries = lax.optimization_barrier((given, queries))
    own = jnp.stack([jnp.stack([heads_of(keys, half), heads_of(values, half)]), given])
    arrived = [send_round(own, kinds) for kinds in ROUNDS[:2]]
    q_far = to_other_core(
        pl.pallas_call(
            pick_kernel,
            in_specs=[smem, hbm],
            out_specs=vmem,
            out_shape=side_shape,
            scratch_shapes=[pltpu.SemaphoreType.DMA],
            name="pick_queries",
            **common,
        )(place, queries)
    )

    chunk_heads = queries.shape[1] // keys.shape[1] // PARTS
    ahead = pltpu.VMEM((chunk_heads * rows, 2 * rows), jnp.float32)
    state_shapes = (placed_shape, max_shape, acc_shape)
    lows_shape = jax.ShapeDtypeStruct((2, rows, rows), jnp.int32)
    bounds_shape = jax.ShapeDtypeStruct((4,), jnp.int32)
    *state, lows, bounds = pl.pallas_call(
        functools.partial(own_kernel, side=0),
        in_specs=[smem, smem, hbm, vmem],
        out_specs=(vmem, vmem, vmem, vmem, smem),
        out_shape=state_shapes + (lows_shape, bounds_shape),
        scratch_shapes=[ahead, pltpu.VMEM((rows, half_heads), queries.dtype), pltpu.SemaphoreType.DMA],
        name="attend_own_near",
        **{**common, "cost_estimate": pl.CostEstimate(flops=10**11, bytes_accessed=0, transcendentals=0)},
    )(place, doc_lengths, queries, own)
    placed, row_max, acc = pl.pallas_call(
        functools.partial(own_kernel, side=1),
        in_specs=[smem, smem] + [vmem] * 6,
        out_specs=(vmem, vmem, vmem),
        out_shape=state_shapes,
        input_output_aliases={4: 0, 5: 1, 6: 2},
        scratch_shapes=[ahead],
        name="attend_own_far",
        **common,
    )(place, doc_lengths, q_far, own, *state, lows)

    def attend(kv, row_max, acc, number):
        return pl.pallas_call(
            functools.partial(span_kernel, numbers=tuple(range(number, number + len(kv)))),
            in_specs=[smem, smem] + [vmem] * (len(kv) + 4),
            out_specs=(vmem, vmem),
            out_shape=(max_shape, acc_shape),
            input_output_aliases={len(kv) + 4: 0, len(kv) + 5: 1},
            scratch_shapes=[ahead],
            name="attend_spans",
            **common,
        )(place, bounds, lows, *kv, placed, row_max, acc)

    behind, acc = lax.optimization_barrier((arrived[0], acc))
    opposite, acc = lax.optimization_barrier((arrived[1], acc))

    def plane_round(number):
        sends = [jnp.where((place_in_group ^ kind) > place_in_group, own, behind) for kind in ROUNDS[number]]
        return jnp.where(half == 0, *sends)

    first = send_round(plane_round(2), ROUNDS[2])
    relayed = send_round(opposite, ROUNDS[3])
    row_max, acc = attend([behind, opposite], row_max, acc, 0)
    to_second, first, acc = lax.optimization_barrier((plane_round(4), first, acc))
    second = send_round(to_second, ROUNDS[4])
    row_max, acc = attend([first], row_max, acc, 2)
    row_max, acc = attend([relayed], row_max, acc, 3)

    last_args = (place, bounds, lows, second, placed, row_max, acc)
    out_far = pl.pallas_call(
        functools.partial(last_kernel, number=4, side=1),
        in_specs=[smem, smem] + [vmem] * 5,
        out_specs=vmem,
        out_shape=side_shape,
        scratch_shapes=[ahead],
        name="attend_last_far",
        **common,
    )(*last_args)
    out = pl.pallas_call(
        functools.partial(last_kernel, number=4, side=0),
        in_specs=[smem, smem] + [vmem] * 5,
        out_specs=anywhere,
        out_shape=jax.ShapeDtypeStruct(queries.shape, queries.dtype),
        scratch_shapes=[
            ahead,
            pltpu.VMEM((rows, half_heads), queries.dtype),
            pltpu.SemaphoreType.DMA((half_heads // (chunk_heads * HD),)),
        ],
        name="attend_last_near",
        **common,
    )(*last_args)
    return pl.pallas_call(
        join_kernel,
        in_specs=[smem, vmem, anywhere],
        out_specs=anywhere,
        out_shape=jax.ShapeDtypeStruct(queries.shape, queries.dtype),
        input_output_aliases={2: 0},
        scratch_shapes=[pltpu.SemaphoreType.DMA((rows // 16,))],
        name="join_heads",
        **common,
    )(place, to_other_core(out_far), out)


def solution(mesh):
    placed = P(AXES, None)
    return jax.shard_map(
        per_device, mesh=mesh, in_specs=(placed, placed, placed, P()), out_specs=placed, check_vma=False
    )
```

```python
import functools
import math

import jax
import jax.numpy as jnp
from jax import lax
from jax.experimental import pallas as pl
from jax.experimental.pallas import tpu as pltpu
from jax.sharding import PartitionSpec as P

HD = 128
REACH = 4
NEVER = -1e30
SCORE_SCALE = HD ** (-0.5) * math.log2(math.e)
PARTS = 1
AXES = ("ctx", "head")
SHIFT, SHIFT_OPPOSITE, OPPOSITE = "shift", "shift opposite", REACH - 1
ROUNDS = ((SHIFT, SHIFT), (OPPOSITE, OPPOSITE), (1, 2), (SHIFT_OPPOSITE, SHIFT_OPPOSITE), (2, 1))


def send_round(block, kinds):
    spans, cores = lax.axis_size("ctx"), lax.axis_size("head")
    pairs = []
    for s in range(spans):
        for core, kind in enumerate(kinds):
            if kind in (SHIFT, SHIFT_OPPOSITE):
                target = s + REACH
                if target >= spans or (kind == SHIFT_OPPOSITE and s % REACH >= REACH // 2):
                    continue
            else:
                target = s ^ kind
            pairs.append((s * cores + core, target * cores + core))
    return lax.ppermute(block, AXES, pairs)


def to_other_core(block):
    cores = lax.axis_size("head")
    return lax.ppermute(block, "head", [(h, cores - 1 - h) for h in range(cores)])


def doc_starts(lengths_ref, first, last):
    def one_doc(i, carry):
        start, lo_first, lo_last = carry
        start = start + lengths_ref[i]
        return start, jnp.where(start <= first, start, lo_first), jnp.where(start <= last, start, lo_last)

    zero = jnp.int32(0)
    _, lo_first, lo_last = lax.fori_loop(0, lengths_ref.shape[0], one_doc, (zero, zero, zero))
    return lo_first, lo_last


def doc_start_rows(lengths_ref, first_query, rows):
    pos = first_query + lax.broadcasted_iota(jnp.int32, (rows, rows), 0)

    def one_doc(i, carry):
        start, lo = carry
        start = start + lengths_ref[i]
        return start, jnp.where(start <= pos, start, lo)

    zero = jnp.zeros((rows, rows), jnp.int32)
    return lax.fori_loop(0, lengths_ref.shape[0], one_doc, (jnp.int32(0), zero))[1]


def block_of(at, size):
    return pl.ds(pl.multiple_of(at * size, size), size)


def positions(start, rows):
    return start + lax.broadcasted_iota(jnp.int32, (rows, rows), 1)


def softmax_step(scores, allowed, max_before):
    if allowed is not None:
        allowed = jnp.concatenate([allowed] * (scores.shape[0] // allowed.shape[0]), axis=0)
        scores = jnp.where(allowed, scores, NEVER)
    row_max = jnp.broadcast_to(jnp.max(scores, axis=1, keepdims=True), (scores.shape[0], HD))
    rescale = None
    if max_before is not None:
        row_max = jnp.maximum(max_before, row_max)
        rescale = jnp.exp2((max_before - row_max) * SCORE_SCALE)
    shift = jnp.concatenate([row_max] * (scores.shape[1] // HD), axis=1)
    return jnp.exp2((scores - shift) * SCORE_SCALE).astype(jnp.bfloat16), row_max, rescale


def scores_for(queries, keys):
    return lax.dot_general(queries, keys, (((1,), (1,)), ((), ())), preferred_element_type=jnp.float32)


def pipeline(kv_heads, ahead_ref, allowed, scores_of, values_of, before_of, store):
    def finish(g, part, scores):
        max_before, acc_before = before_of(g, part)
        weights, row_max, rescale = softmax_step(scores, allowed, max_before)
        values = values_of(g)
        widened = jnp.concatenate([values, jnp.ones_like(values)], axis=1)
        acc = jnp.dot(weights, widened, preferred_element_type=jnp.float32)
        if rescale is not None:
            acc = acc_before * jnp.concatenate([rescale] * 2, axis=1) + acc
        store(g, part, row_max, acc)

    ahead_ref[...] = scores_of(0, 0)

    def one_head(g, _):
        scores = ahead_ref[...]
        for part in range(PARTS):
            if part + 1 < PARTS:
                later = scores_of(g, part + 1)
            else:
                later = scores_of(jnp.minimum(g + 1, kv_heads - 1), 0)
            finish(g, part, scores)
            scores = later
        ahead_ref[...] = scores
        return 0

    lax.fori_loop(0, kv_heads, one_head, 0)


def pick_kernel(place_ref, q_ref, out_ref, sem):
    copy = pltpu.make_async_copy(q_ref.at[:, block_of(1 - place_ref[2], out_ref.shape[1])], out_ref, sem)
    copy.start()
    copy.wait()


def own_kernel(place_ref, lengths_ref, q_ref, kv_ref, *refs, side):
    if side == 0:
        queries_ref, max_ref, acc_ref, lows_ref, bounds_ref, ahead_ref, q_side_ref, sem = refs
        fetch = pltpu.make_async_copy(q_ref.at[:, block_of(place_ref[2], q_side_ref.shape[1])], q_side_ref, sem)
        fetch.start()
    else:
        _, _, _, lows_ref, queries_ref, max_ref, acc_ref, ahead_ref = refs
        q_side_ref = q_ref
    rows, wide = q_side_ref.shape
    kv_heads = kv_ref.shape[3] // HD
    heads = wide // (kv_heads * PARTS * HD)
    half = place_ref[2]
    first, other = place_ref[side], place_ref[1 - side]
    query_pos = first + lax.broadcasted_iota(jnp.int32, (rows, rows), 0)
    if side == 0:
        for i in range(2):
            lows_ref[i] = doc_start_rows(lengths_ref, place_ref[i], rows)
            bounds_ref[2 * i], bounds_ref[2 * i + 1] = doc_starts(lengths_ref, place_ref[i], place_ref[i] + rows - 1)
    lows = lows_ref[side]
    key_pos = positions(first, rows)
    diagonal = (key_pos >= lows) & (key_pos <= query_pos)
    earlier = positions(other, rows) >= lows
    if side == 0:
        fetch.wait()

    def at(g, part):
        return block_of((side * kv_heads + g) * PARTS + part, heads * rows)

    def place_queries(i, _):
        q = q_side_ref[:, block_of(i, heads * HD)]
        queries_ref[block_of(side * kv_heads * PARTS + i, heads * rows), :] = jnp.concatenate(
            [q[:, h * HD : (h + 1) * HD] for h in range(heads)], axis=0
        )
        return 0

    lax.fori_loop(0, kv_heads * PARTS, place_queries, 0)

    def store(g, part, row_max, acc):
        max_ref[at(g, part), :] = row_max
        acc_ref[at(g, part), :] = acc

    def work(blocks, allowed):
        def of(i, g):
            return jnp.concatenate([kv_ref[block, i, :, block_of(g, HD)] for block in blocks], axis=0)

        pipeline(
            kv_heads,
            ahead_ref.at[:, : len(blocks) * rows],
            allowed,
            lambda g, part: scores_for(queries_ref[at(g, part), :], of(0, g)),
            lambda g: of(1, g),
            lambda g, part: (None, None),
            store,
        )

    pl.when(half == side)(lambda: work([side], diagonal))
    pl.when(half != side)(lambda: work([1 - side, side], jnp.concatenate([earlier, diagonal], axis=1)))


def span_steps(place_ref, bounds_ref, lows_ref, kv_ref, queries_ref, ahead_ref, number, side, load, store):
    rows = kv_ref.shape[2]
    kv_heads = kv_ref.shape[3] // HD
    key_starts = place_ref[3 + 2 * number], place_ref[4 + 2 * number]
    lo_first, lo_last = bounds_ref[2 * side], bounds_ref[2 * side + 1]
    needed = jnp.maximum(key_starts[0], key_starts[1]) + rows > lo_first
    whole = jnp.minimum(key_starts[0], key_starts[1]) >= lo_last

    def at(g, part):
        return block_of((side * kv_heads + g) * PARTS + part, ahead_ref.shape[0])

    def of(i, g):
        return jnp.concatenate([kv_ref[block, i, :, block_of(g, HD)] for block in range(2)], axis=0)

    def work(masked):
        allowed = None
        if masked:
            lows = lows_ref[side]
            allowed = jnp.concatenate([positions(start, rows) >= lows for start in key_starts], axis=1)
        pipeline(
            kv_heads,
            ahead_ref,
            allowed,
            lambda g, part: scores_for(queries_ref[at(g, part), :], of(0, g)),
            lambda g: of(1, g),
            lambda g, part: load(at(g, part)),
            lambda g, part, row_max, acc: store(g, part, at(g, part), row_max, acc),
        )

    pl.when(whole)(lambda: work(False))
    pl.when(needed & jnp.logical_not(whole))(lambda: work(True))
    return needed


def span_kernel(place_ref, bounds_ref, lows_ref, *refs, numbers):
    kv_refs, (queries_ref, _, _, max_ref, acc_ref, ahead_ref) = refs[: len(numbers)], refs[len(numbers) :]

    def load(at):
        return max_ref[at, :], acc_ref[at, :]

    def store(g, part, at, row_max, acc):
        max_ref[at, :] = row_max
        acc_ref[at, :] = acc

    for number, kv_ref in zip(numbers, kv_refs):

        def one_side(side, _):
            span_steps(place_ref, bounds_ref, lows_ref, kv_ref, queries_ref, ahead_ref, number, side, load, store)
            return 0

        lax.fori_loop(0, 2, one_side, 0)


def last_kernel(
    place_ref, bounds_ref, lows_ref, kv_ref, queries_ref, max_ref, acc_ref, out_ref, ahead_ref, *refs, number, side
):
    rows = kv_ref.shape[2]
    kv_heads = kv_ref.shape[3] // HD
    chunk = ahead_ref.shape[0]
    heads = chunk // rows
    out = out_ref
    if refs:
        out, sems = refs

    def load(at):
        return max_ref[at, :], acc_ref[at, :]

    def copy_out(piece):
        whole = place_ref[2] * (kv_heads * PARTS) + piece
        return pltpu.make_async_copy(
            out.at[:, block_of(piece, heads * HD)], out_ref.at[:, block_of(whole, heads * HD)], sems.at[piece]
        )

    def finish(g, part, at, row_max, acc):
        finished = (acc[:, :HD] * (1.0 / acc[:, HD:])).astype(out.dtype)
        out[:, block_of(g * PARTS + part, heads * HD)] = jnp.concatenate(
            [finished[h * rows : (h + 1) * rows] for h in range(heads)], axis=1
        )
        if refs:
            copy_out(g * PARTS + part).start()

    needed = span_steps(place_ref, bounds_ref, lows_ref, kv_ref, queries_ref, ahead_ref, number, side, load, finish)

    @pl.when(jnp.logical_not(needed))
    def _():
        def one_head(g, _):
            for part in range(PARTS):
                finish(g, part, None, *load(block_of((side * kv_heads + g) * PARTS + part, chunk)))
            return 0

        lax.fori_loop(0, kv_heads, one_head, 0)

    if refs:
        for piece in range(kv_heads * PARTS):
            copy_out(piece).wait()


def join_kernel(place_ref, far_ref, out_in, out_ref, sems):
    del out_in
    pieces = sems.shape[0]
    rows = far_ref.shape[0] // pieces
    columns = block_of(1 - place_ref[2], far_ref.shape[1])
    copies = [
        pltpu.make_async_copy(
            far_ref.at[pl.ds(i * rows, rows), :], out_ref.at[pl.ds(i * rows, rows), columns], sems.at[i]
        )
        for i in range(pieces)
    ]
    for copy in copies:
        copy.start()
    for copy in copies:
        copy.wait()


def per_device(queries, keys, values, doc_lengths):
    rows, all_heads = queries.shape
    half_heads = all_heads // 2
    head_rows = (all_heads // HD) * rows
    half, span = lax.axis_index("head"), lax.axis_index("ctx")
    cores = lax.axis_size("head")
    place_in_group = lax.rem(span, REACH)

    nowhere = -2 * REACH

    def origin(kind):
        if kind == SHIFT:
            return span - REACH
        late = place_in_group >= REACH // 2
        from_place = place_in_group ^ (OPPOSITE if kind == SHIFT_OPPOSITE else kind)
        here = span - place_in_group + from_place
        if kind == SHIFT_OPPOSITE:
            return jnp.where(late, nowhere, here - REACH)
        if kind == OPPOSITE:
            return jnp.where(late, here, nowhere)
        return here - jnp.where(from_place > place_in_group, REACH, 0)

    parts = [(span * cores + half) * rows, (span * cores + 1 - half) * rows, half]
    for kinds in ROUNDS:
        start = jnp.where(half == 0, origin(kinds[0]), origin(kinds[1]))
        parts += [(start * cores + half) * rows, (start * cores + 1 - half) * rows]
    place = jnp.stack(parts).astype(jnp.int32)

    vmem = pl.BlockSpec(memory_space=pltpu.VMEM)
    smem = pl.BlockSpec(memory_space=pltpu.SMEM)
    anywhere = pl.BlockSpec(memory_space=pl.ANY)
    hbm = pl.BlockSpec(memory_space=pltpu.MemorySpace.HBM)
    placed_shape = jax.ShapeDtypeStruct((head_rows, HD), queries.dtype)
    max_shape = jax.ShapeDtypeStruct((head_rows, HD), jnp.float32)
    acc_shape = jax.ShapeDtypeStruct((head_rows, 2 * HD), jnp.float32)
    side_shape = jax.ShapeDtypeStruct((rows, half_heads), queries.dtype)
    common = dict(
        compiler_params=pltpu.CompilerParams(vmem_limit_bytes=24 * 1024 * 1024),
        cost_estimate=pl.CostEstimate(flops=0, bytes_accessed=0, transcendentals=0),
    )

    def heads_of(array, core):
        width = array.shape[1] // 2
        return lax.dynamic_slice_in_dim(array, core * width, width, 1)

    to_give = jnp.stack([heads_of(keys, 1 - half), heads_of(values, 1 - half)])
    given = to_other_core(to_give)
    given, queries = lax.optimization_barrier((given, queries))
    own = jnp.stack([jnp.stack([heads_of(keys, half), heads_of(values, half)]), given])
    arrived = [send_round(own, kinds) for kinds in ROUNDS[:2]]
    q_far = to_other_core(
        pl.pallas_call(
            pick_kernel,
            in_specs=[smem, hbm],
            out_specs=vmem,
            out_shape=side_shape,
            scratch_shapes=[pltpu.SemaphoreType.DMA],
            name="pick_queries",
            **common,
        )(place, queries)
    )

    chunk_heads = queries.shape[1] // keys.shape[1] // PARTS
    ahead = pltpu.VMEM((chunk_heads * rows, 2 * rows), jnp.float32)
    state_shapes = (placed_shape, max_shape, acc_shape)
    lows_shape = jax.ShapeDtypeStruct((2, rows, rows), jnp.int32)
    bounds_shape = jax.ShapeDtypeStruct((4,), jnp.int32)
    *state, lows, bounds = pl.pallas_call(
        functools.partial(own_kernel, side=0),
        in_specs=[smem, smem, hbm, vmem],
        out_specs=(vmem, vmem, vmem, vmem, smem),
        out_shape=state_shapes + (lows_shape, bounds_shape),
        scratch_shapes=[ahead, pltpu.VMEM((rows, half_heads), queries.dtype), pltpu.SemaphoreType.DMA],
        name="attend_own_near",
        **{**common, "cost_estimate": pl.CostEstimate(flops=10**11, bytes_accessed=0, transcendentals=0)},
    )(place, doc_lengths, queries, own)
    placed, row_max, acc = pl.pallas_call(
        functools.partial(own_kernel, side=1),
        in_specs=[smem, smem] + [vmem] * 6,
        out_specs=(vmem, vmem, vmem),
        out_shape=state_shapes,
        input_output_aliases={4: 0, 5: 1, 6: 2},
        scratch_shapes=[ahead],
        name="attend_own_far",
        **common,
    )(place, doc_lengths, q_far, own, *state, lows)

    def attend(kv, row_max, acc, number):
        return pl.pallas_call(
            functools.partial(span_kernel, numbers=tuple(range(number, number + len(kv)))),
            in_specs=[smem, smem] + [vmem] * (len(kv) + 4),
            out_specs=(vmem, vmem),
            out_shape=(max_shape, acc_shape),
            input_output_aliases={len(kv) + 4: 0, len(kv) + 5: 1},
            scratch_shapes=[ahead],
            name="attend_spans",
            **common,
        )(place, bounds, lows, *kv, placed, row_max, acc)

    behind, acc = lax.optimization_barrier((arrived[0], acc))
    opposite, acc = lax.optimization_barrier((arrived[1], acc))

    def plane_round(number):
        sends = [jnp.where((place_in_group ^ kind) > place_in_group, own, behind) for kind in ROUNDS[number]]
        return jnp.where(half == 0, *sends)

    first = send_round(plane_round(2), ROUNDS[2])
    relayed = send_round(opposite, ROUNDS[3])
    row_max, acc = attend([behind, opposite], row_max, acc, 0)
    to_second, first, acc = lax.optimization_barrier((plane_round(4), first, acc))
    second = send_round(to_second, ROUNDS[4])
    row_max, acc = attend([first], row_max, acc, 2)
    row_max, acc = attend([relayed], row_max, acc, 3)

    last_args = (place, bounds, lows, second, placed, row_max, acc)
    out_far = pl.pallas_call(
        functools.partial(last_kernel, number=4, side=1),
        in_specs=[smem, smem] + [vmem] * 5,
        out_specs=vmem,
        out_shape=side_shape,
        scratch_shapes=[ahead],
        name="attend_last_far",
        **common,
    )(*last_args)
    out = pl.pallas_call(
        functools.partial(last_kernel, number=4, side=0),
        in_specs=[smem, smem] + [vmem] * 5,
        out_specs=anywhere,
        out_shape=jax.ShapeDtypeStruct(queries.shape, queries.dtype),
        scratch_shapes=[
            ahead,
            pltpu.VMEM((rows, half_heads), queries.dtype),
            pltpu.SemaphoreType.DMA((half_heads // (chunk_heads * HD),)),
        ],
        name="attend_last_near",
        **common,
    )(*last_args)
    return pl.pallas_call(
        join_kernel,
        in_specs=[smem, vmem, anywhere],
        out_specs=anywhere,
        out_shape=jax.ShapeDtypeStruct(queries.shape, queries.dtype),
        input_output_aliases={2: 0},
        scratch_shapes=[pltpu.SemaphoreType.DMA((rows // 16,))],
        name="join_heads",
        **common,
    )(place, to_other_core(out_far), out)


def solution(mesh):
    placed = P(AXES, None)
    return jax.shard_map(
        per_device, mesh=mesh, in_specs=(placed, placed, placed, P()), out_specs=placed, check_vma=False
    )
```

```python
import functools
import math

import jax
import jax.numpy as jnp
from jax import lax
from jax.experimental import pallas as pl
from jax.experimental.pallas import tpu as pltpu
from jax.sharding import PartitionSpec as P

HD = 128
REACH = 4
NEVER = -1e30
SCORE_SCALE = HD ** (-0.5) * math.log2(math.e)
PARTS = 2
AXES = ("ctx", "head")
SHIFT, SHIFT_OPPOSITE, OPPOSITE = "shift", "shift opposite", REACH - 1
ROUNDS = ((SHIFT, SHIFT), (OPPOSITE, OPPOSITE), (1, 2), (SHIFT_OPPOSITE, SHIFT_OPPOSITE), (2, 1))


def send_round(block, kinds):
    spans, cores = lax.axis_size("ctx"), lax.axis_size("head")
    pairs = []
    for s in range(spans):
        for core, kind in enumerate(kinds):
            if kind in (SHIFT, SHIFT_OPPOSITE):
                target = s + REACH
                if target >= spans or (kind == SHIFT_OPPOSITE and s % REACH >= REACH // 2):
                    continue
            else:
                target = s ^ kind
            pairs.append((s * cores + core, target * cores + core))
    return lax.ppermute(block, AXES, pairs)


def to_other_core(block):
    cores = lax.axis_size("head")
    return lax.ppermute(block, "head", [(h, cores - 1 - h) for h in range(cores)])


def doc_starts(lengths_ref, first, last):
    def one_doc(i, carry):
        start, lo_first, lo_last = carry
        start = start + lengths_ref[i]
        return start, jnp.where(start <= first, start, lo_first), jnp.where(start <= last, start, lo_last)

    zero = jnp.int32(0)
    _, lo_first, lo_last = lax.fori_loop(0, lengths_ref.shape[0], one_doc, (zero, zero, zero))
    return lo_first, lo_last


def doc_start_rows(lengths_ref, first_query, rows):
    pos = first_query + lax.broadcasted_iota(jnp.int32, (rows, rows), 0)

    def one_doc(i, carry):
        start, lo = carry
        start = start + lengths_ref[i]
        return start, jnp.where(start <= pos, start, lo)

    zero = jnp.zeros((rows, rows), jnp.int32)
    return lax.fori_loop(0, lengths_ref.shape[0], one_doc, (jnp.int32(0), zero))[1]


def block_of(at, size):
    return pl.ds(pl.multiple_of(at * size, size), size)


def positions(start, rows):
    return start + lax.broadcasted_iota(jnp.int32, (rows, rows), 1)


def softmax_step(scores, allowed, max_before):
    if allowed is not None:
        allowed = jnp.concatenate([allowed] * (scores.shape[0] // allowed.shape[0]), axis=0)
        scores = jnp.where(allowed, scores, NEVER)
    row_max = jnp.broadcast_to(jnp.max(scores, axis=1, keepdims=True), (scores.shape[0], HD))
    rescale = None
    if max_before is not None:
        row_max = jnp.maximum(max_before, row_max)
        rescale = jnp.exp2((max_before - row_max) * SCORE_SCALE)
    shift = jnp.concatenate([row_max] * (scores.shape[1] // HD), axis=1)
    return jnp.exp2((scores - shift) * SCORE_SCALE).astype(jnp.bfloat16), row_max, rescale


def scores_for(queries, keys):
    return lax.dot_general(queries, keys, (((1,), (1,)), ((), ())), preferred_element_type=jnp.float32)


def pipeline(kv_heads, ahead_ref, allowed, scores_of, values_of, before_of, store):
    def finish(g, part, scores):
        max_before, acc_before = before_of(g, part)
        weights, row_max, rescale = softmax_step(scores, allowed, max_before)
        values = values_of(g)
        widened = jnp.concatenate([values, jnp.ones_like(values)], axis=1)
        acc = jnp.dot(weights, widened, preferred_element_type=jnp.float32)
        if rescale is not None:
            acc = acc_before * jnp.concatenate([rescale] * 2, axis=1) + acc
        store(g, part, row_max, acc)

    ahead_ref[...] = scores_of(0, 0)

    def one_head(g, _):
        scores = ahead_ref[...]
        for part in range(PARTS):
            if part + 1 < PARTS:
                later = scores_of(g, part + 1)
            else:
                later = scores_of(jnp.minimum(g + 1, kv_heads - 1), 0)
            finish(g, part, scores)
            scores = later
        ahead_ref[...] = scores
        return 0

    lax.fori_loop(0, kv_heads, one_head, 0)


def pick_kernel(place_ref, q_ref, out_ref, sem):
    copy = pltpu.make_async_copy(q_ref.at[:, block_of(1 - place_ref[2], out_ref.shape[1])], out_ref, sem)
    copy.start()
    copy.wait()


def own_kernel(place_ref, lengths_ref, q_ref, kv_ref, *refs, side):
    if side == 0:
        queries_ref, max_ref, acc_ref, lows_ref, bounds_ref, ahead_ref, q_side_ref, sem = refs
        fetch = pltpu.make_async_copy(q_ref.at[:, block_of(place_ref[2], q_side_ref.shape[1])], q_side_ref, sem)
        fetch.start()
    else:
        _, _, _, lows_ref, queries_ref, max_ref, acc_ref, ahead_ref = refs
        q_side_ref = q_ref
    rows, wide = q_side_ref.shape
    kv_heads = kv_ref.shape[3] // HD
    heads = wide // (kv_heads * PARTS * HD)
    half = place_ref[2]
    first, other = place_ref[side], place_ref[1 - side]
    query_pos = first + lax.broadcasted_iota(jnp.int32, (rows, rows), 0)
    if side == 0:
        for i in range(2):
            lows_ref[i] = doc_start_rows(lengths_ref, place_ref[i], rows)
            bounds_ref[2 * i], bounds_ref[2 * i + 1] = doc_starts(lengths_ref, place_ref[i], place_ref[i] + rows - 1)
    lows = lows_ref[side]
    key_pos = positions(first, rows)
    diagonal = (key_pos >= lows) & (key_pos <= query_pos)
    earlier = positions(other, rows) >= lows
    if side == 0:
        fetch.wait()

    def at(g, part):
        return block_of((side * kv_heads + g) * PARTS + part, heads * rows)

    def place_queries(i, _):
        q = q_side_ref[:, block_of(i, heads * HD)]
        queries_ref[block_of(side * kv_heads * PARTS + i, heads * rows), :] = jnp.concatenate(
            [q[:, h * HD : (h + 1) * HD] for h in range(heads)], axis=0
        )
        return 0

    lax.fori_loop(0, kv_heads * PARTS, place_queries, 0)

    def store(g, part, row_max, acc):
        max_ref[at(g, part), :] = row_max
        acc_ref[at(g, part), :] = acc

    def work(blocks, allowed):
        def of(i, g):
            return jnp.concatenate([kv_ref[block, i, :, block_of(g, HD)] for block in blocks], axis=0)

        pipeline(
            kv_heads,
            ahead_ref.at[:, : len(blocks) * rows],
            allowed,
            lambda g, part: scores_for(queries_ref[at(g, part), :], of(0, g)),
            lambda g: of(1, g),
            lambda g, part: (None, None),
            store,
        )

    pl.when(half == side)(lambda: work([side], diagonal))
    pl.when(half != side)(lambda: work([1 - side, side], jnp.concatenate([earlier, diagonal], axis=1)))


def span_steps(place_ref, bounds_ref, lows_ref, kv_refs, queries_ref, ahead_ref, numbers, side, load, store):
    rows = kv_refs[0].shape[2]
    kv_heads = kv_refs[0].shape[3] // HD
    key_starts = [(place_ref[3 + 2 * number], place_ref[4 + 2 * number]) for number in numbers]
    lo_first, lo_last = bounds_ref[2 * side], bounds_ref[2 * side + 1]
    needed = [jnp.maximum(*starts) + rows > lo_first for starts in key_starts]

    def at(g, part):
        return block_of((side * kv_heads + g) * PARTS + part, ahead_ref.shape[0])

    def work(chosen, masked):
        def of(i, g):
            parts = [kv_refs[n][block, i, :, block_of(g, HD)] for n in chosen for block in range(2)]
            return jnp.concatenate(parts, axis=0)

        allowed = None
        if masked:
            lows = lows_ref[side]
            allowed = jnp.concatenate(
                [positions(start, rows) >= lows for n in chosen for start in key_starts[n]], axis=1
            )
        pipeline(
            kv_heads,
            ahead_ref.at[:, : 2 * rows * len(chosen)],
            allowed,
            lambda g, part: scores_for(queries_ref[at(g, part), :], of(0, g)),
            lambda g: of(1, g),
            lambda g, part: load(at(g, part)),
            lambda g, part, row_max, acc: store(g, part, at(g, part), row_max, acc),
        )

    if len(numbers) == 1:
        whole = jnp.minimum(*key_starts[0]) >= lo_last
        pl.when(whole)(lambda: work([0], False))
        pl.when(needed[0] & jnp.logical_not(whole))(lambda: work([0], True))
        return needed[0]
    pl.when(needed[0] & needed[1])(lambda: work([0, 1], True))
    pl.when(needed[0] & jnp.logical_not(needed[1]))(lambda: work([0], True))
    pl.when(needed[1] & jnp.logical_not(needed[0]))(lambda: work([1], True))
    return needed[0] | needed[1]


def span_kernel(place_ref, bounds_ref, lows_ref, *refs, numbers):
    kv_refs, (queries_ref, _, _, max_ref, acc_ref, ahead_ref) = refs[: len(numbers)], refs[len(numbers) :]

    def load(at):
        return max_ref[at, :], acc_ref[at, :]

    def store(g, part, at, row_max, acc):
        max_ref[at, :] = row_max
        acc_ref[at, :] = acc

    def one_side(side, _):
        span_steps(place_ref, bounds_ref, lows_ref, kv_refs, queries_ref, ahead_ref, numbers, side, load, store)
        return 0

    lax.fori_loop(0, 2, one_side, 0)


def last_kernel(place_ref, bounds_ref, lows_ref, *refs, numbers, side):
    kv_refs, (queries_ref, max_ref, acc_ref, out_ref, ahead_ref, *refs) = refs[: len(numbers)], refs[len(numbers) :]
    rows = kv_refs[0].shape[2]
    kv_heads = kv_refs[0].shape[3] // HD
    chunk = ahead_ref.shape[0]
    heads = chunk // rows
    out = out_ref
    if refs:
        out, sems = refs

    def load(at):
        return max_ref[at, :], acc_ref[at, :]

    def copy_out(piece):
        whole = place_ref[2] * (kv_heads * PARTS) + piece
        return pltpu.make_async_copy(
            out.at[:, block_of(piece, heads * HD)], out_ref.at[:, block_of(whole, heads * HD)], sems.at[piece]
        )

    def finish(g, part, at, row_max, acc):
        finished = (acc[:, :HD] * (1.0 / acc[:, HD:])).astype(out.dtype)
        out[:, block_of(g * PARTS + part, heads * HD)] = jnp.concatenate(
            [finished[h * rows : (h + 1) * rows] for h in range(heads)], axis=1
        )
        if refs:
            copy_out(g * PARTS + part).start()

    needed = span_steps(place_ref, bounds_ref, lows_ref, kv_refs, queries_ref, ahead_ref, numbers, side, load, finish)

    @pl.when(jnp.logical_not(needed))
    def _():
        def one_head(g, _):
            for part in range(PARTS):
                finish(g, part, None, *load(block_of((side * kv_heads + g) * PARTS + part, chunk)))
            return 0

        lax.fori_loop(0, kv_heads, one_head, 0)

    if refs:
        for piece in range(kv_heads * PARTS):
            copy_out(piece).wait()


def join_kernel(place_ref, far_ref, out_in, out_ref, sems):
    del out_in
    pieces = sems.shape[0]
    rows = far_ref.shape[0] // pieces
    columns = block_of(1 - place_ref[2], far_ref.shape[1])
    copies = [
        pltpu.make_async_copy(
            far_ref.at[pl.ds(i * rows, rows), :], out_ref.at[pl.ds(i * rows, rows), columns], sems.at[i]
        )
        for i in range(pieces)
    ]
    for copy in copies:
        copy.start()
    for copy in copies:
        copy.wait()


def per_device(queries, keys, values, doc_lengths):
    rows, all_heads = queries.shape
    half_heads = all_heads // 2
    head_rows = (all_heads // HD) * rows
    half, span = lax.axis_index("head"), lax.axis_index("ctx")
    cores = lax.axis_size("head")
    place_in_group = lax.rem(span, REACH)

    nowhere = -2 * REACH

    def origin(kind):
        if kind == SHIFT:
            return span - REACH
        late = place_in_group >= REACH // 2
        from_place = place_in_group ^ (OPPOSITE if kind == SHIFT_OPPOSITE else kind)
        here = span - place_in_group + from_place
        if kind == SHIFT_OPPOSITE:
            return jnp.where(late, nowhere, here - REACH)
        if kind == OPPOSITE:
            return jnp.where(late, here, nowhere)
        return here - jnp.where(from_place > place_in_group, REACH, 0)

    parts = [(span * cores + half) * rows, (span * cores + 1 - half) * rows, half]
    for kinds in ROUNDS:
        start = jnp.where(half == 0, origin(kinds[0]), origin(kinds[1]))
        parts += [(start * cores + half) * rows, (start * cores + 1 - half) * rows]
    place = jnp.stack(parts).astype(jnp.int32)

    vmem = pl.BlockSpec(memory_space=pltpu.VMEM)
    smem = pl.BlockSpec(memory_space=pltpu.SMEM)
    anywhere = pl.BlockSpec(memory_space=pl.ANY)
    hbm = pl.BlockSpec(memory_space=pltpu.MemorySpace.HBM)
    placed_shape = jax.ShapeDtypeStruct((head_rows, HD), queries.dtype)
    max_shape = jax.ShapeDtypeStruct((head_rows, HD), jnp.float32)
    acc_shape = jax.ShapeDtypeStruct((head_rows, 2 * HD), jnp.float32)
    side_shape = jax.ShapeDtypeStruct((rows, half_heads), queries.dtype)
    common = dict(
        compiler_params=pltpu.CompilerParams(vmem_limit_bytes=24 * 1024 * 1024),
        cost_estimate=pl.CostEstimate(flops=0, bytes_accessed=0, transcendentals=0),
    )

    def heads_of(array, core):
        width = array.shape[1] // 2
        return lax.dynamic_slice_in_dim(array, core * width, width, 1)

    to_give = jnp.stack([heads_of(keys, 1 - half), heads_of(values, 1 - half)])
    given = to_other_core(to_give)
    given, queries = lax.optimization_barrier((given, queries))
    own = jnp.stack([jnp.stack([heads_of(keys, half), heads_of(values, half)]), given])
    arrived = [send_round(own, kinds) for kinds in ROUNDS[:2]]
    q_far = to_other_core(
        pl.pallas_call(
            pick_kernel,
            in_specs=[smem, hbm],
            out_specs=vmem,
            out_shape=side_shape,
            scratch_shapes=[pltpu.SemaphoreType.DMA],
            name="pick_queries",
            **common,
        )(place, queries)
    )

    chunk_heads = queries.shape[1] // keys.shape[1] // PARTS
    ahead = pltpu.VMEM((chunk_heads * rows, 4 * rows), jnp.float32)
    state_shapes = (placed_shape, max_shape, acc_shape)
    lows_shape = jax.ShapeDtypeStruct((2, rows, rows), jnp.int32)
    bounds_shape = jax.ShapeDtypeStruct((4,), jnp.int32)
    *state, lows, bounds = pl.pallas_call(
        functools.partial(own_kernel, side=0),
        in_specs=[smem, smem, hbm, vmem],
        out_specs=(vmem, vmem, vmem, vmem, smem),
        out_shape=state_shapes + (lows_shape, bounds_shape),
        scratch_shapes=[ahead, pltpu.VMEM((rows, half_heads), queries.dtype), pltpu.SemaphoreType.DMA],
        name="attend_own_near",
        **{**common, "cost_estimate": pl.CostEstimate(flops=10**11, bytes_accessed=0, transcendentals=0)},
    )(place, doc_lengths, queries, own)
    placed, row_max, acc = pl.pallas_call(
        functools.partial(own_kernel, side=1),
        in_specs=[smem, smem] + [vmem] * 6,
        out_specs=(vmem, vmem, vmem),
        out_shape=state_shapes,
        input_output_aliases={4: 0, 5: 1, 6: 2},
        scratch_shapes=[ahead],
        name="attend_own_far",
        **common,
    )(place, doc_lengths, q_far, own, *state, lows)

    def attend(kv, row_max, acc, number):
        return pl.pallas_call(
            functools.partial(span_kernel, numbers=tuple(range(number, number + len(kv)))),
            in_specs=[smem, smem] + [vmem] * (len(kv) + 4),
            out_specs=(vmem, vmem),
            out_shape=(max_shape, acc_shape),
            input_output_aliases={len(kv) + 4: 0, len(kv) + 5: 1},
            scratch_shapes=[ahead],
            name="attend_spans",
            **common,
        )(place, bounds, lows, *kv, placed, row_max, acc)

    behind, acc = lax.optimization_barrier((arrived[0], acc))
    opposite, acc = lax.optimization_barrier((arrived[1], acc))

    def plane_round(number):
        sends = [jnp.where((place_in_group ^ kind) > place_in_group, own, behind) for kind in ROUNDS[number]]
        return jnp.where(half == 0, *sends)

    first = send_round(plane_round(2), ROUNDS[2])
    relayed = send_round(opposite, ROUNDS[3])
    row_max, acc = attend([behind, opposite], row_max, acc, 0)
    to_second, first, acc = lax.optimization_barrier((plane_round(4), first, acc))
    second = send_round(to_second, ROUNDS[4])
    row_max, acc = attend([first], row_max, acc, 2)

    last_args = (place, bounds, lows, relayed, second, placed, row_max, acc)
    out_far = pl.pallas_call(
        functools.partial(last_kernel, numbers=(3, 4), side=1),
        in_specs=[smem, smem] + [vmem] * 6,
        out_specs=vmem,
        out_shape=side_shape,
        scratch_shapes=[ahead],
        name="attend_last_far",
        **common,
    )(*last_args)
    out = pl.pallas_call(
        functools.partial(last_kernel, numbers=(3, 4), side=0),
        in_specs=[smem, smem] + [vmem] * 6,
        out_specs=anywhere,
        out_shape=jax.ShapeDtypeStruct(queries.shape, queries.dtype),
        scratch_shapes=[
            ahead,
            pltpu.VMEM((rows, half_heads), queries.dtype),
            pltpu.SemaphoreType.DMA((half_heads // (chunk_heads * HD),)),
        ],
        name="attend_last_near",
        **common,
    )(*last_args)
    return pl.pallas_call(
        join_kernel,
        in_specs=[smem, vmem, anywhere],
        out_specs=anywhere,
        out_shape=jax.ShapeDtypeStruct(queries.shape, queries.dtype),
        input_output_aliases={2: 0},
        scratch_shapes=[pltpu.SemaphoreType.DMA((rows // 16,))],
        name="join_heads",
        **common,
    )(place, to_other_core(out_far), out)


def solution(mesh):
    placed = P(AXES, None)
    return jax.shard_map(
        per_device, mesh=mesh, in_specs=(placed, placed, placed, P()), out_specs=placed, check_vma=False
    )
```

```python
import functools
import math

import jax
import jax.numpy as jnp
from jax import lax
from jax.experimental import pallas as pl
from jax.experimental.pallas import tpu as pltpu
from jax.sharding import PartitionSpec as P

HD = 128
REACH = 4
NEVER = -1e30
SCORE_SCALE = HD ** (-0.5) * math.log2(math.e)
PARTS = 2
AXES = ("ctx", "head")
SHIFT, SHIFT_OPPOSITE, OPPOSITE = "shift", "shift opposite", REACH - 1
ROUNDS = ((SHIFT, SHIFT), (OPPOSITE, OPPOSITE), (1, 2), (SHIFT_OPPOSITE, SHIFT_OPPOSITE), (2, 1))


def send_round(block, kinds):
    spans, cores = lax.axis_size("ctx"), lax.axis_size("head")
    pairs = []
    for s in range(spans):
        for core, kind in enumerate(kinds):
            if kind in (SHIFT, SHIFT_OPPOSITE):
                target = s + REACH
                if target >= spans or (kind == SHIFT_OPPOSITE and s % REACH >= REACH // 2):
                    continue
            else:
                target = s ^ kind
            pairs.append((s * cores + core, target * cores + core))
    return lax.ppermute(block, AXES, pairs)


def to_other_core(block):
    cores = lax.axis_size("head")
    return lax.ppermute(block, "head", [(h, cores - 1 - h) for h in range(cores)])


def doc_starts(lengths_ref, first, last):
    def one_doc(i, carry):
        start, lo_first, lo_last = carry
        start = start + lengths_ref[i]
        return start, jnp.where(start <= first, start, lo_first), jnp.where(start <= last, start, lo_last)

    zero = jnp.int32(0)
    _, lo_first, lo_last = lax.fori_loop(0, lengths_ref.shape[0], one_doc, (zero, zero, zero))
    return lo_first, lo_last


def doc_start_rows(lengths_ref, first_query, rows):
    pos = first_query + lax.broadcasted_iota(jnp.int32, (rows, rows), 0)

    def one_doc(i, carry):
        start, lo = carry
        start = start + lengths_ref[i]
        return start, jnp.where(start <= pos, start, lo)

    zero = jnp.zeros((rows, rows), jnp.int32)
    return lax.fori_loop(0, lengths_ref.shape[0], one_doc, (jnp.int32(0), zero))[1]


def block_of(at, size):
    return pl.ds(pl.multiple_of(at * size, size), size)


def positions(start, rows):
    return start + lax.broadcasted_iota(jnp.int32, (rows, rows), 1)


def softmax_step(scores, allowed, max_before):
    if allowed is not None:
        allowed = jnp.concatenate([allowed] * (scores.shape[0] // allowed.shape[0]), axis=0)
        scores = jnp.where(allowed, scores, NEVER)
    row_max = jnp.broadcast_to(jnp.max(scores, axis=1, keepdims=True), (scores.shape[0], HD))
    rescale = None
    if max_before is not None:
        row_max = jnp.maximum(max_before, row_max)
        rescale = jnp.exp2((max_before - row_max) * SCORE_SCALE)
    shift = jnp.concatenate([row_max] * (scores.shape[1] // HD), axis=1)
    return jnp.exp2((scores - shift) * SCORE_SCALE).astype(jnp.bfloat16), row_max, rescale


def scores_for(queries, keys):
    return lax.dot_general(queries, keys, (((1,), (1,)), ((), ())), preferred_element_type=jnp.float32)


def pipeline(kv_heads, ahead_ref, allowed, scores_of, values_of, before_of, store):
    def finish(g, part, scores):
        max_before, acc_before = before_of(g, part)
        weights, row_max, rescale = softmax_step(scores, allowed, max_before)
        values = values_of(g)
        widened = jnp.concatenate([values, jnp.ones_like(values)], axis=1)
        acc = jnp.dot(weights, widened, preferred_element_type=jnp.float32)
        if rescale is not None:
            acc = acc_before * jnp.concatenate([rescale] * 2, axis=1) + acc
        store(g, part, row_max, acc)

    ahead_ref[...] = scores_of(0, 0)

    def one_head(g, _):
        scores = ahead_ref[...]
        for part in range(PARTS):
            if part + 1 < PARTS:
                later = scores_of(g, part + 1)
            else:
                later = scores_of(jnp.minimum(g + 1, kv_heads - 1), 0)
            finish(g, part, scores)
            scores = later
        ahead_ref[...] = scores
        return 0

    lax.fori_loop(0, kv_heads, one_head, 0)


def pick_kernel(place_ref, q_ref, out_ref, sem):
    copy = pltpu.make_async_copy(q_ref.at[:, block_of(1 - place_ref[2], out_ref.shape[1])], out_ref, sem)
    copy.start()
    copy.wait()


def own_kernel(place_ref, lengths_ref, q_ref, kv_ref, *refs, side):
    if side == 0:
        queries_ref, max_ref, acc_ref, lows_ref, bounds_ref, ahead_ref, q_side_ref, sem = refs
        fetch = pltpu.make_async_copy(q_ref.at[:, block_of(place_ref[2], q_side_ref.shape[1])], q_side_ref, sem)
        fetch.start()
    else:
        _, _, _, lows_ref, queries_ref, max_ref, acc_ref, ahead_ref = refs
        q_side_ref = q_ref
    rows, wide = q_side_ref.shape
    kv_heads = kv_ref.shape[3] // HD
    heads = wide // (kv_heads * PARTS * HD)
    half = place_ref[2]
    first, other = place_ref[side], place_ref[1 - side]
    query_pos = first + lax.broadcasted_iota(jnp.int32, (rows, rows), 0)
    if side == 0:
        for i in range(2):
            lows_ref[i] = doc_start_rows(lengths_ref, place_ref[i], rows)
            bounds_ref[2 * i], bounds_ref[2 * i + 1] = doc_starts(lengths_ref, place_ref[i], place_ref[i] + rows - 1)
    lows = lows_ref[side]
    key_pos = positions(first, rows)
    diagonal = (key_pos >= lows) & (key_pos <= query_pos)
    earlier = positions(other, rows) >= lows
    if side == 0:
        fetch.wait()

    def at(g, part):
        return block_of((side * kv_heads + g) * PARTS + part, heads * rows)

    def place_queries(i, _):
        q = q_side_ref[:, block_of(i, heads * HD)]
        queries_ref[block_of(side * kv_heads * PARTS + i, heads * rows), :] = jnp.concatenate(
            [q[:, h * HD : (h + 1) * HD] for h in range(heads)], axis=0
        )
        return 0

    lax.fori_loop(0, kv_heads * PARTS, place_queries, 0)

    def store(g, part, row_max, acc):
        max_ref[at(g, part), :] = row_max
        acc_ref[at(g, part), :] = acc

    def work(blocks, allowed):
        def of(i, g):
            return jnp.concatenate([kv_ref[block, i, :, block_of(g, HD)] for block in blocks], axis=0)

        pipeline(
            kv_heads,
            ahead_ref.at[:, : len(blocks) * rows],
            allowed,
            lambda g, part: scores_for(queries_ref[at(g, part), :], of(0, g)),
            lambda g: of(1, g),
            lambda g, part: (None, None),
            store,
        )

    pl.when(half == side)(lambda: work([side], diagonal))
    pl.when(half != side)(lambda: work([1 - side, side], jnp.concatenate([earlier, diagonal], axis=1)))


def span_steps(place_ref, bounds_ref, lows_ref, kv_refs, queries_ref, ahead_ref, numbers, side, load, store):
    rows = kv_refs[0].shape[2]
    kv_heads = kv_refs[0].shape[3] // HD
    key_starts = [(place_ref[3 + 2 * number], place_ref[4 + 2 * number]) for number in numbers]
    lo_first, lo_last = bounds_ref[2 * side], bounds_ref[2 * side + 1]
    needed = [jnp.maximum(*starts) + rows > lo_first for starts in key_starts]

    def at(g, part):
        return block_of((side * kv_heads + g) * PARTS + part, ahead_ref.shape[0])

    def work(chosen, masked):
        def of(i, g):
            parts = [kv_refs[n][block, i, :, block_of(g, HD)] for n in chosen for block in range(2)]
            return jnp.concatenate(parts, axis=0)

        allowed = None
        if masked:
            lows = lows_ref[side]
            allowed = jnp.concatenate(
                [positions(start, rows) >= lows for n in chosen for start in key_starts[n]], axis=1
            )
        pipeline(
            kv_heads,
            ahead_ref.at[:, : 2 * rows * len(chosen)],
            allowed,
            lambda g, part: scores_for(queries_ref[at(g, part), :], of(0, g)),
            lambda g: of(1, g),
            lambda g, part: load(at(g, part)),
            lambda g, part, row_max, acc: store(g, part, at(g, part), row_max, acc),
        )

    if len(numbers) == 1:
        whole = jnp.minimum(*key_starts[0]) >= lo_last
        pl.when(whole)(lambda: work([0], False))
        pl.when(needed[0] & jnp.logical_not(whole))(lambda: work([0], True))
        return needed[0]
    pl.when(needed[0] & needed[1])(lambda: work([0, 1], True))
    pl.when(needed[0] & jnp.logical_not(needed[1]))(lambda: work([0], True))
    pl.when(needed[1] & jnp.logical_not(needed[0]))(lambda: work([1], True))
    return needed[0] | needed[1]


def span_kernel(place_ref, bounds_ref, lows_ref, *refs, numbers):
    kv_refs, (queries_ref, _, _, max_ref, acc_ref, ahead_ref) = refs[: len(numbers)], refs[len(numbers) :]

    def load(at):
        return max_ref[at, :], acc_ref[at, :]

    def store(g, part, at, row_max, acc):
        max_ref[at, :] = row_max
        acc_ref[at, :] = acc

    def one_side(side, _):
        span_steps(place_ref, bounds_ref, lows_ref, kv_refs, queries_ref, ahead_ref, numbers, side, load, store)
        return 0

    lax.fori_loop(0, 2, one_side, 0)


def last_kernel(place_ref, bounds_ref, lows_ref, *refs, numbers, side):
    kv_refs, (queries_ref, max_ref, acc_ref, out_ref, ahead_ref) = refs[: len(numbers)], refs[len(numbers) :]
    rows = kv_refs[0].shape[2]
    kv_heads = kv_refs[0].shape[3] // HD
    chunk = ahead_ref.shape[0]
    heads = chunk // rows

    def load(at):
        return max_ref[at, :], acc_ref[at, :]

    def finish(g, part, at, row_max, acc):
        finished = (acc[:, :HD] * (1.0 / acc[:, HD:])).astype(out_ref.dtype)
        out_ref[:, block_of(g * PARTS + part, heads * HD)] = jnp.concatenate(
            [finished[h * rows : (h + 1) * rows] for h in range(heads)], axis=1
        )

    needed = span_steps(place_ref, bounds_ref, lows_ref, kv_refs, queries_ref, ahead_ref, numbers, side, load, finish)

    @pl.when(jnp.logical_not(needed))
    def _():
        def one_head(g, _):
            for part in range(PARTS):
                finish(g, part, None, *load(block_of((side * kv_heads + g) * PARTS + part, chunk)))
            return 0

        lax.fori_loop(0, kv_heads, one_head, 0)


def join_kernel(place_ref, near_ref, far_ref, out_ref, sems):
    pieces = sems.shape[1]
    rows = far_ref.shape[0] // pieces
    copies = []
    for side, source in enumerate((near_ref, far_ref)):
        columns = block_of(place_ref[2] if side == 0 else 1 - place_ref[2], source.shape[1])
        for i in range(pieces):
            here = pl.ds(i * rows, rows)
            copies.append(pltpu.make_async_copy(source.at[here, :], out_ref.at[here, columns], sems.at[side, i]))
    for copy in copies:
        copy.start()
    for copy in copies:
        copy.wait()


def per_device(queries, keys, values, doc_lengths):
    rows, all_heads = queries.shape
    half_heads = all_heads // 2
    head_rows = (all_heads // HD) * rows
    half, span = lax.axis_index("head"), lax.axis_index("ctx")
    cores = lax.axis_size("head")
    place_in_group = lax.rem(span, REACH)

    nowhere = -2 * REACH

    def origin(kind):
        if kind == SHIFT:
            return span - REACH
        late = place_in_group >= REACH // 2
        from_place = place_in_group ^ (OPPOSITE if kind == SHIFT_OPPOSITE else kind)
        here = span - place_in_group + from_place
        if kind == SHIFT_OPPOSITE:
            return jnp.where(late, nowhere, here - REACH)
        if kind == OPPOSITE:
            return jnp.where(late, here, nowhere)
        return here - jnp.where(from_place > place_in_group, REACH, 0)

    parts = [(span * cores + half) * rows, (span * cores + 1 - half) * rows, half]
    for kinds in ROUNDS:
        start = jnp.where(half == 0, origin(kinds[0]), origin(kinds[1]))
        parts += [(start * cores + half) * rows, (start * cores + 1 - half) * rows]
    place = jnp.stack(parts).astype(jnp.int32)

    vmem = pl.BlockSpec(memory_space=pltpu.VMEM)
    smem = pl.BlockSpec(memory_space=pltpu.SMEM)
    anywhere = pl.BlockSpec(memory_space=pl.ANY)
    hbm = pl.BlockSpec(memory_space=pltpu.MemorySpace.HBM)
    placed_shape = jax.ShapeDtypeStruct((head_rows, HD), queries.dtype)
    max_shape = jax.ShapeDtypeStruct((head_rows, HD), jnp.float32)
    acc_shape = jax.ShapeDtypeStruct((head_rows, 2 * HD), jnp.float32)
    side_shape = jax.ShapeDtypeStruct((rows, half_heads), queries.dtype)
    common = dict(
        compiler_params=pltpu.CompilerParams(vmem_limit_bytes=24 * 1024 * 1024),
        cost_estimate=pl.CostEstimate(flops=0, bytes_accessed=0, transcendentals=0),
    )

    def heads_of(array, core):
        width = array.shape[1] // 2
        return lax.dynamic_slice_in_dim(array, core * width, width, 1)

    to_give = jnp.stack([heads_of(keys, 1 - half), heads_of(values, 1 - half)])
    given = to_other_core(to_give)
    given, queries = lax.optimization_barrier((given, queries))
    own = jnp.stack([jnp.stack([heads_of(keys, half), heads_of(values, half)]), given])
    arrived = [send_round(own, kinds) for kinds in ROUNDS[:2]]
    q_far = to_other_core(
        pl.pallas_call(
            pick_kernel,
            in_specs=[smem, hbm],
            out_specs=vmem,
            out_shape=side_shape,
            scratch_shapes=[pltpu.SemaphoreType.DMA],
            name="pick_queries",
            **common,
        )(place, queries)
    )

    chunk_heads = queries.shape[1] // keys.shape[1] // PARTS
    ahead = pltpu.VMEM((chunk_heads * rows, 4 * rows), jnp.float32)
    state_shapes = (placed_shape, max_shape, acc_shape)
    lows_shape = jax.ShapeDtypeStruct((2, rows, rows), jnp.int32)
    bounds_shape = jax.ShapeDtypeStruct((4,), jnp.int32)
    *state, lows, bounds = pl.pallas_call(
        functools.partial(own_kernel, side=0),
        in_specs=[smem, smem, hbm, vmem],
        out_specs=(vmem, vmem, vmem, vmem, smem),
        out_shape=state_shapes + (lows_shape, bounds_shape),
        scratch_shapes=[ahead, pltpu.VMEM((rows, half_heads), queries.dtype), pltpu.SemaphoreType.DMA],
        name="attend_own_near",
        **{**common, "cost_estimate": pl.CostEstimate(flops=10**11, bytes_accessed=0, transcendentals=0)},
    )(place, doc_lengths, queries, own)
    placed, row_max, acc = pl.pallas_call(
        functools.partial(own_kernel, side=1),
        in_specs=[smem, smem] + [vmem] * 6,
        out_specs=(vmem, vmem, vmem),
        out_shape=state_shapes,
        input_output_aliases={4: 0, 5: 1, 6: 2},
        scratch_shapes=[ahead],
        name="attend_own_far",
        **common,
    )(place, doc_lengths, q_far, own, *state, lows)

    def attend(kv, row_max, acc, number):
        return pl.pallas_call(
            functools.partial(span_kernel, numbers=tuple(range(number, number + len(kv)))),
            in_specs=[smem, smem] + [vmem] * (len(kv) + 4),
            out_specs=(vmem, vmem),
            out_shape=(max_shape, acc_shape),
            input_output_aliases={len(kv) + 4: 0, len(kv) + 5: 1},
            scratch_shapes=[ahead],
            name="attend_spans",
            **common,
        )(place, bounds, lows, *kv, placed, row_max, acc)

    behind, acc = lax.optimization_barrier((arrived[0], acc))
    opposite, acc = lax.optimization_barrier((arrived[1], acc))

    def plane_round(number):
        sends = [jnp.where((place_in_group ^ kind) > place_in_group, own, behind) for kind in ROUNDS[number]]
        return jnp.where(half == 0, *sends)

    first = send_round(plane_round(2), ROUNDS[2])
    relayed = send_round(opposite, ROUNDS[3])
    row_max, acc = attend([behind, opposite], row_max, acc, 0)
    to_second, first, acc = lax.optimization_barrier((plane_round(4), first, acc))
    second = send_round(to_second, ROUNDS[4])
    row_max, acc = attend([first], row_max, acc, 2)

    last_args = (place, bounds, lows, relayed, second, placed, row_max, acc)
    def finish(side, name):
        return pl.pallas_call(
            functools.partial(last_kernel, numbers=(3, 4), side=side),
            in_specs=[smem, smem] + [vmem] * 6,
            out_specs=vmem,
            out_shape=side_shape,
            scratch_shapes=[ahead],
            name=name,
            **common,
        )(*last_args)

    out_far = to_other_core(finish(1, "attend_last_far"))
    return pl.pallas_call(
        join_kernel,
        in_specs=[smem, vmem, vmem],
        out_specs=anywhere,
        out_shape=jax.ShapeDtypeStruct(queries.shape, queries.dtype),
        scratch_shapes=[pltpu.SemaphoreType.DMA((2, 4))],
        name="join_heads",
        **common,
    )(place, finish(0, "attend_last_near"), out_far)


def solution(mesh):
    placed = P(AXES, None)
    return jax.shard_map(
        per_device, mesh=mesh, in_specs=(placed, placed, placed, P()), out_specs=placed, check_vma=False
    )
```

```python
import functools
import math

import jax
import jax.numpy as jnp
from jax import lax
from jax.experimental import pallas as pl
from jax.experimental.pallas import tpu as pltpu
from jax.sharding import PartitionSpec as P

HD = 128
REACH = 4
NEVER = -1e30
SCORE_SCALE = HD ** (-0.5) * math.log2(math.e)
PARTS = 2
AXES = ("ctx", "head")
SHIFT, SHIFT_OPPOSITE, OPPOSITE = "shift", "shift opposite", REACH - 1
ROUNDS = ((SHIFT, SHIFT), (OPPOSITE, OPPOSITE), (1, 2), (SHIFT_OPPOSITE, SHIFT_OPPOSITE), (2, 1))
BOUNDS = 3 + 2 * len(ROUNDS)


def send_round(block, kinds):
    spans, cores = lax.axis_size("ctx"), lax.axis_size("head")
    pairs = []
    for s in range(spans):
        for core, kind in enumerate(kinds):
            if kind in (SHIFT, SHIFT_OPPOSITE):
                target = s + REACH
                if target >= spans or (kind == SHIFT_OPPOSITE and s % REACH >= REACH // 2):
                    continue
            else:
                target = s ^ kind
            pairs.append((s * cores + core, target * cores + core))
    return lax.ppermute(block, AXES, pairs)


def to_other_core(block):
    cores = lax.axis_size("head")
    return lax.ppermute(block, "head", [(h, cores - 1 - h) for h in range(cores)])


def doc_starts(lengths_ref, first, last):
    def one_doc(i, carry):
        start, lo_first, lo_last = carry
        start = start + lengths_ref[i]
        return start, jnp.where(start <= first, start, lo_first), jnp.where(start <= last, start, lo_last)

    zero = jnp.int32(0)
    _, lo_first, lo_last = lax.fori_loop(0, lengths_ref.shape[0], one_doc, (zero, zero, zero))
    return lo_first, lo_last


def doc_start_rows(lengths_ref, first_query, rows):
    pos = first_query + lax.broadcasted_iota(jnp.int32, (rows, rows), 0)

    def one_doc(i, carry):
        start, lo = carry
        start = start + lengths_ref[i]
        return start, jnp.where(start <= pos, start, lo)

    zero = jnp.zeros((rows, rows), jnp.int32)
    return lax.fori_loop(0, lengths_ref.shape[0], one_doc, (jnp.int32(0), zero))[1]


def block_of(at, size):
    return pl.ds(pl.multiple_of(at * size, size), size)


def positions(start, rows):
    return start + lax.broadcasted_iota(jnp.int32, (rows, rows), 1)


def softmax_step(scores, allowed, max_before):
    if allowed is not None:
        allowed = jnp.concatenate([allowed] * (scores.shape[0] // allowed.shape[0]), axis=0)
        scores = jnp.where(allowed, scores, NEVER)
    row_max = jnp.broadcast_to(jnp.max(scores, axis=1, keepdims=True), (scores.shape[0], HD))
    rescale = None
    if max_before is not None:
        row_max = jnp.maximum(max_before, row_max)
        rescale = jnp.exp2((max_before - row_max) * SCORE_SCALE)
    shift = jnp.concatenate([row_max] * (scores.shape[1] // HD), axis=1)
    return jnp.exp2((scores - shift) * SCORE_SCALE).astype(jnp.bfloat16), row_max, rescale


def scores_for(queries, keys):
    return lax.dot_general(queries, keys, (((1,), (1,)), ((), ())), preferred_element_type=jnp.float32)


def pipeline(kv_heads, ahead_ref, allowed, scores_of, values_of, before_of, store):
    def finish(g, part, scores):
        max_before, acc_before = before_of(g, part)
        weights, row_max, rescale = softmax_step(scores, allowed, max_before)
        values = values_of(g)
        widened = jnp.concatenate([values, jnp.ones_like(values)], axis=1)
        acc = jnp.dot(weights, widened, preferred_element_type=jnp.float32)
        if rescale is not None:
            acc = acc_before * jnp.concatenate([rescale] * 2, axis=1) + acc
        store(g, part, row_max, acc)

    ahead_ref[...] = scores_of(0, 0)

    def one_head(g, _):
        scores = ahead_ref[...]
        for part in range(PARTS):
            if part + 1 < PARTS:
                later = scores_of(g, part + 1)
            else:
                later = scores_of(jnp.minimum(g + 1, kv_heads - 1), 0)
            finish(g, part, scores)
            scores = later
        ahead_ref[...] = scores
        return 0

    lax.fori_loop(0, kv_heads, one_head, 0)


def pick_kernel(place_ref, q_ref, out_ref, sem):
    copy = pltpu.make_async_copy(q_ref.at[:, block_of(1 - place_ref[2], out_ref.shape[1])], out_ref, sem)
    copy.start()
    copy.wait()


def own_kernel(place_ref, *refs, side):
    if side == 0:
        lengths_ref, q_ref, kv_ref, *refs = refs
        queries_ref, max_ref, acc_ref, lows_ref, info_ref, ahead_ref, q_side_ref, sem = refs
        fetch = pltpu.make_async_copy(q_ref.at[:, block_of(place_ref[2], q_side_ref.shape[1])], q_side_ref, sem)
        fetch.start()
    else:
        q_ref, kv_ref, _, _, _, lows_ref, queries_ref, max_ref, acc_ref, ahead_ref = refs
        q_side_ref = q_ref
    rows, wide = q_side_ref.shape
    kv_heads = kv_ref.shape[3] // HD
    heads = wide // (kv_heads * PARTS * HD)
    half = place_ref[2]
    first, other = place_ref[side], place_ref[1 - side]
    query_pos = first + lax.broadcasted_iota(jnp.int32, (rows, rows), 0)
    if side == 0:
        for i in range(2):
            lows_ref[i] = doc_start_rows(lengths_ref, place_ref[i], rows)
            low, high = doc_starts(lengths_ref, place_ref[i], place_ref[i] + rows - 1)
            info_ref[BOUNDS + 2 * i], info_ref[BOUNDS + 2 * i + 1] = low, high
        for i in range(BOUNDS):
            info_ref[i] = place_ref[i]
    lows = lows_ref[side]
    key_pos = positions(first, rows)
    diagonal = (key_pos >= lows) & (key_pos <= query_pos)
    earlier = positions(other, rows) >= lows
    if side == 0:
        fetch.wait()

    def at(g, part):
        return block_of((side * kv_heads + g) * PARTS + part, heads * rows)

    def place_queries(i, _):
        q = q_side_ref[:, block_of(i, heads * HD)]
        queries_ref[block_of(side * kv_heads * PARTS + i, heads * rows), :] = jnp.concatenate(
            [q[:, h * HD : (h + 1) * HD] for h in range(heads)], axis=0
        )
        return 0

    lax.fori_loop(0, kv_heads * PARTS, place_queries, 0)

    def store(g, part, row_max, acc):
        max_ref[at(g, part), :] = row_max
        acc_ref[at(g, part), :] = acc

    def work(blocks, allowed):
        def of(i, g):
            return jnp.concatenate([kv_ref[block, i, :, block_of(g, HD)] for block in blocks], axis=0)

        pipeline(
            kv_heads,
            ahead_ref.at[:, : len(blocks) * rows],
            allowed,
            lambda g, part: scores_for(queries_ref[at(g, part), :], of(0, g)),
            lambda g: of(1, g),
            lambda g, part: (None, None),
            store,
        )

    pl.when(half == side)(lambda: work([side], diagonal))
    pl.when(half != side)(lambda: work([1 - side, side], jnp.concatenate([earlier, diagonal], axis=1)))


def span_steps(place_ref, lows_ref, kv_refs, queries_ref, ahead_ref, numbers, side, load, store):
    rows = kv_refs[0].shape[2]
    kv_heads = kv_refs[0].shape[3] // HD
    key_starts = [(place_ref[3 + 2 * number], place_ref[4 + 2 * number]) for number in numbers]
    lo_first, lo_last = place_ref[BOUNDS + 2 * side], place_ref[BOUNDS + 2 * side + 1]
    needed = [jnp.maximum(*starts) + rows > lo_first for starts in key_starts]

    def at(g, part):
        return block_of((side * kv_heads + g) * PARTS + part, ahead_ref.shape[0])

    def work(chosen, masked):
        def of(i, g):
            parts = [kv_refs[n][block, i, :, block_of(g, HD)] for n in chosen for block in range(2)]
            return jnp.concatenate(parts, axis=0)

        allowed = None
        if masked:
            lows = lows_ref[side]
            allowed = jnp.concatenate(
                [positions(start, rows) >= lows for n in chosen for start in key_starts[n]], axis=1
            )
        pipeline(
            kv_heads,
            ahead_ref.at[:, : 2 * rows * len(chosen)],
            allowed,
            lambda g, part: scores_for(queries_ref[at(g, part), :], of(0, g)),
            lambda g: of(1, g),
            lambda g, part: load(at(g, part)),
            lambda g, part, row_max, acc: store(g, part, at(g, part), row_max, acc),
        )

    if len(numbers) == 1:
        whole = jnp.minimum(*key_starts[0]) >= lo_last
        pl.when(whole)(lambda: work([0], False))
        pl.when(needed[0] & jnp.logical_not(whole))(lambda: work([0], True))
        return needed[0]
    pl.when(needed[0] & needed[1])(lambda: work([0, 1], True))
    pl.when(needed[0] & jnp.logical_not(needed[1]))(lambda: work([0], True))
    pl.when(needed[1] & jnp.logical_not(needed[0]))(lambda: work([1], True))
    return needed[0] | needed[1]


def span_kernel(place_ref, lows_ref, *refs, numbers):
    kv_refs, (queries_ref, _, _, max_ref, acc_ref, ahead_ref) = refs[: len(numbers)], refs[len(numbers) :]

    def load(at):
        return max_ref[at, :], acc_ref[at, :]

    def store(g, part, at, row_max, acc):
        max_ref[at, :] = row_max
        acc_ref[at, :] = acc

    def one_side(side, _):
        span_steps(place_ref, lows_ref, kv_refs, queries_ref, ahead_ref, numbers, side, load, store)
        return 0

    lax.fori_loop(0, 2, one_side, 0)


def last_kernel(place_ref, lows_ref, *refs, numbers, side):
    kv_refs, (queries_ref, max_ref, acc_ref, out_ref, ahead_ref) = refs[: len(numbers)], refs[len(numbers) :]
    rows = kv_refs[0].shape[2]
    kv_heads = kv_refs[0].shape[3] // HD
    chunk = ahead_ref.shape[0]
    heads = chunk // rows

    def load(at):
        return max_ref[at, :], acc_ref[at, :]

    def finish(g, part, at, row_max, acc):
        finished = (acc[:, :HD] * (1.0 / acc[:, HD:])).astype(out_ref.dtype)
        out_ref[:, block_of(g * PARTS + part, heads * HD)] = jnp.concatenate(
            [finished[h * rows : (h + 1) * rows] for h in range(heads)], axis=1
        )

    needed = span_steps(place_ref, lows_ref, kv_refs, queries_ref, ahead_ref, numbers, side, load, finish)

    @pl.when(jnp.logical_not(needed))
    def _():
        def one_head(g, _):
            for part in range(PARTS):
                finish(g, part, None, *load(block_of((side * kv_heads + g) * PARTS + part, chunk)))
            return 0

        lax.fori_loop(0, kv_heads, one_head, 0)


def join_kernel(place_ref, near_ref, far_ref, out_ref, sems):
    pieces = sems.shape[1]
    rows = far_ref.shape[0] // pieces
    copies = []
    for side, source in enumerate((near_ref, far_ref)):
        columns = block_of(place_ref[2] if side == 0 else 1 - place_ref[2], source.shape[1])
        for i in range(pieces):
            here = pl.ds(i * rows, rows)
            copies.append(pltpu.make_async_copy(source.at[here, :], out_ref.at[here, columns], sems.at[side, i]))
    for copy in copies:
        copy.start()
    for copy in copies:
        copy.wait()


def per_device(queries, keys, values, doc_lengths):
    rows, all_heads = queries.shape
    half_heads = all_heads // 2
    head_rows = (all_heads // HD) * rows
    half, span = lax.axis_index("head"), lax.axis_index("ctx")
    cores = lax.axis_size("head")
    place_in_group = lax.rem(span, REACH)

    nowhere = -2 * REACH

    def origin(kind):
        if kind == SHIFT:
            return span - REACH
        late = place_in_group >= REACH // 2
        from_place = place_in_group ^ (OPPOSITE if kind == SHIFT_OPPOSITE else kind)
        here = span - place_in_group + from_place
        if kind == SHIFT_OPPOSITE:
            return jnp.where(late, nowhere, here - REACH)
        if kind == OPPOSITE:
            return jnp.where(late, here, nowhere)
        return here - jnp.where(from_place > place_in_group, REACH, 0)

    parts = [(span * cores + half) * rows, (span * cores + 1 - half) * rows, half]
    for kinds in ROUNDS:
        start = jnp.where(half == 0, origin(kinds[0]), origin(kinds[1]))
        parts += [(start * cores + half) * rows, (start * cores + 1 - half) * rows]
    place = jnp.stack(parts).astype(jnp.int32)

    vmem = pl.BlockSpec(memory_space=pltpu.VMEM)
    smem = pl.BlockSpec(memory_space=pltpu.SMEM)
    anywhere = pl.BlockSpec(memory_space=pl.ANY)
    hbm = pl.BlockSpec(memory_space=pltpu.MemorySpace.HBM)
    placed_shape = jax.ShapeDtypeStruct((head_rows, HD), queries.dtype)
    max_shape = jax.ShapeDtypeStruct((head_rows, HD), jnp.float32)
    acc_shape = jax.ShapeDtypeStruct((head_rows, 2 * HD), jnp.float32)
    side_shape = jax.ShapeDtypeStruct((rows, half_heads), queries.dtype)
    common = dict(
        compiler_params=pltpu.CompilerParams(vmem_limit_bytes=24 * 1024 * 1024),
        cost_estimate=pl.CostEstimate(flops=0, bytes_accessed=0, transcendentals=0),
    )

    def heads_of(array, core):
        width = array.shape[1] // 2
        return lax.dynamic_slice_in_dim(array, core * width, width, 1)

    to_give = jnp.stack([heads_of(keys, 1 - half), heads_of(values, 1 - half)])
    given = to_other_core(to_give)
    given, queries = lax.optimization_barrier((given, queries))
    own = jnp.stack([jnp.stack([heads_of(keys, half), heads_of(values, half)]), given])
    arrived = [send_round(own, kinds) for kinds in ROUNDS[:2]]
    q_far = to_other_core(
        pl.pallas_call(
            pick_kernel,
            in_specs=[smem, hbm],
            out_specs=vmem,
            out_shape=side_shape,
            scratch_shapes=[pltpu.SemaphoreType.DMA],
            name="pick_queries",
            **common,
        )(place, queries)
    )

    chunk_heads = queries.shape[1] // keys.shape[1] // PARTS
    ahead = pltpu.VMEM((chunk_heads * rows, 4 * rows), jnp.float32)
    state_shapes = (placed_shape, max_shape, acc_shape)
    lows_shape = jax.ShapeDtypeStruct((2, rows, rows), jnp.int32)
    info_shape = jax.ShapeDtypeStruct((BOUNDS + 4,), jnp.int32)
    *state, lows, info = pl.pallas_call(
        functools.partial(own_kernel, side=0),
        in_specs=[smem, smem, hbm, vmem],
        out_specs=(vmem, vmem, vmem, vmem, smem),
        out_shape=state_shapes + (lows_shape, info_shape),
        scratch_shapes=[ahead, pltpu.VMEM((rows, half_heads), queries.dtype), pltpu.SemaphoreType.DMA],
        name="attend_own_near",
        **{**common, "cost_estimate": pl.CostEstimate(flops=10**11, bytes_accessed=0, transcendentals=0)},
    )(place, doc_lengths, queries, own)
    placed, row_max, acc = pl.pallas_call(
        functools.partial(own_kernel, side=1),
        in_specs=[smem] + [vmem] * 6,
        out_specs=(vmem, vmem, vmem),
        out_shape=state_shapes,
        input_output_aliases={3: 0, 4: 1, 5: 2},
        scratch_shapes=[ahead],
        name="attend_own_far",
        **common,
    )(info, q_far, own, *state, lows)

    def attend(kv, row_max, acc, number):
        return pl.pallas_call(
            functools.partial(span_kernel, numbers=tuple(range(number, number + len(kv)))),
            in_specs=[smem] + [vmem] * (len(kv) + 4),
            out_specs=(vmem, vmem),
            out_shape=(max_shape, acc_shape),
            input_output_aliases={len(kv) + 3: 0, len(kv) + 4: 1},
            scratch_shapes=[ahead],
            name="attend_spans",
            **common,
        )(info, lows, *kv, placed, row_max, acc)

    behind, acc = lax.optimization_barrier((arrived[0], acc))
    opposite, acc = lax.optimization_barrier((arrived[1], acc))

    def plane_round(number):
        sends = [jnp.where((place_in_group ^ kind) > place_in_group, own, behind) for kind in ROUNDS[number]]
        return jnp.where(half == 0, *sends)

    first = send_round(plane_round(2), ROUNDS[2])
    relayed = send_round(opposite, ROUNDS[3])
    row_max, acc = attend([behind, opposite], row_max, acc, 0)
    to_second, first, acc = lax.optimization_barrier((plane_round(4), first, acc))
    second = send_round(to_second, ROUNDS[4])
    row_max, acc = attend([first], row_max, acc, 2)

    last_args = (info, lows, relayed, second, placed, row_max, acc)
    def finish(side, name):
        return pl.pallas_call(
            functools.partial(last_kernel, numbers=(3, 4), side=side),
            in_specs=[smem] + [vmem] * 6,
            out_specs=vmem,
            out_shape=side_shape,
            scratch_shapes=[ahead],
            name=name,
            **common,
        )(*last_args)

    out_far = to_other_core(finish(1, "attend_last_far"))
    return pl.pallas_call(
        join_kernel,
        in_specs=[smem, vmem, vmem],
        out_specs=anywhere,
        out_shape=jax.ShapeDtypeStruct(queries.shape, queries.dtype),
        scratch_shapes=[pltpu.SemaphoreType.DMA((2, 4))],
        name="join_heads",
        **common,
    )(info, finish(0, "attend_last_near"), out_far)


def solution(mesh):
    placed = P(AXES, None)
    return jax.shard_map(
        per_device, mesh=mesh, in_specs=(placed, placed, placed, P()), out_specs=placed, check_vma=False
    )
```

```python
import functools
import math

import jax
import jax.numpy as jnp
from jax import lax
from jax.experimental import pallas as pl
from jax.experimental.pallas import tpu as pltpu
from jax.sharding import PartitionSpec as P

HD = 128
REACH = 4
NEVER = -1e30
SCORE_SCALE = HD ** (-0.5) * math.log2(math.e)
PARTS = 2
AXES = ("ctx", "head")
SHIFT, SHIFT_OPPOSITE, OPPOSITE = "shift", "shift opposite", REACH - 1
ROUNDS = ((SHIFT, SHIFT), (OPPOSITE, OPPOSITE), (1, 2), (SHIFT_OPPOSITE, SHIFT_OPPOSITE), (2, 1), (2, 1))
EARLY, LATE = len(ROUNDS) - 2, len(ROUNDS) - 1
BOUNDS = 3 + 2 * len(ROUNDS)


def takes_part(number, core, place):
    late = (core == 1) & (place >= REACH // 2)
    return late if number == LATE else (number != EARLY) | (late ^ True)


def send_round(block, number):
    spans, cores = lax.axis_size("ctx"), lax.axis_size("head")
    pairs = []
    for s in range(spans):
        for core, kind in enumerate(ROUNDS[number]):
            if not takes_part(number, core, s % REACH):
                continue
            if kind in (SHIFT, SHIFT_OPPOSITE):
                target = s + REACH
                if target >= spans or (kind == SHIFT_OPPOSITE and s % REACH >= REACH // 2):
                    continue
            else:
                target = s ^ kind
            pairs.append((s * cores + core, target * cores + core))
    return lax.ppermute(block, AXES, pairs)


def to_other_core(block):
    cores = lax.axis_size("head")
    return lax.ppermute(block, "head", [(h, cores - 1 - h) for h in range(cores)])


def doc_starts(lengths_ref, first, last):
    def one_doc(i, carry):
        start, lo_first, lo_last = carry
        start = start + lengths_ref[i]
        return start, jnp.where(start <= first, start, lo_first), jnp.where(start <= last, start, lo_last)

    zero = jnp.int32(0)
    _, lo_first, lo_last = lax.fori_loop(0, lengths_ref.shape[0], one_doc, (zero, zero, zero))
    return lo_first, lo_last


def doc_start_rows(lengths_ref, first_query, rows):
    pos = first_query + lax.broadcasted_iota(jnp.int32, (rows, rows), 0)

    def one_doc(i, carry):
        start, lo = carry
        start = start + lengths_ref[i]
        return start, jnp.where(start <= pos, start, lo)

    zero = jnp.zeros((rows, rows), jnp.int32)
    return lax.fori_loop(0, lengths_ref.shape[0], one_doc, (jnp.int32(0), zero))[1]


def block_of(at, size):
    return pl.ds(pl.multiple_of(at * size, size), size)


def positions(start, rows):
    return start + lax.broadcasted_iota(jnp.int32, (rows, rows), 1)


def softmax_step(scores, allowed, max_before):
    if allowed is not None:
        allowed = jnp.concatenate([allowed] * (scores.shape[0] // allowed.shape[0]), axis=0)
        scores = jnp.where(allowed, scores, NEVER)
    row_max = jnp.broadcast_to(jnp.max(scores, axis=1, keepdims=True), (scores.shape[0], HD))
    rescale = None
    if max_before is not None:
        row_max = jnp.maximum(max_before, row_max)
        rescale = jnp.exp2((max_before - row_max) * SCORE_SCALE)
    shift = jnp.concatenate([row_max] * (scores.shape[1] // HD), axis=1)
    return jnp.exp2((scores - shift) * SCORE_SCALE).astype(jnp.bfloat16), row_max, rescale


def scores_for(queries, keys):
    return lax.dot_general(queries, keys, (((1,), (1,)), ((), ())), preferred_element_type=jnp.float32)


def pipeline(kv_heads, ahead_ref, allowed, scores_of, values_of, before_of, store):
    def finish(g, part, scores):
        max_before, acc_before = before_of(g, part)
        weights, row_max, rescale = softmax_step(scores, allowed, max_before)
        values = values_of(g)
        widened = jnp.concatenate([values, jnp.ones_like(values)], axis=1)
        acc = jnp.dot(weights, widened, preferred_element_type=jnp.float32)
        if rescale is not None:
            acc = acc_before * jnp.concatenate([rescale] * 2, axis=1) + acc
        store(g, part, row_max, acc)

    ahead_ref[...] = scores_of(0, 0)

    def one_head(g, _):
        scores = ahead_ref[...]
        for part in range(PARTS):
            if part + 1 < PARTS:
                later = scores_of(g, part + 1)
            else:
                later = scores_of(jnp.minimum(g + 1, kv_heads - 1), 0)
            finish(g, part, scores)
            scores = later
        ahead_ref[...] = scores
        return 0

    lax.fori_loop(0, kv_heads, one_head, 0)


def pick_kernel(place_ref, q_ref, out_ref, sem):
    copy = pltpu.make_async_copy(q_ref.at[:, block_of(1 - place_ref[2], out_ref.shape[1])], out_ref, sem)
    copy.start()
    copy.wait()


def own_kernel(place_ref, *refs, side):
    if side == 0:
        lengths_ref, q_ref, kv_ref, *refs = refs
        queries_ref, max_ref, acc_ref, lows_ref, info_ref, ahead_ref, q_side_ref, sem = refs
        fetch = pltpu.make_async_copy(q_ref.at[:, block_of(place_ref[2], q_side_ref.shape[1])], q_side_ref, sem)
        fetch.start()
    else:
        q_ref, kv_ref, _, _, _, lows_ref, queries_ref, max_ref, acc_ref, ahead_ref = refs
        q_side_ref = q_ref
    rows, wide = q_side_ref.shape
    kv_heads = kv_ref.shape[3] // HD
    heads = wide // (kv_heads * PARTS * HD)
    half = place_ref[2]
    first, other = place_ref[side], place_ref[1 - side]
    query_pos = first + lax.broadcasted_iota(jnp.int32, (rows, rows), 0)
    if side == 0:
        for i in range(2):
            lows_ref[i] = doc_start_rows(lengths_ref, place_ref[i], rows)
            low, high = doc_starts(lengths_ref, place_ref[i], place_ref[i] + rows - 1)
            info_ref[BOUNDS + 2 * i], info_ref[BOUNDS + 2 * i + 1] = low, high
        for i in range(BOUNDS):
            info_ref[i] = place_ref[i]
    lows = lows_ref[side]
    key_pos = positions(first, rows)
    diagonal = (key_pos >= lows) & (key_pos <= query_pos)
    earlier = positions(other, rows) >= lows
    if side == 0:
        fetch.wait()

    def at(g, part):
        return block_of((side * kv_heads + g) * PARTS + part, heads * rows)

    def place_queries(i, _):
        q = q_side_ref[:, block_of(i, heads * HD)]
        queries_ref[block_of(side * kv_heads * PARTS + i, heads * rows), :] = jnp.concatenate(
            [q[:, h * HD : (h + 1) * HD] for h in range(heads)], axis=0
        )
        return 0

    lax.fori_loop(0, kv_heads * PARTS, place_queries, 0)

    def store(g, part, row_max, acc):
        max_ref[at(g, part), :] = row_max
        acc_ref[at(g, part), :] = acc

    def work(blocks, allowed):
        def of(i, g):
            return jnp.concatenate([kv_ref[block, i, :, block_of(g, HD)] for block in blocks], axis=0)

        pipeline(
            kv_heads,
            ahead_ref.at[:, : len(blocks) * rows],
            allowed,
            lambda g, part: scores_for(queries_ref[at(g, part), :], of(0, g)),
            lambda g: of(1, g),
            lambda g, part: (None, None),
            store,
        )

    pl.when(half == side)(lambda: work([side], diagonal))
    pl.when(half != side)(lambda: work([1 - side, side], jnp.concatenate([earlier, diagonal], axis=1)))


def span_steps(place_ref, lows_ref, kv_refs, queries_ref, ahead_ref, numbers, side, load, store):
    rows = kv_refs[0].shape[2]
    kv_heads = kv_refs[0].shape[3] // HD
    key_starts = [(place_ref[3 + 2 * number], place_ref[4 + 2 * number]) for number in numbers]
    lo_first, lo_last = place_ref[BOUNDS + 2 * side], place_ref[BOUNDS + 2 * side + 1]
    needed = [jnp.maximum(*starts) + rows > lo_first for starts in key_starts]

    def at(g, part):
        return block_of((side * kv_heads + g) * PARTS + part, ahead_ref.shape[0])

    def work(chosen, masked):
        def of(i, g):
            parts = [kv_refs[n][block, i, :, block_of(g, HD)] for n in chosen for block in range(2)]
            return jnp.concatenate(parts, axis=0)

        allowed = None
        if masked:
            lows = lows_ref[side]
            allowed = jnp.concatenate(
                [positions(start, rows) >= lows for n in chosen for start in key_starts[n]], axis=1
            )
        pipeline(
            kv_heads,
            ahead_ref.at[:, : 2 * rows * len(chosen)],
            allowed,
            lambda g, part: scores_for(queries_ref[at(g, part), :], of(0, g)),
            lambda g: of(1, g),
            lambda g, part: load(at(g, part)),
            lambda g, part, row_max, acc: store(g, part, at(g, part), row_max, acc),
        )

    if len(numbers) == 1:
        whole = jnp.minimum(*key_starts[0]) >= lo_last
        pl.when(whole)(lambda: work([0], False))
        pl.when(needed[0] & jnp.logical_not(whole))(lambda: work([0], True))
        return needed[0]
    pl.when(needed[0] & needed[1])(lambda: work([0, 1], True))
    pl.when(needed[0] & jnp.logical_not(needed[1]))(lambda: work([0], True))
    pl.when(needed[1] & jnp.logical_not(needed[0]))(lambda: work([1], True))
    if len(numbers) == 3:
        pl.when(needed[2])(lambda: work([2], True))
        return needed[0] | needed[1] | needed[2]
    return needed[0] | needed[1]


def span_kernel(place_ref, lows_ref, *refs, numbers):
    kv_refs, (queries_ref, _, _, max_ref, acc_ref, ahead_ref) = refs[: len(numbers)], refs[len(numbers) :]

    def load(at):
        return max_ref[at, :], acc_ref[at, :]

    def store(g, part, at, row_max, acc):
        max_ref[at, :] = row_max
        acc_ref[at, :] = acc

    def one_side(side, _):
        span_steps(place_ref, lows_ref, kv_refs, queries_ref, ahead_ref, numbers, side, load, store)
        return 0

    lax.fori_loop(0, 2, one_side, 0)


def last_kernel(place_ref, lows_ref, *refs, numbers, side):
    kv_refs, (queries_ref, max_ref, acc_ref, out_ref, ahead_ref) = refs[: len(numbers)], refs[len(numbers) :]
    rows = kv_refs[0].shape[2]
    kv_heads = kv_refs[0].shape[3] // HD
    chunk = ahead_ref.shape[0]
    heads = chunk // rows

    def load(at):
        return max_ref[at, :], acc_ref[at, :]

    def finish(g, part, at, row_max, acc):
        finished = (acc[:, :HD] * (1.0 / acc[:, HD:])).astype(out_ref.dtype)
        out_ref[:, block_of(g * PARTS + part, heads * HD)] = jnp.concatenate(
            [finished[h * rows : (h + 1) * rows] for h in range(heads)], axis=1
        )

    needed = span_steps(place_ref, lows_ref, kv_refs, queries_ref, ahead_ref, numbers, side, load, finish)

    @pl.when(jnp.logical_not(needed))
    def _():
        def one_head(g, _):
            for part in range(PARTS):
                finish(g, part, None, *load(block_of((side * kv_heads + g) * PARTS + part, chunk)))
            return 0

        lax.fori_loop(0, kv_heads, one_head, 0)


def join_kernel(place_ref, near_ref, far_ref, out_ref, sems):
    pieces = sems.shape[1]
    rows = far_ref.shape[0] // pieces
    copies = []
    for side, source in enumerate((near_ref, far_ref)):
        columns = block_of(place_ref[2] if side == 0 else 1 - place_ref[2], source.shape[1])
        for i in range(pieces):
            here = pl.ds(i * rows, rows)
            copies.append(pltpu.make_async_copy(source.at[here, :], out_ref.at[here, columns], sems.at[side, i]))
    for copy in copies:
        copy.start()
    for copy in copies:
        copy.wait()


def per_device(queries, keys, values, doc_lengths):
    rows, all_heads = queries.shape
    half_heads = all_heads // 2
    head_rows = (all_heads // HD) * rows
    half, span = lax.axis_index("head"), lax.axis_index("ctx")
    cores = lax.axis_size("head")
    place_in_group = lax.rem(span, REACH)

    nowhere = -2 * REACH

    def origin(kind):
        if kind == SHIFT:
            return span - REACH
        late = place_in_group >= REACH // 2
        from_place = place_in_group ^ (OPPOSITE if kind == SHIFT_OPPOSITE else kind)
        here = span - place_in_group + from_place
        if kind == SHIFT_OPPOSITE:
            return jnp.where(late, nowhere, here - REACH)
        if kind == OPPOSITE:
            return jnp.where(late, here, nowhere)
        return here - jnp.where(from_place > place_in_group, REACH, 0)

    parts = [(span * cores + half) * rows, (span * cores + 1 - half) * rows, half]
    for number, kinds in enumerate(ROUNDS):
        start = jnp.where(half == 0, origin(kinds[0]), origin(kinds[1]))
        if number in (EARLY, LATE):
            start = jnp.where(takes_part(number, half, place_in_group), start, nowhere)
        parts += [(start * cores + half) * rows, (start * cores + 1 - half) * rows]
    place = jnp.stack(parts).astype(jnp.int32)

    vmem = pl.BlockSpec(memory_space=pltpu.VMEM)
    smem = pl.BlockSpec(memory_space=pltpu.SMEM)
    anywhere = pl.BlockSpec(memory_space=pl.ANY)
    hbm = pl.BlockSpec(memory_space=pltpu.MemorySpace.HBM)
    placed_shape = jax.ShapeDtypeStruct((head_rows, HD), queries.dtype)
    max_shape = jax.ShapeDtypeStruct((head_rows, HD), jnp.float32)
    acc_shape = jax.ShapeDtypeStruct((head_rows, 2 * HD), jnp.float32)
    side_shape = jax.ShapeDtypeStruct((rows, half_heads), queries.dtype)
    common = dict(
        compiler_params=pltpu.CompilerParams(vmem_limit_bytes=24 * 1024 * 1024),
        cost_estimate=pl.CostEstimate(flops=0, bytes_accessed=0, transcendentals=0),
    )

    def heads_of(array, core):
        width = array.shape[1] // 2
        return lax.dynamic_slice_in_dim(array, core * width, width, 1)

    to_give = jnp.stack([heads_of(keys, 1 - half), heads_of(values, 1 - half)])
    given = to_other_core(to_give)
    given, queries = lax.optimization_barrier((given, queries))
    own = jnp.stack([jnp.stack([heads_of(keys, half), heads_of(values, half)]), given])
    arrived = [send_round(own, number) for number in range(2)]
    q_far = to_other_core(
        pl.pallas_call(
            pick_kernel,
            in_specs=[smem, hbm],
            out_specs=vmem,
            out_shape=side_shape,
            scratch_shapes=[pltpu.SemaphoreType.DMA],
            name="pick_queries",
            **common,
        )(place, queries)
    )

    chunk_heads = queries.shape[1] // keys.shape[1] // PARTS
    ahead = pltpu.VMEM((chunk_heads * rows, 4 * rows), jnp.float32)
    state_shapes = (placed_shape, max_shape, acc_shape)
    lows_shape = jax.ShapeDtypeStruct((2, rows, rows), jnp.int32)
    info_shape = jax.ShapeDtypeStruct((BOUNDS + 4,), jnp.int32)
    *state, lows, info = pl.pallas_call(
        functools.partial(own_kernel, side=0),
        in_specs=[smem, smem, hbm, vmem],
        out_specs=(vmem, vmem, vmem, vmem, smem),
        out_shape=state_shapes + (lows_shape, info_shape),
        scratch_shapes=[ahead, pltpu.VMEM((rows, half_heads), queries.dtype), pltpu.SemaphoreType.DMA],
        name="attend_own_near",
        **{**common, "cost_estimate": pl.CostEstimate(flops=10**11, bytes_accessed=0, transcendentals=0)},
    )(place, doc_lengths, queries, own)
    placed, row_max, acc = pl.pallas_call(
        functools.partial(own_kernel, side=1),
        in_specs=[smem] + [vmem] * 6,
        out_specs=(vmem, vmem, vmem),
        out_shape=state_shapes,
        input_output_aliases={3: 0, 4: 1, 5: 2},
        scratch_shapes=[ahead],
        name="attend_own_far",
        **common,
    )(info, q_far, own, *state, lows)

    def attend(kv, row_max, acc, number):
        return pl.pallas_call(
            functools.partial(span_kernel, numbers=tuple(range(number, number + len(kv)))),
            in_specs=[smem] + [vmem] * (len(kv) + 4),
            out_specs=(vmem, vmem),
            out_shape=(max_shape, acc_shape),
            input_output_aliases={len(kv) + 3: 0, len(kv) + 4: 1},
            scratch_shapes=[ahead],
            name="attend_spans",
            **common,
        )(info, lows, *kv, placed, row_max, acc)

    behind, acc = lax.optimization_barrier((arrived[0], acc))
    opposite, acc = lax.optimization_barrier((arrived[1], acc))

    def plane_round(number):
        sends = [jnp.where((place_in_group ^ kind) > place_in_group, own, behind) for kind in ROUNDS[number]]
        return jnp.where(half == 0, *sends)

    first = send_round(plane_round(2), 2)
    relayed = send_round(opposite, 3)
    row_max, acc = attend([behind, opposite], row_max, acc, 0)
    to_second, acc = lax.optimization_barrier((plane_round(EARLY), acc))
    second = send_round(to_second, EARLY)
    to_third, first, acc = lax.optimization_barrier((to_second, first, acc))
    third = send_round(to_third, LATE)
    row_max, acc = attend([first], row_max, acc, 2)

    last_args = (info, lows, relayed, second, third, placed, row_max, acc)
    def finish(side, name):
        return pl.pallas_call(
            functools.partial(last_kernel, numbers=(3, EARLY, LATE), side=side),
            in_specs=[smem] + [vmem] * 7,
            out_specs=vmem,
            out_shape=side_shape,
            scratch_shapes=[ahead],
            name=name,
            **common,
        )(*last_args)

    out_far = to_other_core(finish(1, "attend_last_far"))
    return pl.pallas_call(
        join_kernel,
        in_specs=[smem, vmem, vmem],
        out_specs=anywhere,
        out_shape=jax.ShapeDtypeStruct(queries.shape, queries.dtype),
        scratch_shapes=[pltpu.SemaphoreType.DMA((2, 4))],
        name="join_heads",
        **common,
    )(info, finish(0, "attend_last_near"), out_far)


def solution(mesh):
    placed = P(AXES, None)
    return jax.shard_map(
        per_device, mesh=mesh, in_specs=(placed, placed, placed, P()), out_specs=placed, check_vma=False
    )
```

```python
import functools
import math

import jax
import jax.numpy as jnp
from jax import lax
from jax.experimental import pallas as pl
from jax.experimental.pallas import tpu as pltpu
from jax.sharding import PartitionSpec as P

HD = 128
REACH = 4
NEVER = -1e30
SCORE_SCALE = HD ** (-0.5) * math.log2(math.e)
PARTS = 2
AXES = ("ctx", "head")
SHIFT, SHIFT_OPPOSITE, OPPOSITE = "shift", "shift opposite", REACH - 1
ROUNDS = ((SHIFT, SHIFT), (OPPOSITE, OPPOSITE), (1, 2), (SHIFT_OPPOSITE, SHIFT_OPPOSITE), (2, 1))
BOUNDS = 3 + 2 * len(ROUNDS)


def send_round(block, kinds):
    spans, cores = lax.axis_size("ctx"), lax.axis_size("head")
    pairs = []
    for s in range(spans):
        for core, kind in enumerate(kinds):
            if kind in (SHIFT, SHIFT_OPPOSITE):
                target = s + REACH
                if target >= spans or (kind == SHIFT_OPPOSITE and s % REACH >= REACH // 2):
                    continue
            else:
                target = s ^ kind
            pairs.append((s * cores + core, target * cores + core))
    return lax.ppermute(block, AXES, pairs)


def to_other_core(block):
    cores = lax.axis_size("head")
    return lax.ppermute(block, "head", [(h, cores - 1 - h) for h in range(cores)])


def doc_starts(lengths_ref, first, last):
    def one_doc(i, carry):
        start, lo_first, lo_last = carry
        start = start + lengths_ref[i]
        return start, jnp.where(start <= first, start, lo_first), jnp.where(start <= last, start, lo_last)

    zero = jnp.int32(0)
    _, lo_first, lo_last = lax.fori_loop(0, lengths_ref.shape[0], one_doc, (zero, zero, zero))
    return lo_first, lo_last


def doc_start_rows(lengths_ref, first_query, rows):
    pos = first_query + lax.broadcasted_iota(jnp.int32, (rows, rows), 0)

    def one_doc(i, carry):
        start, lo = carry
        start = start + lengths_ref[i]
        return start, jnp.where(start <= pos, start, lo)

    zero = jnp.zeros((rows, rows), jnp.int32)
    return lax.fori_loop(0, lengths_ref.shape[0], one_doc, (jnp.int32(0), zero))[1]


def block_of(at, size):
    return pl.ds(pl.multiple_of(at * size, size), size)


def positions(start, rows):
    return start + lax.broadcasted_iota(jnp.int32, (rows, rows), 1)


def softmax_step(scores, allowed, max_before):
    if allowed is not None:
        allowed = jnp.concatenate([allowed] * (scores.shape[0] // allowed.shape[0]), axis=0)
        scores = jnp.where(allowed, scores, NEVER)
    row_max = jnp.broadcast_to(jnp.max(scores, axis=1, keepdims=True), (scores.shape[0], HD))
    rescale = None
    if max_before is not None:
        row_max = jnp.maximum(max_before, row_max)
        rescale = jnp.exp2((max_before - row_max) * SCORE_SCALE)
    shift = jnp.concatenate([row_max] * (scores.shape[1] // HD), axis=1)
    weights = jnp.exp2((scores - shift) * SCORE_SCALE)
    sums = weights[:, :HD]
    for begin in range(HD, scores.shape[1], HD):
        sums = sums + weights[:, begin : begin + HD]
    return weights.astype(jnp.bfloat16), sums, row_max, rescale


def scores_for(queries, keys):
    return lax.dot_general(queries, keys, (((1,), (1,)), ((), ())), preferred_element_type=jnp.float32)


def pipeline(kv_heads, ahead_ref, allowed, scores_of, values_of, before_of, store):
    def finish(g, part, scores):
        max_before, acc_before = before_of(g, part)
        weights, sums, row_max, rescale = softmax_step(scores, allowed, max_before)
        acc = jnp.dot(weights, values_of(g), preferred_element_type=jnp.float32)
        if rescale is not None:
            acc = acc_before[:, :HD] * rescale + acc
            sums = acc_before[:, HD:] * rescale + sums
        store(g, part, row_max, jnp.concatenate([acc, sums], axis=1))

    ahead_ref[...] = scores_of(0, 0)

    def one_head(g, _):
        scores = ahead_ref[...]
        for part in range(PARTS):
            if part + 1 < PARTS:
                later = scores_of(g, part + 1)
            else:
                later = scores_of(jnp.minimum(g + 1, kv_heads - 1), 0)
            finish(g, part, scores)
            scores = later
        ahead_ref[...] = scores
        return 0

    lax.fori_loop(0, kv_heads, one_head, 0)


def pick_kernel(place_ref, q_ref, out_ref, sem):
    copy = pltpu.make_async_copy(q_ref.at[:, block_of(1 - place_ref[2], out_ref.shape[1])], out_ref, sem)
    copy.start()
    copy.wait()


def own_kernel(place_ref, *refs, side):
    if side == 0:
        lengths_ref, q_ref, kv_ref, *refs = refs
        queries_ref, max_ref, acc_ref, lows_ref, info_ref, ahead_ref, q_side_ref, sem = refs
        fetch = pltpu.make_async_copy(q_ref.at[:, block_of(place_ref[2], q_side_ref.shape[1])], q_side_ref, sem)
        fetch.start()
    else:
        q_ref, kv_ref, _, _, _, lows_ref, queries_ref, max_ref, acc_ref, ahead_ref = refs
        q_side_ref = q_ref
    rows, wide = q_side_ref.shape
    kv_heads = kv_ref.shape[3] // HD
    heads = wide // (kv_heads * PARTS * HD)
    half = place_ref[2]
    first, other = place_ref[side], place_ref[1 - side]
    query_pos = first + lax.broadcasted_iota(jnp.int32, (rows, rows), 0)
    if side == 0:
        for i in range(2):
            lows_ref[i] = doc_start_rows(lengths_ref, place_ref[i], rows)
            low, high = doc_starts(lengths_ref, place_ref[i], place_ref[i] + rows - 1)
            info_ref[BOUNDS + 2 * i], info_ref[BOUNDS + 2 * i + 1] = low, high
        for i in range(BOUNDS):
            info_ref[i] = place_ref[i]
    lows = lows_ref[side]
    key_pos = positions(first, rows)
    diagonal = (key_pos >= lows) & (key_pos <= query_pos)
    earlier = positions(other, rows) >= lows
    if side == 0:
        fetch.wait()

    def at(g, part):
        return block_of((side * kv_heads + g) * PARTS + part, heads * rows)

    def place_queries(i, _):
        q = q_side_ref[:, block_of(i, heads * HD)]
        queries_ref[block_of(side * kv_heads * PARTS + i, heads * rows), :] = jnp.concatenate(
            [q[:, h * HD : (h + 1) * HD] for h in range(heads)], axis=0
        )
        return 0

    lax.fori_loop(0, kv_heads * PARTS, place_queries, 0)

    def store(g, part, row_max, acc):
        max_ref[at(g, part), :] = row_max
        acc_ref[at(g, part), :] = acc

    def work(blocks, allowed):
        def of(i, g):
            return jnp.concatenate([kv_ref[block, i, :, block_of(g, HD)] for block in blocks], axis=0)

        pipeline(
            kv_heads,
            ahead_ref.at[:, : len(blocks) * rows],
            allowed,
            lambda g, part: scores_for(queries_ref[at(g, part), :], of(0, g)),
            lambda g: of(1, g),
            lambda g, part: (None, None),
            store,
        )

    pl.when(half == side)(lambda: work([side], diagonal))
    pl.when(half != side)(lambda: work([1 - side, side], jnp.concatenate([earlier, diagonal], axis=1)))


def span_steps(place_ref, lows_ref, kv_refs, queries_ref, ahead_ref, numbers, side, load, store):
    rows = kv_refs[0].shape[2]
    kv_heads = kv_refs[0].shape[3] // HD
    key_starts = [(place_ref[3 + 2 * number], place_ref[4 + 2 * number]) for number in numbers]
    lo_first, lo_last = place_ref[BOUNDS + 2 * side], place_ref[BOUNDS + 2 * side + 1]
    needed = [jnp.maximum(*starts) + rows > lo_first for starts in key_starts]

    def at(g, part):
        return block_of((side * kv_heads + g) * PARTS + part, ahead_ref.shape[0])

    def work(chosen, masked):
        def of(i, g):
            parts = [kv_refs[n][block, i, :, block_of(g, HD)] for n in chosen for block in range(2)]
            return jnp.concatenate(parts, axis=0)

        allowed = None
        if masked:
            lows = lows_ref[side]
            allowed = jnp.concatenate(
                [positions(start, rows) >= lows for n in chosen for start in key_starts[n]], axis=1
            )
        pipeline(
            kv_heads,
            ahead_ref.at[:, : 2 * rows * len(chosen)],
            allowed,
            lambda g, part: scores_for(queries_ref[at(g, part), :], of(0, g)),
            lambda g: of(1, g),
            lambda g, part: load(at(g, part)),
            lambda g, part, row_max, acc: store(g, part, at(g, part), row_max, acc),
        )

    if len(numbers) == 1:
        whole = jnp.minimum(*key_starts[0]) >= lo_last
        pl.when(whole)(lambda: work([0], False))
        pl.when(needed[0] & jnp.logical_not(whole))(lambda: work([0], True))
        return needed[0]
    pl.when(needed[0] & needed[1])(lambda: work([0, 1], True))
    pl.when(needed[0] & jnp.logical_not(needed[1]))(lambda: work([0], True))
    pl.when(needed[1] & jnp.logical_not(needed[0]))(lambda: work([1], True))
    return needed[0] | needed[1]


def span_kernel(place_ref, lows_ref, *refs, numbers):
    kv_refs, (queries_ref, _, _, max_ref, acc_ref, ahead_ref) = refs[: len(numbers)], refs[len(numbers) :]

    def load(at):
        return max_ref[at, :], acc_ref[at, :]

    def store(g, part, at, row_max, acc):
        max_ref[at, :] = row_max
        acc_ref[at, :] = acc

    def one_side(side, _):
        span_steps(place_ref, lows_ref, kv_refs, queries_ref, ahead_ref, numbers, side, load, store)
        return 0

    lax.fori_loop(0, 2, one_side, 0)


def last_kernel(place_ref, lows_ref, *refs, numbers, side):
    kv_refs, (queries_ref, max_ref, acc_ref, out_ref, ahead_ref) = refs[: len(numbers)], refs[len(numbers) :]
    rows = kv_refs[0].shape[2]
    kv_heads = kv_refs[0].shape[3] // HD
    chunk = ahead_ref.shape[0]
    heads = chunk // rows

    def load(at):
        return max_ref[at, :], acc_ref[at, :]

    def finish(g, part, at, row_max, acc):
        total = jnp.sum(acc[:, HD:], axis=1, keepdims=True)
        finished = (acc[:, :HD] * (1.0 / total)).astype(out_ref.dtype)
        out_ref[:, block_of(g * PARTS + part, heads * HD)] = jnp.concatenate(
            [finished[h * rows : (h + 1) * rows] for h in range(heads)], axis=1
        )

    needed = span_steps(place_ref, lows_ref, kv_refs, queries_ref, ahead_ref, numbers, side, load, finish)

    @pl.when(jnp.logical_not(needed))
    def _():
        def one_head(g, _):
            for part in range(PARTS):
                finish(g, part, None, *load(block_of((side * kv_heads + g) * PARTS + part, chunk)))
            return 0

        lax.fori_loop(0, kv_heads, one_head, 0)


def join_kernel(place_ref, near_ref, far_ref, out_ref, sems):
    pieces = sems.shape[1]
    rows = far_ref.shape[0] // pieces
    copies = []
    for side, source in enumerate((near_ref, far_ref)):
        columns = block_of(place_ref[2] if side == 0 else 1 - place_ref[2], source.shape[1])
        for i in range(pieces):
            here = pl.ds(i * rows, rows)
            copies.append(pltpu.make_async_copy(source.at[here, :], out_ref.at[here, columns], sems.at[side, i]))
    for copy in copies:
        copy.start()
    for copy in copies:
        copy.wait()


def per_device(queries, keys, values, doc_lengths):
    rows, all_heads = queries.shape
    half_heads = all_heads // 2
    head_rows = (all_heads // HD) * rows
    half, span = lax.axis_index("head"), lax.axis_index("ctx")
    cores = lax.axis_size("head")
    place_in_group = lax.rem(span, REACH)

    nowhere = -2 * REACH

    def origin(kind):
        if kind == SHIFT:
            return span - REACH
        late = place_in_group >= REACH // 2
        from_place = place_in_group ^ (OPPOSITE if kind == SHIFT_OPPOSITE else kind)
        here = span - place_in_group + from_place
        if kind == SHIFT_OPPOSITE:
            return jnp.where(late, nowhere, here - REACH)
        if kind == OPPOSITE:
            return jnp.where(late, here, nowhere)
        return here - jnp.where(from_place > place_in_group, REACH, 0)

    parts = [(span * cores + half) * rows, (span * cores + 1 - half) * rows, half]
    for kinds in ROUNDS:
        start = jnp.where(half == 0, origin(kinds[0]), origin(kinds[1]))
        parts += [(start * cores + half) * rows, (start * cores + 1 - half) * rows]
    place = jnp.stack(parts).astype(jnp.int32)

    vmem = pl.BlockSpec(memory_space=pltpu.VMEM)
    smem = pl.BlockSpec(memory_space=pltpu.SMEM)
    anywhere = pl.BlockSpec(memory_space=pl.ANY)
    hbm = pl.BlockSpec(memory_space=pltpu.MemorySpace.HBM)
    placed_shape = jax.ShapeDtypeStruct((head_rows, HD), queries.dtype)
    max_shape = jax.ShapeDtypeStruct((head_rows, HD), jnp.float32)
    acc_shape = jax.ShapeDtypeStruct((head_rows, 2 * HD), jnp.float32)
    side_shape = jax.ShapeDtypeStruct((rows, half_heads), queries.dtype)
    common = dict(
        compiler_params=pltpu.CompilerParams(vmem_limit_bytes=24 * 1024 * 1024),
        cost_estimate=pl.CostEstimate(flops=0, bytes_accessed=0, transcendentals=0),
    )

    def heads_of(array, core):
        width = array.shape[1] // 2
        return lax.dynamic_slice_in_dim(array, core * width, width, 1)

    to_give = jnp.stack([heads_of(keys, 1 - half), heads_of(values, 1 - half)])
    given = to_other_core(to_give)
    given, queries = lax.optimization_barrier((given, queries))
    own = jnp.stack([jnp.stack([heads_of(keys, half), heads_of(values, half)]), given])
    arrived = [send_round(own, kinds) for kinds in ROUNDS[:2]]
    q_far = to_other_core(
        pl.pallas_call(
            pick_kernel,
            in_specs=[smem, hbm],
            out_specs=vmem,
            out_shape=side_shape,
            scratch_shapes=[pltpu.SemaphoreType.DMA],
            name="pick_queries",
            **common,
        )(place, queries)
    )

    chunk_heads = queries.shape[1] // keys.shape[1] // PARTS
    ahead = pltpu.VMEM((chunk_heads * rows, 4 * rows), jnp.float32)
    state_shapes = (placed_shape, max_shape, acc_shape)
    lows_shape = jax.ShapeDtypeStruct((2, rows, rows), jnp.int32)
    info_shape = jax.ShapeDtypeStruct((BOUNDS + 4,), jnp.int32)
    *state, lows, info = pl.pallas_call(
        functools.partial(own_kernel, side=0),
        in_specs=[smem, smem, hbm, vmem],
        out_specs=(vmem, vmem, vmem, vmem, smem),
        out_shape=state_shapes + (lows_shape, info_shape),
        scratch_shapes=[ahead, pltpu.VMEM((rows, half_heads), queries.dtype), pltpu.SemaphoreType.DMA],
        name="attend_own_near",
        **{**common, "cost_estimate": pl.CostEstimate(flops=10**11, bytes_accessed=0, transcendentals=0)},
    )(place, doc_lengths, queries, own)
    placed, row_max, acc = pl.pallas_call(
        functools.partial(own_kernel, side=1),
        in_specs=[smem] + [vmem] * 6,
        out_specs=(vmem, vmem, vmem),
        out_shape=state_shapes,
        input_output_aliases={3: 0, 4: 1, 5: 2},
        scratch_shapes=[ahead],
        name="attend_own_far",
        **common,
    )(info, q_far, own, *state, lows)

    def attend(kv, row_max, acc, number):
        return pl.pallas_call(
            functools.partial(span_kernel, numbers=tuple(range(number, number + len(kv)))),
            in_specs=[smem] + [vmem] * (len(kv) + 4),
            out_specs=(vmem, vmem),
            out_shape=(max_shape, acc_shape),
            input_output_aliases={len(kv) + 3: 0, len(kv) + 4: 1},
            scratch_shapes=[ahead],
            name="attend_spans",
            **common,
        )(info, lows, *kv, placed, row_max, acc)

    behind, acc = lax.optimization_barrier((arrived[0], acc))
    opposite, acc = lax.optimization_barrier((arrived[1], acc))

    def plane_round(number):
        sends = [jnp.where((place_in_group ^ kind) > place_in_group, own, behind) for kind in ROUNDS[number]]
        return jnp.where(half == 0, *sends)

    first = send_round(plane_round(2), ROUNDS[2])
    relayed = send_round(opposite, ROUNDS[3])
    row_max, acc = attend([behind, opposite], row_max, acc, 0)
    to_second, first, acc = lax.optimization_barrier((plane_round(4), first, acc))
    second = send_round(to_second, ROUNDS[4])
    row_max, acc = attend([first], row_max, acc, 2)

    last_args = (info, lows, relayed, second, placed, row_max, acc)
    def finish(side, name):
        return pl.pallas_call(
            functools.partial(last_kernel, numbers=(3, 4), side=side),
            in_specs=[smem] + [vmem] * 6,
            out_specs=vmem,
            out_shape=side_shape,
            scratch_shapes=[ahead],
            name=name,
            **common,
        )(*last_args)

    out_far = to_other_core(finish(1, "attend_last_far"))
    return pl.pallas_call(
        join_kernel,
        in_specs=[smem, vmem, vmem],
        out_specs=anywhere,
        out_shape=jax.ShapeDtypeStruct(queries.shape, queries.dtype),
        scratch_shapes=[pltpu.SemaphoreType.DMA((2, 4))],
        name="join_heads",
        **common,
    )(info, finish(0, "attend_last_near"), out_far)


def solution(mesh):
    placed = P(AXES, None)
    return jax.shard_map(
        per_device, mesh=mesh, in_specs=(placed, placed, placed, P()), out_specs=placed, check_vma=False
    )
```

```python
import functools
import math

import jax
import jax.numpy as jnp
from jax import lax
from jax.experimental import pallas as pl
from jax.experimental.pallas import tpu as pltpu
from jax.sharding import PartitionSpec as P

HD = 128
REACH = 4
NEVER = -1e30
SCORE_SCALE = HD ** (-0.5) * math.log2(math.e)
PARTS = 2
AXES = ("ctx", "head")
SHIFT, SHIFT_OPPOSITE, OPPOSITE = "shift", "shift opposite", REACH - 1
ROUNDS = ((SHIFT, SHIFT), (OPPOSITE, OPPOSITE), (2, 1), (SHIFT_OPPOSITE, SHIFT_OPPOSITE), (1, 2))
BOUNDS = 3 + 2 * len(ROUNDS)


def send_round(block, kinds):
    spans, cores = lax.axis_size("ctx"), lax.axis_size("head")
    pairs = []
    for s in range(spans):
        for core, kind in enumerate(kinds):
            if kind in (SHIFT, SHIFT_OPPOSITE):
                target = s + REACH
                if target >= spans or (kind == SHIFT_OPPOSITE and s % REACH >= REACH // 2):
                    continue
            else:
                target = s ^ kind
            pairs.append((s * cores + core, target * cores + core))
    return lax.ppermute(block, AXES, pairs)


def to_other_core(block):
    cores = lax.axis_size("head")
    return lax.ppermute(block, "head", [(h, cores - 1 - h) for h in range(cores)])


def doc_starts(lengths_ref, first, last):
    def one_doc(i, carry):
        start, lo_first, lo_last = carry
        start = start + lengths_ref[i]
        return start, jnp.where(start <= first, start, lo_first), jnp.where(start <= last, start, lo_last)

    zero = jnp.int32(0)
    _, lo_first, lo_last = lax.fori_loop(0, lengths_ref.shape[0], one_doc, (zero, zero, zero))
    return lo_first, lo_last


def doc_start_rows(lengths_ref, first_query, rows):
    pos = first_query + lax.broadcasted_iota(jnp.int32, (rows, rows), 0)

    def one_doc(i, carry):
        start, lo = carry
        start = start + lengths_ref[i]
        return start, jnp.where(start <= pos, start, lo)

    zero = jnp.zeros((rows, rows), jnp.int32)
    return lax.fori_loop(0, lengths_ref.shape[0], one_doc, (jnp.int32(0), zero))[1]


def block_of(at, size):
    return pl.ds(pl.multiple_of(at * size, size), size)


def positions(start, rows):
    return start + lax.broadcasted_iota(jnp.int32, (rows, rows), 1)


def softmax_step(scores, allowed, max_before):
    if allowed is not None:
        allowed = jnp.concatenate([allowed] * (scores.shape[0] // allowed.shape[0]), axis=0)
        scores = jnp.where(allowed, scores, NEVER)
    row_max = jnp.broadcast_to(jnp.max(scores, axis=1, keepdims=True), (scores.shape[0], HD))
    rescale = None
    if max_before is not None:
        row_max = jnp.maximum(max_before, row_max)
        rescale = jnp.exp2((max_before - row_max) * SCORE_SCALE)
    shift = jnp.concatenate([row_max] * (scores.shape[1] // HD), axis=1)
    return jnp.exp2((scores - shift) * SCORE_SCALE).astype(jnp.bfloat16), row_max, rescale


def scores_for(queries, keys):
    return lax.dot_general(queries, keys, (((1,), (1,)), ((), ())), preferred_element_type=jnp.float32)


def pipeline(kv_heads, ahead_ref, allowed, scores_of, values_of, before_of, store):
    def finish(g, part, scores):
        max_before, acc_before = before_of(g, part)
        weights, row_max, rescale = softmax_step(scores, allowed, max_before)
        values = values_of(g)
        widened = jnp.concatenate([values, jnp.ones_like(values)], axis=1)
        acc = jnp.dot(weights, widened, preferred_element_type=jnp.float32)
        if rescale is not None:
            acc = acc_before * jnp.concatenate([rescale] * 2, axis=1) + acc
        store(g, part, row_max, acc)

    ahead_ref[...] = scores_of(0, 0)

    def one_head(g, _):
        scores = ahead_ref[...]
        for part in range(PARTS):
            if part + 1 < PARTS:
                later = scores_of(g, part + 1)
            else:
                later = scores_of(jnp.minimum(g + 1, kv_heads - 1), 0)
            finish(g, part, scores)
            scores = later
        ahead_ref[...] = scores
        return 0

    lax.fori_loop(0, kv_heads, one_head, 0)


def pick_kernel(place_ref, q_ref, out_ref, sem):
    copy = pltpu.make_async_copy(q_ref.at[:, block_of(1 - place_ref[2], out_ref.shape[1])], out_ref, sem)
    copy.start()
    copy.wait()


def own_kernel(place_ref, *refs, side):
    if side == 0:
        lengths_ref, q_ref, kv_ref, *refs = refs
        queries_ref, max_ref, acc_ref, lows_ref, info_ref, ahead_ref, q_side_ref, sem = refs
        fetch = pltpu.make_async_copy(q_ref.at[:, block_of(place_ref[2], q_side_ref.shape[1])], q_side_ref, sem)
        fetch.start()
    else:
        q_ref, kv_ref, _, _, _, lows_ref, queries_ref, max_ref, acc_ref, ahead_ref = refs
        q_side_ref = q_ref
    rows, wide = q_side_ref.shape
    kv_heads = kv_ref.shape[3] // HD
    heads = wide // (kv_heads * PARTS * HD)
    half = place_ref[2]
    first, other = place_ref[side], place_ref[1 - side]
    query_pos = first + lax.broadcasted_iota(jnp.int32, (rows, rows), 0)
    if side == 0:
        for i in range(2):
            lows_ref[i] = doc_start_rows(lengths_ref, place_ref[i], rows)
            low, high = doc_starts(lengths_ref, place_ref[i], place_ref[i] + rows - 1)
            info_ref[BOUNDS + 2 * i], info_ref[BOUNDS + 2 * i + 1] = low, high
        for i in range(BOUNDS):
            info_ref[i] = place_ref[i]
    lows = lows_ref[side]
    key_pos = positions(first, rows)
    diagonal = (key_pos >= lows) & (key_pos <= query_pos)
    earlier = positions(other, rows) >= lows
    if side == 0:
        fetch.wait()

    def at(g, part):
        return block_of((side * kv_heads + g) * PARTS + part, heads * rows)

    def place_queries(i, _):
        q = q_side_ref[:, block_of(i, heads * HD)]
        queries_ref[block_of(side * kv_heads * PARTS + i, heads * rows), :] = jnp.concatenate(
            [q[:, h * HD : (h + 1) * HD] for h in range(heads)], axis=0
        )
        return 0

    lax.fori_loop(0, kv_heads * PARTS, place_queries, 0)

    def store(g, part, row_max, acc):
        max_ref[at(g, part), :] = row_max
        acc_ref[at(g, part), :] = acc

    def work(blocks, allowed):
        def of(i, g):
            return jnp.concatenate([kv_ref[block, i, :, block_of(g, HD)] for block in blocks], axis=0)

        pipeline(
            kv_heads,
            ahead_ref.at[:, : len(blocks) * rows],
            allowed,
            lambda g, part: scores_for(queries_ref[at(g, part), :], of(0, g)),
            lambda g: of(1, g),
            lambda g, part: (None, None),
            store,
        )

    pl.when(half == side)(lambda: work([side], diagonal))
    pl.when(half != side)(lambda: work([1 - side, side], jnp.concatenate([earlier, diagonal], axis=1)))


def span_steps(place_ref, lows_ref, kv_refs, queries_ref, ahead_ref, numbers, side, load, store):
    rows = kv_refs[0].shape[2]
    kv_heads = kv_refs[0].shape[3] // HD
    key_starts = [(place_ref[3 + 2 * number], place_ref[4 + 2 * number]) for number in numbers]
    lo_first, lo_last = place_ref[BOUNDS + 2 * side], place_ref[BOUNDS + 2 * side + 1]
    needed = [jnp.maximum(*starts) + rows > lo_first for starts in key_starts]

    def at(g, part):
        return block_of((side * kv_heads + g) * PARTS + part, ahead_ref.shape[0])

    def work(chosen, masked):
        def of(i, g):
            parts = [kv_refs[n][block, i, :, block_of(g, HD)] for n in chosen for block in range(2)]
            return jnp.concatenate(parts, axis=0)

        allowed = None
        if masked:
            lows = lows_ref[side]
            allowed = jnp.concatenate(
                [positions(start, rows) >= lows for n in chosen for start in key_starts[n]], axis=1
            )
        pipeline(
            kv_heads,
            ahead_ref.at[:, : 2 * rows * len(chosen)],
            allowed,
            lambda g, part: scores_for(queries_ref[at(g, part), :], of(0, g)),
            lambda g: of(1, g),
            lambda g, part: load(at(g, part)),
            lambda g, part, row_max, acc: store(g, part, at(g, part), row_max, acc),
        )

    if len(numbers) == 1:
        whole = jnp.minimum(*key_starts[0]) >= lo_last
        pl.when(whole)(lambda: work([0], False))
        pl.when(needed[0] & jnp.logical_not(whole))(lambda: work([0], True))
        return needed[0]
    pl.when(needed[0] & needed[1])(lambda: work([0, 1], True))
    pl.when(needed[0] & jnp.logical_not(needed[1]))(lambda: work([0], True))
    pl.when(needed[1] & jnp.logical_not(needed[0]))(lambda: work([1], True))
    return needed[0] | needed[1]


def span_kernel(place_ref, lows_ref, *refs, numbers):
    kv_refs, (queries_ref, _, _, max_ref, acc_ref, ahead_ref) = refs[: len(numbers)], refs[len(numbers) :]

    def load(at):
        return max_ref[at, :], acc_ref[at, :]

    def store(g, part, at, row_max, acc):
        max_ref[at, :] = row_max
        acc_ref[at, :] = acc

    def one_side(side, _):
        span_steps(place_ref, lows_ref, kv_refs, queries_ref, ahead_ref, numbers, side, load, store)
        return 0

    lax.fori_loop(0, 2, one_side, 0)


def last_kernel(place_ref, lows_ref, *refs, numbers, side):
    kv_refs, (queries_ref, max_ref, acc_ref, out_ref, ahead_ref) = refs[: len(numbers)], refs[len(numbers) :]
    rows = kv_refs[0].shape[2]
    kv_heads = kv_refs[0].shape[3] // HD
    chunk = ahead_ref.shape[0]
    heads = chunk // rows

    def load(at):
        return max_ref[at, :], acc_ref[at, :]

    def finish(g, part, at, row_max, acc):
        finished = (acc[:, :HD] * (1.0 / acc[:, HD:])).astype(out_ref.dtype)
        out_ref[:, block_of(g * PARTS + part, heads * HD)] = jnp.concatenate(
            [finished[h * rows : (h + 1) * rows] for h in range(heads)], axis=1
        )

    needed = span_steps(place_ref, lows_ref, kv_refs, queries_ref, ahead_ref, numbers, side, load, finish)

    @pl.when(jnp.logical_not(needed))
    def _():
        def one_head(g, _):
            for part in range(PARTS):
                finish(g, part, None, *load(block_of((side * kv_heads + g) * PARTS + part, chunk)))
            return 0

        lax.fori_loop(0, kv_heads, one_head, 0)


def join_kernel(place_ref, near_ref, far_ref, out_ref, sems):
    pieces = sems.shape[1]
    rows = far_ref.shape[0] // pieces
    copies = []
    for side, source in enumerate((near_ref, far_ref)):
        columns = block_of(place_ref[2] if side == 0 else 1 - place_ref[2], source.shape[1])
        for i in range(pieces):
            here = pl.ds(i * rows, rows)
            copies.append(pltpu.make_async_copy(source.at[here, :], out_ref.at[here, columns], sems.at[side, i]))
    for copy in copies:
        copy.start()
    for copy in copies:
        copy.wait()


def per_device(queries, keys, values, doc_lengths):
    rows, all_heads = queries.shape
    half_heads = all_heads // 2
    head_rows = (all_heads // HD) * rows
    half, span = lax.axis_index("head"), lax.axis_index("ctx")
    cores = lax.axis_size("head")
    place_in_group = lax.rem(span, REACH)

    nowhere = -2 * REACH

    def origin(kind):
        if kind == SHIFT:
            return span - REACH
        late = place_in_group >= REACH // 2
        from_place = place_in_group ^ (OPPOSITE if kind == SHIFT_OPPOSITE else kind)
        here = span - place_in_group + from_place
        if kind == SHIFT_OPPOSITE:
            return jnp.where(late, nowhere, here - REACH)
        if kind == OPPOSITE:
            return jnp.where(late, here, nowhere)
        return here - jnp.where(from_place > place_in_group, REACH, 0)

    parts = [(span * cores + half) * rows, (span * cores + 1 - half) * rows, half]
    for kinds in ROUNDS:
        start = jnp.where(half == 0, origin(kinds[0]), origin(kinds[1]))
        parts += [(start * cores + half) * rows, (start * cores + 1 - half) * rows]
    place = jnp.stack(parts).astype(jnp.int32)

    vmem = pl.BlockSpec(memory_space=pltpu.VMEM)
    smem = pl.BlockSpec(memory_space=pltpu.SMEM)
    anywhere = pl.BlockSpec(memory_space=pl.ANY)
    hbm = pl.BlockSpec(memory_space=pltpu.MemorySpace.HBM)
    placed_shape = jax.ShapeDtypeStruct((head_rows, HD), queries.dtype)
    max_shape = jax.ShapeDtypeStruct((head_rows, HD), jnp.float32)
    acc_shape = jax.ShapeDtypeStruct((head_rows, 2 * HD), jnp.float32)
    side_shape = jax.ShapeDtypeStruct((rows, half_heads), queries.dtype)
    common = dict(
        compiler_params=pltpu.CompilerParams(vmem_limit_bytes=24 * 1024 * 1024),
        cost_estimate=pl.CostEstimate(flops=0, bytes_accessed=0, transcendentals=0),
    )

    def heads_of(array, core):
        width = array.shape[1] // 2
        return lax.dynamic_slice_in_dim(array, core * width, width, 1)

    to_give = jnp.stack([heads_of(keys, 1 - half), heads_of(values, 1 - half)])
    given = to_other_core(to_give)
    given, queries = lax.optimization_barrier((given, queries))
    own = jnp.stack([jnp.stack([heads_of(keys, half), heads_of(values, half)]), given])
    arrived = [send_round(own, kinds) for kinds in ROUNDS[:2]]
    q_far = to_other_core(
        pl.pallas_call(
            pick_kernel,
            in_specs=[smem, hbm],
            out_specs=vmem,
            out_shape=side_shape,
            scratch_shapes=[pltpu.SemaphoreType.DMA],
            name="pick_queries",
            **common,
        )(place, queries)
    )

    chunk_heads = queries.shape[1] // keys.shape[1] // PARTS
    ahead = pltpu.VMEM((chunk_heads * rows, 4 * rows), jnp.float32)
    state_shapes = (placed_shape, max_shape, acc_shape)
    lows_shape = jax.ShapeDtypeStruct((2, rows, rows), jnp.int32)
    info_shape = jax.ShapeDtypeStruct((BOUNDS + 4,), jnp.int32)
    *state, lows, info = pl.pallas_call(
        functools.partial(own_kernel, side=0),
        in_specs=[smem, smem, hbm, vmem],
        out_specs=(vmem, vmem, vmem, vmem, smem),
        out_shape=state_shapes + (lows_shape, info_shape),
        scratch_shapes=[ahead, pltpu.VMEM((rows, half_heads), queries.dtype), pltpu.SemaphoreType.DMA],
        name="attend_own_near",
        **{**common, "cost_estimate": pl.CostEstimate(flops=10**11, bytes_accessed=0, transcendentals=0)},
    )(place, doc_lengths, queries, own)
    placed, row_max, acc = pl.pallas_call(
        functools.partial(own_kernel, side=1),
        in_specs=[smem] + [vmem] * 6,
        out_specs=(vmem, vmem, vmem),
        out_shape=state_shapes,
        input_output_aliases={3: 0, 4: 1, 5: 2},
        scratch_shapes=[ahead],
        name="attend_own_far",
        **common,
    )(info, q_far, own, *state, lows)

    def attend(kv, row_max, acc, number):
        return pl.pallas_call(
            functools.partial(span_kernel, numbers=tuple(range(number, number + len(kv)))),
            in_specs=[smem] + [vmem] * (len(kv) + 4),
            out_specs=(vmem, vmem),
            out_shape=(max_shape, acc_shape),
            input_output_aliases={len(kv) + 3: 0, len(kv) + 4: 1},
            scratch_shapes=[ahead],
            name="attend_spans",
            **common,
        )(info, lows, *kv, placed, row_max, acc)

    behind, acc = lax.optimization_barrier((arrived[0], acc))
    opposite, acc = lax.optimization_barrier((arrived[1], acc))

    def plane_round(number):
        sends = [jnp.where((place_in_group ^ kind) > place_in_group, own, behind) for kind in ROUNDS[number]]
        return jnp.where(half == 0, *sends)

    first = send_round(plane_round(2), ROUNDS[2])
    relayed = send_round(opposite, ROUNDS[3])
    row_max, acc = attend([behind, opposite], row_max, acc, 0)
    to_second, first, acc = lax.optimization_barrier((plane_round(4), first, acc))
    second = send_round(to_second, ROUNDS[4])
    row_max, acc = attend([first], row_max, acc, 2)

    last_args = (info, lows, relayed, second, placed, row_max, acc)
    def finish(side, name):
        return pl.pallas_call(
            functools.partial(last_kernel, numbers=(3, 4), side=side),
            in_specs=[smem] + [vmem] * 6,
            out_specs=vmem,
            out_shape=side_shape,
            scratch_shapes=[ahead],
            name=name,
            **common,
        )(*last_args)

    out_far = to_other_core(finish(1, "attend_last_far"))
    return pl.pallas_call(
        join_kernel,
        in_specs=[smem, vmem, vmem],
        out_specs=anywhere,
        out_shape=jax.ShapeDtypeStruct(queries.shape, queries.dtype),
        scratch_shapes=[pltpu.SemaphoreType.DMA((2, 4))],
        name="join_heads",
        **common,
    )(info, finish(0, "attend_last_near"), out_far)


def solution(mesh):
    placed = P(AXES, None)
    return jax.shard_map(
        per_device, mesh=mesh, in_specs=(placed, placed, placed, P()), out_specs=placed, check_vma=False
    )
```

```python
import functools
import math

import jax
import jax.numpy as jnp
from jax import lax
from jax.experimental import pallas as pl
from jax.experimental.pallas import tpu as pltpu
from jax.sharding import PartitionSpec as P

HD = 128
REACH = 4
NEVER = -1e30
SCORE_SCALE = HD ** (-0.5) * math.log2(math.e)
PARTS = 4
AXES = ("ctx", "head")
SHIFT, SHIFT_OPPOSITE, OPPOSITE = "shift", "shift opposite", REACH - 1
ROUNDS = ((SHIFT, SHIFT), (OPPOSITE, OPPOSITE), (1, 2), (SHIFT_OPPOSITE, SHIFT_OPPOSITE), (2, 1))
BOUNDS = 3 + 2 * len(ROUNDS)


def send_round(block, kinds):
    spans, cores = lax.axis_size("ctx"), lax.axis_size("head")
    pairs = []
    for s in range(spans):
        for core, kind in enumerate(kinds):
            if kind in (SHIFT, SHIFT_OPPOSITE):
                target = s + REACH
                if target >= spans or (kind == SHIFT_OPPOSITE and s % REACH >= REACH // 2):
                    continue
            else:
                target = s ^ kind
            pairs.append((s * cores + core, target * cores + core))
    return lax.ppermute(block, AXES, pairs)


def to_other_core(block):
    cores = lax.axis_size("head")
    return lax.ppermute(block, "head", [(h, cores - 1 - h) for h in range(cores)])


def doc_starts(lengths_ref, first, last):
    def one_doc(i, carry):
        start, lo_first, lo_last = carry
        start = start + lengths_ref[i]
        return start, jnp.where(start <= first, start, lo_first), jnp.where(start <= last, start, lo_last)

    zero = jnp.int32(0)
    _, lo_first, lo_last = lax.fori_loop(0, lengths_ref.shape[0], one_doc, (zero, zero, zero))
    return lo_first, lo_last


def doc_start_rows(lengths_ref, first_query, rows):
    pos = first_query + lax.broadcasted_iota(jnp.int32, (rows, rows), 0)

    def one_doc(i, carry):
        start, lo = carry
        start = start + lengths_ref[i]
        return start, jnp.where(start <= pos, start, lo)

    zero = jnp.zeros((rows, rows), jnp.int32)
    return lax.fori_loop(0, lengths_ref.shape[0], one_doc, (jnp.int32(0), zero))[1]


def block_of(at, size):
    return pl.ds(pl.multiple_of(at * size, size), size)


def positions(start, rows):
    return start + lax.broadcasted_iota(jnp.int32, (rows, rows), 1)


def softmax_step(scores, allowed, max_before):
    if allowed is not None:
        allowed = jnp.concatenate([allowed] * (scores.shape[0] // allowed.shape[0]), axis=0)
        scores = jnp.where(allowed, scores, NEVER)
    row_max = jnp.broadcast_to(jnp.max(scores, axis=1, keepdims=True), (scores.shape[0], HD))
    rescale = None
    if max_before is not None:
        row_max = jnp.maximum(max_before, row_max)
        rescale = jnp.exp2((max_before - row_max) * SCORE_SCALE)
    shift = jnp.concatenate([row_max] * (scores.shape[1] // HD), axis=1)
    return jnp.exp2((scores - shift) * SCORE_SCALE).astype(jnp.bfloat16), row_max, rescale


def scores_for(queries, keys):
    return lax.dot_general(queries, keys, (((1,), (1,)), ((), ())), preferred_element_type=jnp.float32)


def pipeline(kv_heads, ahead_ref, allowed, scores_of, values_of, before_of, store):
    def finish(g, part, scores):
        max_before, acc_before = before_of(g, part)
        weights, row_max, rescale = softmax_step(scores, allowed, max_before)
        values = values_of(g)
        widened = jnp.concatenate([values, jnp.ones_like(values)], axis=1)
        acc = jnp.dot(weights, widened, preferred_element_type=jnp.float32)
        if rescale is not None:
            acc = acc_before * jnp.concatenate([rescale] * 2, axis=1) + acc
        store(g, part, row_max, acc)

    ahead_ref[...] = scores_of(0, 0)

    def one_head(g, _):
        scores = ahead_ref[...]
        for part in range(PARTS):
            if part + 1 < PARTS:
                later = scores_of(g, part + 1)
            else:
                later = scores_of(jnp.minimum(g + 1, kv_heads - 1), 0)
            finish(g, part, scores)
            scores = later
        ahead_ref[...] = scores
        return 0

    lax.fori_loop(0, kv_heads, one_head, 0)


def pick_kernel(place_ref, q_ref, out_ref, sem):
    copy = pltpu.make_async_copy(q_ref.at[:, block_of(1 - place_ref[2], out_ref.shape[1])], out_ref, sem)
    copy.start()
    copy.wait()


def own_kernel(place_ref, *refs, side):
    if side == 0:
        lengths_ref, q_ref, kv_ref, *refs = refs
        queries_ref, max_ref, acc_ref, lows_ref, info_ref, ahead_ref, q_side_ref, sem = refs
        fetch = pltpu.make_async_copy(q_ref.at[:, block_of(place_ref[2], q_side_ref.shape[1])], q_side_ref, sem)
        fetch.start()
    else:
        q_ref, kv_ref, _, _, _, lows_ref, queries_ref, max_ref, acc_ref, ahead_ref = refs
        q_side_ref = q_ref
    rows, wide = q_side_ref.shape
    kv_heads = kv_ref.shape[3] // HD
    heads = wide // (kv_heads * PARTS * HD)
    half = place_ref[2]
    first, other = place_ref[side], place_ref[1 - side]
    query_pos = first + lax.broadcasted_iota(jnp.int32, (rows, rows), 0)
    if side == 0:
        for i in range(2):
            lows_ref[i] = doc_start_rows(lengths_ref, place_ref[i], rows)
            low, high = doc_starts(lengths_ref, place_ref[i], place_ref[i] + rows - 1)
            info_ref[BOUNDS + 2 * i], info_ref[BOUNDS + 2 * i + 1] = low, high
        for i in range(BOUNDS):
            info_ref[i] = place_ref[i]
    lows = lows_ref[side]
    key_pos = positions(first, rows)
    diagonal = (key_pos >= lows) & (key_pos <= query_pos)
    earlier = positions(other, rows) >= lows
    if side == 0:
        fetch.wait()

    def at(g, part):
        return block_of((side * kv_heads + g) * PARTS + part, heads * rows)

    def place_queries(i, _):
        q = q_side_ref[:, block_of(i, heads * HD)]
        queries_ref[block_of(side * kv_heads * PARTS + i, heads * rows), :] = jnp.concatenate(
            [q[:, h * HD : (h + 1) * HD] for h in range(heads)], axis=0
        )
        return 0

    lax.fori_loop(0, kv_heads * PARTS, place_queries, 0)

    def store(g, part, row_max, acc):
        max_ref[at(g, part), :] = row_max
        acc_ref[at(g, part), :] = acc

    def work(blocks, allowed):
        def of(i, g):
            return jnp.concatenate([kv_ref[block, i, :, block_of(g, HD)] for block in blocks], axis=0)

        pipeline(
            kv_heads,
            ahead_ref.at[:, : len(blocks) * rows],
            allowed,
            lambda g, part: scores_for(queries_ref[at(g, part), :], of(0, g)),
            lambda g: of(1, g),
            lambda g, part: (None, None),
            store,
        )

    pl.when(half == side)(lambda: work([side], diagonal))
    pl.when(half != side)(lambda: work([1 - side, side], jnp.concatenate([earlier, diagonal], axis=1)))


def span_steps(place_ref, lows_ref, kv_refs, queries_ref, ahead_ref, numbers, side, load, store):
    rows = kv_refs[0].shape[2]
    kv_heads = kv_refs[0].shape[3] // HD
    key_starts = [(place_ref[3 + 2 * number], place_ref[4 + 2 * number]) for number in numbers]
    lo_first, lo_last = place_ref[BOUNDS + 2 * side], place_ref[BOUNDS + 2 * side + 1]
    needed = [jnp.maximum(*starts) + rows > lo_first for starts in key_starts]

    def at(g, part):
        return block_of((side * kv_heads + g) * PARTS + part, ahead_ref.shape[0])

    def work(chosen, masked):
        def of(i, g):
            parts = [kv_refs[n][block, i, :, block_of(g, HD)] for n in chosen for block in range(2)]
            return jnp.concatenate(parts, axis=0)

        allowed = None
        if masked:
            lows = lows_ref[side]
            allowed = jnp.concatenate(
                [positions(start, rows) >= lows for n in chosen for start in key_starts[n]], axis=1
            )
        pipeline(
            kv_heads,
            ahead_ref.at[:, : 2 * rows * len(chosen)],
            allowed,
            lambda g, part: scores_for(queries_ref[at(g, part), :], of(0, g)),
            lambda g: of(1, g),
            lambda g, part: load(at(g, part)),
            lambda g, part, row_max, acc: store(g, part, at(g, part), row_max, acc),
        )

    if len(numbers) == 1:
        whole = jnp.minimum(*key_starts[0]) >= lo_last
        pl.when(whole)(lambda: work([0], False))
        pl.when(needed[0] & jnp.logical_not(whole))(lambda: work([0], True))
        return needed[0]
    pl.when(needed[0] & needed[1])(lambda: work([0, 1], True))
    pl.when(needed[0] & jnp.logical_not(needed[1]))(lambda: work([0], True))
    pl.when(needed[1] & jnp.logical_not(needed[0]))(lambda: work([1], True))
    return needed[0] | needed[1]


def span_kernel(place_ref, lows_ref, *refs, numbers):
    kv_refs, (queries_ref, _, _, max_ref, acc_ref, ahead_ref) = refs[: len(numbers)], refs[len(numbers) :]

    def load(at):
        return max_ref[at, :], acc_ref[at, :]

    def store(g, part, at, row_max, acc):
        max_ref[at, :] = row_max
        acc_ref[at, :] = acc

    def one_side(side, _):
        span_steps(place_ref, lows_ref, kv_refs, queries_ref, ahead_ref, numbers, side, load, store)
        return 0

    lax.fori_loop(0, 2, one_side, 0)


def last_kernel(place_ref, lows_ref, *refs, numbers, side):
    kv_refs, (queries_ref, max_ref, acc_ref, out_ref, ahead_ref) = refs[: len(numbers)], refs[len(numbers) :]
    rows = kv_refs[0].shape[2]
    kv_heads = kv_refs[0].shape[3] // HD
    chunk = ahead_ref.shape[0]
    heads = chunk // rows

    def load(at):
        return max_ref[at, :], acc_ref[at, :]

    def finish(g, part, at, row_max, acc):
        finished = (acc[:, :HD] * (1.0 / acc[:, HD:])).astype(out_ref.dtype)
        out_ref[:, block_of(g * PARTS + part, heads * HD)] = jnp.concatenate(
            [finished[h * rows : (h + 1) * rows] for h in range(heads)], axis=1
        )

    needed = span_steps(place_ref, lows_ref, kv_refs, queries_ref, ahead_ref, numbers, side, load, finish)

    @pl.when(jnp.logical_not(needed))
    def _():
        def one_head(g, _):
            for part in range(PARTS):
                finish(g, part, None, *load(block_of((side * kv_heads + g) * PARTS + part, chunk)))
            return 0

        lax.fori_loop(0, kv_heads, one_head, 0)


def join_kernel(place_ref, near_ref, far_ref, out_ref, sems):
    pieces = sems.shape[1]
    rows = far_ref.shape[0] // pieces
    copies = []
    for side, source in enumerate((near_ref, far_ref)):
        columns = block_of(place_ref[2] if side == 0 else 1 - place_ref[2], source.shape[1])
        for i in range(pieces):
            here = pl.ds(i * rows, rows)
            copies.append(pltpu.make_async_copy(source.at[here, :], out_ref.at[here, columns], sems.at[side, i]))
    for copy in copies:
        copy.start()
    for copy in copies:
        copy.wait()


def per_device(queries, keys, values, doc_lengths):
    rows, all_heads = queries.shape
    half_heads = all_heads // 2
    head_rows = (all_heads // HD) * rows
    half, span = lax.axis_index("head"), lax.axis_index("ctx")
    cores = lax.axis_size("head")
    place_in_group = lax.rem(span, REACH)

    nowhere = -2 * REACH

    def origin(kind):
        if kind == SHIFT:
            return span - REACH
        late = place_in_group >= REACH // 2
        from_place = place_in_group ^ (OPPOSITE if kind == SHIFT_OPPOSITE else kind)
        here = span - place_in_group + from_place
        if kind == SHIFT_OPPOSITE:
            return jnp.where(late, nowhere, here - REACH)
        if kind == OPPOSITE:
            return jnp.where(late, here, nowhere)
        return here - jnp.where(from_place > place_in_group, REACH, 0)

    parts = [(span * cores + half) * rows, (span * cores + 1 - half) * rows, half]
    for kinds in ROUNDS:
        start = jnp.where(half == 0, origin(kinds[0]), origin(kinds[1]))
        parts += [(start * cores + half) * rows, (start * cores + 1 - half) * rows]
    place = jnp.stack(parts).astype(jnp.int32)

    vmem = pl.BlockSpec(memory_space=pltpu.VMEM)
    smem = pl.BlockSpec(memory_space=pltpu.SMEM)
    anywhere = pl.BlockSpec(memory_space=pl.ANY)
    hbm = pl.BlockSpec(memory_space=pltpu.MemorySpace.HBM)
    placed_shape = jax.ShapeDtypeStruct((head_rows, HD), queries.dtype)
    max_shape = jax.ShapeDtypeStruct((head_rows, HD), jnp.float32)
    acc_shape = jax.ShapeDtypeStruct((head_rows, 2 * HD), jnp.float32)
    side_shape = jax.ShapeDtypeStruct((rows, half_heads), queries.dtype)
    common = dict(
        compiler_params=pltpu.CompilerParams(vmem_limit_bytes=24 * 1024 * 1024),
        cost_estimate=pl.CostEstimate(flops=0, bytes_accessed=0, transcendentals=0),
    )

    def heads_of(array, core):
        width = array.shape[1] // 2
        return lax.dynamic_slice_in_dim(array, core * width, width, 1)

    to_give = jnp.stack([heads_of(keys, 1 - half), heads_of(values, 1 - half)])
    given = to_other_core(to_give)
    given, queries = lax.optimization_barrier((given, queries))
    own = jnp.stack([jnp.stack([heads_of(keys, half), heads_of(values, half)]), given])
    arrived = [send_round(own, kinds) for kinds in ROUNDS[:2]]
    q_far = to_other_core(
        pl.pallas_call(
            pick_kernel,
            in_specs=[smem, hbm],
            out_specs=vmem,
            out_shape=side_shape,
            scratch_shapes=[pltpu.SemaphoreType.DMA],
            name="pick_queries",
            **common,
        )(place, queries)
    )

    chunk_heads = queries.shape[1] // keys.shape[1] // PARTS
    ahead = pltpu.VMEM((chunk_heads * rows, 4 * rows), jnp.float32)
    state_shapes = (placed_shape, max_shape, acc_shape)
    lows_shape = jax.ShapeDtypeStruct((2, rows, rows), jnp.int32)
    info_shape = jax.ShapeDtypeStruct((BOUNDS + 4,), jnp.int32)
    *state, lows, info = pl.pallas_call(
        functools.partial(own_kernel, side=0),
        in_specs=[smem, smem, hbm, vmem],
        out_specs=(vmem, vmem, vmem, vmem, smem),
        out_shape=state_shapes + (lows_shape, info_shape),
        scratch_shapes=[ahead, pltpu.VMEM((rows, half_heads), queries.dtype), pltpu.SemaphoreType.DMA],
        name="attend_own_near",
        **{**common, "cost_estimate": pl.CostEstimate(flops=10**11, bytes_accessed=0, transcendentals=0)},
    )(place, doc_lengths, queries, own)
    placed, row_max, acc = pl.pallas_call(
        functools.partial(own_kernel, side=1),
        in_specs=[smem] + [vmem] * 6,
        out_specs=(vmem, vmem, vmem),
        out_shape=state_shapes,
        input_output_aliases={3: 0, 4: 1, 5: 2},
        scratch_shapes=[ahead],
        name="attend_own_far",
        **common,
    )(info, q_far, own, *state, lows)

    def attend(kv, row_max, acc, number):
        return pl.pallas_call(
            functools.partial(span_kernel, numbers=tuple(range(number, number + len(kv)))),
            in_specs=[smem] + [vmem] * (len(kv) + 4),
            out_specs=(vmem, vmem),
            out_shape=(max_shape, acc_shape),
            input_output_aliases={len(kv) + 3: 0, len(kv) + 4: 1},
            scratch_shapes=[ahead],
            name="attend_spans",
            **common,
        )(info, lows, *kv, placed, row_max, acc)

    behind, acc = lax.optimization_barrier((arrived[0], acc))
    opposite, acc = lax.optimization_barrier((arrived[1], acc))

    def plane_round(number):
        sends = [jnp.where((place_in_group ^ kind) > place_in_group, own, behind) for kind in ROUNDS[number]]
        return jnp.where(half == 0, *sends)

    first = send_round(plane_round(2), ROUNDS[2])
    relayed = send_round(opposite, ROUNDS[3])
    row_max, acc = attend([behind, opposite], row_max, acc, 0)
    to_second, first, acc = lax.optimization_barrier((plane_round(4), first, acc))
    second = send_round(to_second, ROUNDS[4])
    row_max, acc = attend([first], row_max, acc, 2)

    last_args = (info, lows, relayed, second, placed, row_max, acc)
    def finish(side, name):
        return pl.pallas_call(
            functools.partial(last_kernel, numbers=(3, 4), side=side),
            in_specs=[smem] + [vmem] * 6,
            out_specs=vmem,
            out_shape=side_shape,
            scratch_shapes=[ahead],
            name=name,
            **common,
        )(*last_args)

    out_far = to_other_core(finish(1, "attend_last_far"))
    return pl.pallas_call(
        join_kernel,
        in_specs=[smem, vmem, vmem],
        out_specs=anywhere,
        out_shape=jax.ShapeDtypeStruct(queries.shape, queries.dtype),
        scratch_shapes=[pltpu.SemaphoreType.DMA((2, 4))],
        name="join_heads",
        **common,
    )(info, finish(0, "attend_last_near"), out_far)


def solution(mesh):
    placed = P(AXES, None)
    return jax.shard_map(
        per_device, mesh=mesh, in_specs=(placed, placed, placed, P()), out_specs=placed, check_vma=False
    )
```

```python
import functools
import math

import jax
import jax.numpy as jnp
from jax import lax
from jax.experimental import pallas as pl
from jax.experimental.pallas import tpu as pltpu
from jax.sharding import PartitionSpec as P

HD = 128
REACH = 4
NEVER = -1e30
SCORE_SCALE = HD ** (-0.5) * math.log2(math.e)
PARTS = 2
AXES = ("ctx", "head")
SHIFT, SHIFT_OPPOSITE, OPPOSITE = "shift", "shift opposite", REACH - 1
ROUNDS = ((SHIFT, SHIFT), (OPPOSITE, OPPOSITE), (1, 2), (SHIFT_OPPOSITE, SHIFT_OPPOSITE), (2, 1))
BOUNDS = 3 + 2 * len(ROUNDS)


def send_round(block, kinds):
    spans, cores = lax.axis_size("ctx"), lax.axis_size("head")
    pairs = []
    for s in range(spans):
        for core, kind in enumerate(kinds):
            if kind in (SHIFT, SHIFT_OPPOSITE):
                target = s + REACH
                if target >= spans or (kind == SHIFT_OPPOSITE and s % REACH >= REACH // 2):
                    continue
            else:
                target = s ^ kind
            pairs.append((s * cores + core, target * cores + core))
    return lax.ppermute(block, AXES, pairs)


def to_other_core(block):
    cores = lax.axis_size("head")
    return lax.ppermute(block, "head", [(h, cores - 1 - h) for h in range(cores)])


def doc_starts(lengths_ref, first, last):
    def one_doc(i, carry):
        start, lo_first, lo_last = carry
        start = start + lengths_ref[i]
        return start, jnp.where(start <= first, start, lo_first), jnp.where(start <= last, start, lo_last)

    zero = jnp.int32(0)
    _, lo_first, lo_last = lax.fori_loop(0, lengths_ref.shape[0], one_doc, (zero, zero, zero))
    return lo_first, lo_last


def doc_start_rows(lengths_ref, first_query, rows):
    pos = first_query + lax.broadcasted_iota(jnp.int32, (rows, rows), 0)

    def one_doc(i, carry):
        start, lo = carry
        start = start + lengths_ref[i]
        return start, jnp.where(start <= pos, start, lo)

    zero = jnp.zeros((rows, rows), jnp.int32)
    return lax.fori_loop(0, lengths_ref.shape[0], one_doc, (jnp.int32(0), zero))[1]


def block_of(at, size):
    return pl.ds(pl.multiple_of(at * size, size), size)


def positions(start, rows):
    return start + lax.broadcasted_iota(jnp.int32, (rows, rows), 1)


def softmax_step(scores, allowed, max_before):
    if allowed is not None:
        allowed = jnp.concatenate([allowed] * (scores.shape[0] // allowed.shape[0]), axis=0)
        scores = jnp.where(allowed, scores, NEVER)
    row_max = jnp.broadcast_to(jnp.max(scores, axis=1, keepdims=True), (scores.shape[0], HD))
    rescale = None
    if max_before is not None:
        row_max = jnp.maximum(max_before, row_max)
        rescale = jnp.exp2((max_before - row_max) * SCORE_SCALE)
    shift = jnp.concatenate([row_max] * (scores.shape[1] // HD), axis=1)
    return jnp.exp2((scores - shift) * SCORE_SCALE).astype(jnp.bfloat16), row_max, rescale


def scores_for(queries, keys):
    return lax.dot_general(queries, keys, (((1,), (1,)), ((), ())), preferred_element_type=jnp.float32)


def pipeline(kv_heads, ahead_ref, allowed, scores_of, values_of, before_of, store):
    def finish(g, part, scores):
        max_before, acc_before = before_of(g, part)
        weights, row_max, rescale = softmax_step(scores, allowed, max_before)
        values = values_of(g)
        widened = jnp.concatenate([values, jnp.ones_like(values)], axis=1)
        acc = jnp.dot(weights, widened, preferred_element_type=jnp.float32)
        if rescale is not None:
            acc = acc_before * jnp.concatenate([rescale] * 2, axis=1) + acc
        store(g, part, row_max, acc)

    ahead_ref[...] = scores_of(0, 0)
    step = 2 if kv_heads % 2 == 0 else 1

    def some_heads(i, _):
        scores = ahead_ref[...]
        for number in range(step * PARTS):
            if number + 1 < step * PARTS:
                later = scores_of(i * step + (number + 1) // PARTS, (number + 1) % PARTS)
            else:
                later = scores_of(jnp.minimum((i + 1) * step, kv_heads - 1), 0)
            finish(i * step + number // PARTS, number % PARTS, scores)
            scores = later
        ahead_ref[...] = scores
        return 0

    lax.fori_loop(0, kv_heads // step, some_heads, 0)


def pick_kernel(place_ref, q_ref, out_ref, sem):
    copy = pltpu.make_async_copy(q_ref.at[:, block_of(1 - place_ref[2], out_ref.shape[1])], out_ref, sem)
    copy.start()
    copy.wait()


def own_kernel(place_ref, *refs, side):
    if side == 0:
        lengths_ref, q_ref, kv_ref, *refs = refs
        queries_ref, max_ref, acc_ref, lows_ref, info_ref, ahead_ref, q_side_ref, sem = refs
        fetch = pltpu.make_async_copy(q_ref.at[:, block_of(place_ref[2], q_side_ref.shape[1])], q_side_ref, sem)
        fetch.start()
    else:
        q_ref, kv_ref, _, _, _, lows_ref, queries_ref, max_ref, acc_ref, ahead_ref = refs
        q_side_ref = q_ref
    rows, wide = q_side_ref.shape
    kv_heads = kv_ref.shape[3] // HD
    heads = wide // (kv_heads * PARTS * HD)
    half = place_ref[2]
    first, other = place_ref[side], place_ref[1 - side]
    query_pos = first + lax.broadcasted_iota(jnp.int32, (rows, rows), 0)
    if side == 0:
        for i in range(2):
            lows_ref[i] = doc_start_rows(lengths_ref, place_ref[i], rows)
            low, high = doc_starts(lengths_ref, place_ref[i], place_ref[i] + rows - 1)
            info_ref[BOUNDS + 2 * i], info_ref[BOUNDS + 2 * i + 1] = low, high
        for i in range(BOUNDS):
            info_ref[i] = place_ref[i]
    lows = lows_ref[side]
    key_pos = positions(first, rows)
    diagonal = (key_pos >= lows) & (key_pos <= query_pos)
    earlier = positions(other, rows) >= lows
    if side == 0:
        fetch.wait()

    def at(g, part):
        return block_of((side * kv_heads + g) * PARTS + part, heads * rows)

    def place_queries(i, _):
        q = q_side_ref[:, block_of(i, heads * HD)]
        queries_ref[block_of(side * kv_heads * PARTS + i, heads * rows), :] = jnp.concatenate(
            [q[:, h * HD : (h + 1) * HD] for h in range(heads)], axis=0
        )
        return 0

    lax.fori_loop(0, kv_heads * PARTS, place_queries, 0)

    def store(g, part, row_max, acc):
        max_ref[at(g, part), :] = row_max
        acc_ref[at(g, part), :] = acc

    def work(blocks, allowed):
        def of(i, g):
            return jnp.concatenate([kv_ref[block, i, :, block_of(g, HD)] for block in blocks], axis=0)

        pipeline(
            kv_heads,
            ahead_ref.at[:, : len(blocks) * rows],
            allowed,
            lambda g, part: scores_for(queries_ref[at(g, part), :], of(0, g)),
            lambda g: of(1, g),
            lambda g, part: (None, None),
            store,
        )

    pl.when(half == side)(lambda: work([side], diagonal))
    pl.when(half != side)(lambda: work([1 - side, side], jnp.concatenate([earlier, diagonal], axis=1)))


def span_steps(place_ref, lows_ref, kv_refs, queries_ref, ahead_ref, numbers, side, load, store):
    rows = kv_refs[0].shape[2]
    kv_heads = kv_refs[0].shape[3] // HD
    key_starts = [(place_ref[3 + 2 * number], place_ref[4 + 2 * number]) for number in numbers]
    lo_first, lo_last = place_ref[BOUNDS + 2 * side], place_ref[BOUNDS + 2 * side + 1]
    needed = [jnp.maximum(*starts) + rows > lo_first for starts in key_starts]

    def at(g, part):
        return block_of((side * kv_heads + g) * PARTS + part, ahead_ref.shape[0])

    def work(chosen, masked):
        def of(i, g):
            parts = [kv_refs[n][block, i, :, block_of(g, HD)] for n in chosen for block in range(2)]
            return jnp.concatenate(parts, axis=0)

        allowed = None
        if masked:
            lows = lows_ref[side]
            allowed = jnp.concatenate(
                [positions(start, rows) >= lows for n in chosen for start in key_starts[n]], axis=1
            )
        pipeline(
            kv_heads,
            ahead_ref.at[:, : 2 * rows * len(chosen)],
            allowed,
            lambda g, part: scores_for(queries_ref[at(g, part), :], of(0, g)),
            lambda g: of(1, g),
            lambda g, part: load(at(g, part)),
            lambda g, part, row_max, acc: store(g, part, at(g, part), row_max, acc),
        )

    if len(numbers) == 1:
        whole = jnp.minimum(*key_starts[0]) >= lo_last
        pl.when(whole)(lambda: work([0], False))
        pl.when(needed[0] & jnp.logical_not(whole))(lambda: work([0], True))
        return needed[0]
    pl.when(needed[0] & needed[1])(lambda: work([0, 1], True))
    pl.when(needed[0] & jnp.logical_not(needed[1]))(lambda: work([0], True))
    pl.when(needed[1] & jnp.logical_not(needed[0]))(lambda: work([1], True))
    return needed[0] | needed[1]


def span_kernel(place_ref, lows_ref, *refs, numbers):
    kv_refs, (queries_ref, _, _, max_ref, acc_ref, ahead_ref) = refs[: len(numbers)], refs[len(numbers) :]

    def load(at):
        return max_ref[at, :], acc_ref[at, :]

    def store(g, part, at, row_max, acc):
        max_ref[at, :] = row_max
        acc_ref[at, :] = acc

    def one_side(side, _):
        span_steps(place_ref, lows_ref, kv_refs, queries_ref, ahead_ref, numbers, side, load, store)
        return 0

    lax.fori_loop(0, 2, one_side, 0)


def last_kernel(place_ref, lows_ref, *refs, numbers, side):
    kv_refs, (queries_ref, max_ref, acc_ref, out_ref, ahead_ref) = refs[: len(numbers)], refs[len(numbers) :]
    rows = kv_refs[0].shape[2]
    kv_heads = kv_refs[0].shape[3] // HD
    chunk = ahead_ref.shape[0]
    heads = chunk // rows

    def load(at):
        return max_ref[at, :], acc_ref[at, :]

    def finish(g, part, at, row_max, acc):
        finished = (acc[:, :HD] * (1.0 / acc[:, HD:])).astype(out_ref.dtype)
        out_ref[:, block_of(g * PARTS + part, heads * HD)] = jnp.concatenate(
            [finished[h * rows : (h + 1) * rows] for h in range(heads)], axis=1
        )

    needed = span_steps(place_ref, lows_ref, kv_refs, queries_ref, ahead_ref, numbers, side, load, finish)

    @pl.when(jnp.logical_not(needed))
    def _():
        def one_head(g, _):
            for part in range(PARTS):
                finish(g, part, None, *load(block_of((side * kv_heads + g) * PARTS + part, chunk)))
            return 0

        lax.fori_loop(0, kv_heads, one_head, 0)


def join_kernel(place_ref, near_ref, far_ref, out_ref, sems):
    pieces = sems.shape[1]
    rows = far_ref.shape[0] // pieces
    copies = []
    for side, source in enumerate((near_ref, far_ref)):
        columns = block_of(place_ref[2] if side == 0 else 1 - place_ref[2], source.shape[1])
        for i in range(pieces):
            here = pl.ds(i * rows, rows)
            copies.append(pltpu.make_async_copy(source.at[here, :], out_ref.at[here, columns], sems.at[side, i]))
    for copy in copies:
        copy.start()
    for copy in copies:
        copy.wait()


def per_device(queries, keys, values, doc_lengths):
    rows, all_heads = queries.shape
    half_heads = all_heads // 2
    head_rows = (all_heads // HD) * rows
    half, span = lax.axis_index("head"), lax.axis_index("ctx")
    cores = lax.axis_size("head")
    place_in_group = lax.rem(span, REACH)

    nowhere = -2 * REACH

    def origin(kind):
        if kind == SHIFT:
            return span - REACH
        late = place_in_group >= REACH // 2
        from_place = place_in_group ^ (OPPOSITE if kind == SHIFT_OPPOSITE else kind)
        here = span - place_in_group + from_place
        if kind == SHIFT_OPPOSITE:
            return jnp.where(late, nowhere, here - REACH)
        if kind == OPPOSITE:
            return jnp.where(late, here, nowhere)
        return here - jnp.where(from_place > place_in_group, REACH, 0)

    parts = [(span * cores + half) * rows, (span * cores + 1 - half) * rows, half]
    for kinds in ROUNDS:
        start = jnp.where(half == 0, origin(kinds[0]), origin(kinds[1]))
        parts += [(start * cores + half) * rows, (start * cores + 1 - half) * rows]
    place = jnp.stack(parts).astype(jnp.int32)

    vmem = pl.BlockSpec(memory_space=pltpu.VMEM)
    smem = pl.BlockSpec(memory_space=pltpu.SMEM)
    anywhere = pl.BlockSpec(memory_space=pl.ANY)
    hbm = pl.BlockSpec(memory_space=pltpu.MemorySpace.HBM)
    placed_shape = jax.ShapeDtypeStruct((head_rows, HD), queries.dtype)
    max_shape = jax.ShapeDtypeStruct((head_rows, HD), jnp.float32)
    acc_shape = jax.ShapeDtypeStruct((head_rows, 2 * HD), jnp.float32)
    side_shape = jax.ShapeDtypeStruct((rows, half_heads), queries.dtype)
    common = dict(
        compiler_params=pltpu.CompilerParams(vmem_limit_bytes=24 * 1024 * 1024),
        cost_estimate=pl.CostEstimate(flops=0, bytes_accessed=0, transcendentals=0),
    )

    def heads_of(array, core):
        width = array.shape[1] // 2
        return lax.dynamic_slice_in_dim(array, core * width, width, 1)

    to_give = jnp.stack([heads_of(keys, 1 - half), heads_of(values, 1 - half)])
    given = to_other_core(to_give)
    given, queries = lax.optimization_barrier((given, queries))
    own = jnp.stack([jnp.stack([heads_of(keys, half), heads_of(values, half)]), given])
    arrived = [send_round(own, kinds) for kinds in ROUNDS[:2]]
    q_far = to_other_core(
        pl.pallas_call(
            pick_kernel,
            in_specs=[smem, hbm],
            out_specs=vmem,
            out_shape=side_shape,
            scratch_shapes=[pltpu.SemaphoreType.DMA],
            name="pick_queries",
            **common,
        )(place, queries)
    )

    chunk_heads = queries.shape[1] // keys.shape[1] // PARTS
    ahead = pltpu.VMEM((chunk_heads * rows, 4 * rows), jnp.float32)
    state_shapes = (placed_shape, max_shape, acc_shape)
    lows_shape = jax.ShapeDtypeStruct((2, rows, rows), jnp.int32)
    info_shape = jax.ShapeDtypeStruct((BOUNDS + 4,), jnp.int32)
    *state, lows, info = pl.pallas_call(
        functools.partial(own_kernel, side=0),
        in_specs=[smem, smem, hbm, vmem],
        out_specs=(vmem, vmem, vmem, vmem, smem),
        out_shape=state_shapes + (lows_shape, info_shape),
        scratch_shapes=[ahead, pltpu.VMEM((rows, half_heads), queries.dtype), pltpu.SemaphoreType.DMA],
        name="attend_own_near",
        **{**common, "cost_estimate": pl.CostEstimate(flops=10**11, bytes_accessed=0, transcendentals=0)},
    )(place, doc_lengths, queries, own)
    placed, row_max, acc = pl.pallas_call(
        functools.partial(own_kernel, side=1),
        in_specs=[smem] + [vmem] * 6,
        out_specs=(vmem, vmem, vmem),
        out_shape=state_shapes,
        input_output_aliases={3: 0, 4: 1, 5: 2},
        scratch_shapes=[ahead],
        name="attend_own_far",
        **common,
    )(info, q_far, own, *state, lows)

    def attend(kv, row_max, acc, number):
        return pl.pallas_call(
            functools.partial(span_kernel, numbers=tuple(range(number, number + len(kv)))),
            in_specs=[smem] + [vmem] * (len(kv) + 4),
            out_specs=(vmem, vmem),
            out_shape=(max_shape, acc_shape),
            input_output_aliases={len(kv) + 3: 0, len(kv) + 4: 1},
            scratch_shapes=[ahead],
            name="attend_spans",
            **common,
        )(info, lows, *kv, placed, row_max, acc)

    behind, acc = lax.optimization_barrier((arrived[0], acc))
    opposite, acc = lax.optimization_barrier((arrived[1], acc))

    def plane_round(number):
        sends = [jnp.where((place_in_group ^ kind) > place_in_group, own, behind) for kind in ROUNDS[number]]
        return jnp.where(half == 0, *sends)

    first = send_round(plane_round(2), ROUNDS[2])
    relayed = send_round(opposite, ROUNDS[3])
    row_max, acc = attend([behind, opposite], row_max, acc, 0)
    to_second, first, acc = lax.optimization_barrier((plane_round(4), first, acc))
    second = send_round(to_second, ROUNDS[4])
    row_max, acc = attend([first], row_max, acc, 2)

    last_args = (info, lows, relayed, second, placed, row_max, acc)
    def finish(side, name):
        return pl.pallas_call(
            functools.partial(last_kernel, numbers=(3, 4), side=side),
            in_specs=[smem] + [vmem] * 6,
            out_specs=vmem,
            out_shape=side_shape,
            scratch_shapes=[ahead],
            name=name,
            **common,
        )(*last_args)

    out_far = to_other_core(finish(1, "attend_last_far"))
    return pl.pallas_call(
        join_kernel,
        in_specs=[smem, vmem, vmem],
        out_specs=anywhere,
        out_shape=jax.ShapeDtypeStruct(queries.shape, queries.dtype),
        scratch_shapes=[pltpu.SemaphoreType.DMA((2, 4))],
        name="join_heads",
        **common,
    )(info, finish(0, "attend_last_near"), out_far)


def solution(mesh):
    placed = P(AXES, None)
    return jax.shard_map(
        per_device, mesh=mesh, in_specs=(placed, placed, placed, P()), out_specs=placed, check_vma=False
    )
```

```python
import functools
import math

import jax
import jax.numpy as jnp
from jax import lax
from jax.experimental import pallas as pl
from jax.experimental.pallas import tpu as pltpu
from jax.sharding import PartitionSpec as P

HD = 128
REACH = 4
NEVER = -1e30
SCORE_SCALE = HD ** (-0.5) * math.log2(math.e)
PARTS = 2
AXES = ("ctx", "head")
SHIFT, SHIFT_OPPOSITE, OPPOSITE = "shift", "shift opposite", REACH - 1
ROUNDS = ((SHIFT, SHIFT), (OPPOSITE, OPPOSITE), (1, 2), (SHIFT_OPPOSITE, SHIFT_OPPOSITE), (2, 1))
BOUNDS = 3 + 2 * len(ROUNDS)


def send_round(block, kinds):
    spans, cores = lax.axis_size("ctx"), lax.axis_size("head")
    pairs = []
    for s in range(spans):
        for core, kind in enumerate(kinds):
            if kind in (SHIFT, SHIFT_OPPOSITE):
                target = s + REACH
                if target >= spans or (kind == SHIFT_OPPOSITE and s % REACH >= REACH // 2):
                    continue
            else:
                target = s ^ kind
            pairs.append((s * cores + core, target * cores + core))
    return lax.ppermute(block, AXES, pairs)


def to_other_core(block):
    cores = lax.axis_size("head")
    return lax.ppermute(block, "head", [(h, cores - 1 - h) for h in range(cores)])


def doc_starts(lengths_ref, first, last):
    def one_doc(i, carry):
        start, lo_first, lo_last = carry
        start = start + lengths_ref[i]
        return start, jnp.where(start <= first, start, lo_first), jnp.where(start <= last, start, lo_last)

    zero = jnp.int32(0)
    _, lo_first, lo_last = lax.fori_loop(0, lengths_ref.shape[0], one_doc, (zero, zero, zero))
    return lo_first, lo_last


def doc_start_rows(lengths_ref, first_query, rows):
    pos = first_query + lax.broadcasted_iota(jnp.int32, (rows, rows), 0)

    def one_doc(i, carry):
        start, lo = carry
        start = start + lengths_ref[i]
        return start, jnp.where(start <= pos, start, lo)

    zero = jnp.zeros((rows, rows), jnp.int32)
    return lax.fori_loop(0, lengths_ref.shape[0], one_doc, (jnp.int32(0), zero))[1]


def block_of(at, size):
    return pl.ds(pl.multiple_of(at * size, size), size)


def positions(start, rows):
    return start + lax.broadcasted_iota(jnp.int32, (rows, rows), 1)


def softmax_step(scores, allowed, max_before):
    if allowed is not None:
        allowed = jnp.concatenate([allowed] * (scores.shape[0] // allowed.shape[0]), axis=0)
        scores = jnp.where(allowed, scores, NEVER)
    row_max = jnp.broadcast_to(jnp.max(scores, axis=1, keepdims=True), (scores.shape[0], HD))
    rescale = None
    if max_before is not None:
        row_max = jnp.maximum(max_before, row_max)
        rescale = jnp.exp2((max_before - row_max) * SCORE_SCALE)
    shift = jnp.concatenate([row_max] * (scores.shape[1] // HD), axis=1)
    return jnp.exp2((scores - shift) * SCORE_SCALE).astype(jnp.bfloat16), row_max, rescale


def scores_for(queries, keys):
    return lax.dot_general(queries, keys, (((1,), (1,)), ((), ())), preferred_element_type=jnp.float32)


def pipeline(kv_heads, ahead_ref, allowed, scores_of, values_of, before_of, store, step=2):
    def finish(g, part, scores):
        max_before, acc_before = before_of(g, part)
        weights, row_max, rescale = softmax_step(scores, allowed, max_before)
        values = values_of(g)
        widened = jnp.concatenate([values, jnp.ones_like(values)], axis=1)
        acc = jnp.dot(weights, widened, preferred_element_type=jnp.float32)
        if rescale is not None:
            acc = acc_before * jnp.concatenate([rescale] * 2, axis=1) + acc
        store(g, part, row_max, acc)

    ahead_ref[...] = scores_of(0, 0)
    step = step if kv_heads % step == 0 else 1

    def some_heads(i, _):
        scores = ahead_ref[...]
        for number in range(step * PARTS):
            if number + 1 < step * PARTS:
                later = scores_of(i * step + (number + 1) // PARTS, (number + 1) % PARTS)
            else:
                later = scores_of(jnp.minimum((i + 1) * step, kv_heads - 1), 0)
            finish(i * step + number // PARTS, number % PARTS, scores)
            scores = later
        ahead_ref[...] = scores
        return 0

    lax.fori_loop(0, kv_heads // step, some_heads, 0)


def pick_kernel(place_ref, q_ref, out_ref, sem):
    copy = pltpu.make_async_copy(q_ref.at[:, block_of(1 - place_ref[2], out_ref.shape[1])], out_ref, sem)
    copy.start()
    copy.wait()


def own_kernel(place_ref, *refs, side):
    if side == 0:
        lengths_ref, q_ref, kv_ref, *refs = refs
        queries_ref, max_ref, acc_ref, lows_ref, info_ref, ahead_ref, q_side_ref, sem = refs
        fetch = pltpu.make_async_copy(q_ref.at[:, block_of(place_ref[2], q_side_ref.shape[1])], q_side_ref, sem)
        fetch.start()
    else:
        q_ref, kv_ref, _, _, _, lows_ref, queries_ref, max_ref, acc_ref, ahead_ref = refs
        q_side_ref = q_ref
    rows, wide = q_side_ref.shape
    kv_heads = kv_ref.shape[3] // HD
    heads = wide // (kv_heads * PARTS * HD)
    half = place_ref[2]
    first, other = place_ref[side], place_ref[1 - side]
    query_pos = first + lax.broadcasted_iota(jnp.int32, (rows, rows), 0)
    if side == 0:
        for i in range(2):
            lows_ref[i] = doc_start_rows(lengths_ref, place_ref[i], rows)
            low, high = doc_starts(lengths_ref, place_ref[i], place_ref[i] + rows - 1)
            info_ref[BOUNDS + 2 * i], info_ref[BOUNDS + 2 * i + 1] = low, high
        for i in range(BOUNDS):
            info_ref[i] = place_ref[i]
    lows = lows_ref[side]
    key_pos = positions(first, rows)
    diagonal = (key_pos >= lows) & (key_pos <= query_pos)
    earlier = positions(other, rows) >= lows
    if side == 0:
        fetch.wait()

    def at(g, part):
        return block_of((side * kv_heads + g) * PARTS + part, heads * rows)

    def place_queries(i, _):
        q = q_side_ref[:, block_of(i, heads * HD)]
        queries_ref[block_of(side * kv_heads * PARTS + i, heads * rows), :] = jnp.concatenate(
            [q[:, h * HD : (h + 1) * HD] for h in range(heads)], axis=0
        )
        return 0

    lax.fori_loop(0, kv_heads * PARTS, place_queries, 0)

    def store(g, part, row_max, acc):
        max_ref[at(g, part), :] = row_max
        acc_ref[at(g, part), :] = acc

    def work(blocks, allowed):
        def of(i, g):
            return jnp.concatenate([kv_ref[block, i, :, block_of(g, HD)] for block in blocks], axis=0)

        pipeline(
            kv_heads,
            ahead_ref.at[:, : len(blocks) * rows],
            allowed,
            lambda g, part: scores_for(queries_ref[at(g, part), :], of(0, g)),
            lambda g: of(1, g),
            lambda g, part: (None, None),
            store,
        )

    pl.when(half == side)(lambda: work([side], diagonal))
    pl.when(half != side)(lambda: work([1 - side, side], jnp.concatenate([earlier, diagonal], axis=1)))


def span_steps(place_ref, lows_ref, kv_refs, queries_ref, ahead_ref, numbers, side, load, store, step=2):
    rows = kv_refs[0].shape[2]
    kv_heads = kv_refs[0].shape[3] // HD
    key_starts = [(place_ref[3 + 2 * number], place_ref[4 + 2 * number]) for number in numbers]
    lo_first, lo_last = place_ref[BOUNDS + 2 * side], place_ref[BOUNDS + 2 * side + 1]
    needed = [jnp.maximum(*starts) + rows > lo_first for starts in key_starts]

    def at(g, part):
        return block_of((side * kv_heads + g) * PARTS + part, ahead_ref.shape[0])

    def work(chosen, masked):
        def of(i, g):
            parts = [kv_refs[n][block, i, :, block_of(g, HD)] for n in chosen for block in range(2)]
            return jnp.concatenate(parts, axis=0)

        allowed = None
        if masked:
            lows = lows_ref[side]
            allowed = jnp.concatenate(
                [positions(start, rows) >= lows for n in chosen for start in key_starts[n]], axis=1
            )
        pipeline(
            kv_heads,
            ahead_ref.at[:, : 2 * rows * len(chosen)],
            allowed,
            lambda g, part: scores_for(queries_ref[at(g, part), :], of(0, g)),
            lambda g: of(1, g),
            lambda g, part: load(at(g, part)),
            lambda g, part, row_max, acc: store(g, part, at(g, part), row_max, acc),
            step,
        )

    if len(numbers) == 1:
        whole = jnp.minimum(*key_starts[0]) >= lo_last
        pl.when(whole)(lambda: work([0], False))
        pl.when(needed[0] & jnp.logical_not(whole))(lambda: work([0], True))
        return needed[0]
    pl.when(needed[0] & needed[1])(lambda: work([0, 1], True))
    pl.when(needed[0] & jnp.logical_not(needed[1]))(lambda: work([0], True))
    pl.when(needed[1] & jnp.logical_not(needed[0]))(lambda: work([1], True))
    return needed[0] | needed[1]


def span_kernel(place_ref, lows_ref, *refs, numbers):
    kv_refs, (queries_ref, _, _, max_ref, acc_ref, ahead_ref) = refs[: len(numbers)], refs[len(numbers) :]

    def load(at):
        return max_ref[at, :], acc_ref[at, :]

    def store(g, part, at, row_max, acc):
        max_ref[at, :] = row_max
        acc_ref[at, :] = acc

    def one_side(side, _):
        span_steps(place_ref, lows_ref, kv_refs, queries_ref, ahead_ref, numbers, side, load, store)
        return 0

    lax.fori_loop(0, 2, one_side, 0)


def last_kernel(place_ref, lows_ref, *refs, numbers, side):
    kv_refs, (queries_ref, max_ref, acc_ref, out_ref, ahead_ref) = refs[: len(numbers)], refs[len(numbers) :]
    rows = kv_refs[0].shape[2]
    kv_heads = kv_refs[0].shape[3] // HD
    chunk = ahead_ref.shape[0]
    heads = chunk // rows

    def load(at):
        return max_ref[at, :], acc_ref[at, :]

    def finish(g, part, at, row_max, acc):
        finished = (acc[:, :HD] * (1.0 / acc[:, HD:])).astype(out_ref.dtype)
        out_ref[:, block_of(g * PARTS + part, heads * HD)] = jnp.concatenate(
            [finished[h * rows : (h + 1) * rows] for h in range(heads)], axis=1
        )

    needed = span_steps(place_ref, lows_ref, kv_refs, queries_ref, ahead_ref, numbers, side, load, finish, 4)

    @pl.when(jnp.logical_not(needed))
    def _():
        def one_head(g, _):
            for part in range(PARTS):
                finish(g, part, None, *load(block_of((side * kv_heads + g) * PARTS + part, chunk)))
            return 0

        lax.fori_loop(0, kv_heads, one_head, 0)


def join_kernel(place_ref, near_ref, far_ref, out_ref, sems):
    pieces = sems.shape[1]
    rows = far_ref.shape[0] // pieces
    copies = []
    for side, source in enumerate((near_ref, far_ref)):
        columns = block_of(place_ref[2] if side == 0 else 1 - place_ref[2], source.shape[1])
        for i in range(pieces):
            here = pl.ds(i * rows, rows)
            copies.append(pltpu.make_async_copy(source.at[here, :], out_ref.at[here, columns], sems.at[side, i]))
    for copy in copies:
        copy.start()
    for copy in copies:
        copy.wait()


def per_device(queries, keys, values, doc_lengths):
    rows, all_heads = queries.shape
    half_heads = all_heads // 2
    head_rows = (all_heads // HD) * rows
    half, span = lax.axis_index("head"), lax.axis_index("ctx")
    cores = lax.axis_size("head")
    place_in_group = lax.rem(span, REACH)

    nowhere = -2 * REACH

    def origin(kind):
        if kind == SHIFT:
            return span - REACH
        late = place_in_group >= REACH // 2
        from_place = place_in_group ^ (OPPOSITE if kind == SHIFT_OPPOSITE else kind)
        here = span - place_in_group + from_place
        if kind == SHIFT_OPPOSITE:
            return jnp.where(late, nowhere, here - REACH)
        if kind == OPPOSITE:
            return jnp.where(late, here, nowhere)
        return here - jnp.where(from_place > place_in_group, REACH, 0)

    parts = [(span * cores + half) * rows, (span * cores + 1 - half) * rows, half]
    for kinds in ROUNDS:
        start = jnp.where(half == 0, origin(kinds[0]), origin(kinds[1]))
        parts += [(start * cores + half) * rows, (start * cores + 1 - half) * rows]
    place = jnp.stack(parts).astype(jnp.int32)

    vmem = pl.BlockSpec(memory_space=pltpu.VMEM)
    smem = pl.BlockSpec(memory_space=pltpu.SMEM)
    anywhere = pl.BlockSpec(memory_space=pl.ANY)
    hbm = pl.BlockSpec(memory_space=pltpu.MemorySpace.HBM)
    placed_shape = jax.ShapeDtypeStruct((head_rows, HD), queries.dtype)
    max_shape = jax.ShapeDtypeStruct((head_rows, HD), jnp.float32)
    acc_shape = jax.ShapeDtypeStruct((head_rows, 2 * HD), jnp.float32)
    side_shape = jax.ShapeDtypeStruct((rows, half_heads), queries.dtype)
    common = dict(
        compiler_params=pltpu.CompilerParams(vmem_limit_bytes=24 * 1024 * 1024),
        cost_estimate=pl.CostEstimate(flops=0, bytes_accessed=0, transcendentals=0),
    )

    def heads_of(array, core):
        width = array.shape[1] // 2
        return lax.dynamic_slice_in_dim(array, core * width, width, 1)

    to_give = jnp.stack([heads_of(keys, 1 - half), heads_of(values, 1 - half)])
    given = to_other_core(to_give)
    given, queries = lax.optimization_barrier((given, queries))
    own = jnp.stack([jnp.stack([heads_of(keys, half), heads_of(values, half)]), given])
    arrived = [send_round(own, kinds) for kinds in ROUNDS[:2]]
    q_far = to_other_core(
        pl.pallas_call(
            pick_kernel,
            in_specs=[smem, hbm],
            out_specs=vmem,
            out_shape=side_shape,
            scratch_shapes=[pltpu.SemaphoreType.DMA],
            name="pick_queries",
            **common,
        )(place, queries)
    )

    chunk_heads = queries.shape[1] // keys.shape[1] // PARTS
    ahead = pltpu.VMEM((chunk_heads * rows, 4 * rows), jnp.float32)
    state_shapes = (placed_shape, max_shape, acc_shape)
    lows_shape = jax.ShapeDtypeStruct((2, rows, rows), jnp.int32)
    info_shape = jax.ShapeDtypeStruct((BOUNDS + 4,), jnp.int32)
    *state, lows, info = pl.pallas_call(
        functools.partial(own_kernel, side=0),
        in_specs=[smem, smem, hbm, vmem],
        out_specs=(vmem, vmem, vmem, vmem, smem),
        out_shape=state_shapes + (lows_shape, info_shape),
        scratch_shapes=[ahead, pltpu.VMEM((rows, half_heads), queries.dtype), pltpu.SemaphoreType.DMA],
        name="attend_own_near",
        **{**common, "cost_estimate": pl.CostEstimate(flops=10**11, bytes_accessed=0, transcendentals=0)},
    )(place, doc_lengths, queries, own)
    placed, row_max, acc = pl.pallas_call(
        functools.partial(own_kernel, side=1),
        in_specs=[smem] + [vmem] * 6,
        out_specs=(vmem, vmem, vmem),
        out_shape=state_shapes,
        input_output_aliases={3: 0, 4: 1, 5: 2},
        scratch_shapes=[ahead],
        name="attend_own_far",
        **common,
    )(info, q_far, own, *state, lows)

    def attend(kv, row_max, acc, number):
        return pl.pallas_call(
            functools.partial(span_kernel, numbers=tuple(range(number, number + len(kv)))),
            in_specs=[smem] + [vmem] * (len(kv) + 4),
            out_specs=(vmem, vmem),
            out_shape=(max_shape, acc_shape),
            input_output_aliases={len(kv) + 3: 0, len(kv) + 4: 1},
            scratch_shapes=[ahead],
            name="attend_spans",
            **common,
        )(info, lows, *kv, placed, row_max, acc)

    behind, acc = lax.optimization_barrier((arrived[0], acc))
    opposite, acc = lax.optimization_barrier((arrived[1], acc))

    def plane_round(number):
        sends = [jnp.where((place_in_group ^ kind) > place_in_group, own, behind) for kind in ROUNDS[number]]
        return jnp.where(half == 0, *sends)

    first = send_round(plane_round(2), ROUNDS[2])
    relayed = send_round(opposite, ROUNDS[3])
    row_max, acc = attend([behind, opposite], row_max, acc, 0)
    to_second, first, acc = lax.optimization_barrier((plane_round(4), first, acc))
    second = send_round(to_second, ROUNDS[4])
    row_max, acc = attend([first], row_max, acc, 2)

    last_args = (info, lows, relayed, second, placed, row_max, acc)
    def finish(side, name):
        return pl.pallas_call(
            functools.partial(last_kernel, numbers=(3, 4), side=side),
            in_specs=[smem] + [vmem] * 6,
            out_specs=vmem,
            out_shape=side_shape,
            scratch_shapes=[ahead],
            name=name,
            **common,
        )(*last_args)

    out_far = to_other_core(finish(1, "attend_last_far"))
    return pl.pallas_call(
        join_kernel,
        in_specs=[smem, vmem, vmem],
        out_specs=anywhere,
        out_shape=jax.ShapeDtypeStruct(queries.shape, queries.dtype),
        scratch_shapes=[pltpu.SemaphoreType.DMA((2, 4))],
        name="join_heads",
        **common,
    )(info, finish(0, "attend_last_near"), out_far)


def solution(mesh):
    placed = P(AXES, None)
    return jax.shard_map(
        per_device, mesh=mesh, in_specs=(placed, placed, placed, P()), out_specs=placed, check_vma=False
    )
```

```python
import functools
import math

import jax
import jax.numpy as jnp
from jax import lax
from jax.experimental import pallas as pl
from jax.experimental.pallas import tpu as pltpu
from jax.sharding import PartitionSpec as P

HD = 128
REACH = 4
NEVER = -1e30
SCORE_SCALE = HD ** (-0.5) * math.log2(math.e)
PARTS = 2
AXES = ("ctx", "head")
SHIFT, SHIFT_OPPOSITE, OPPOSITE = "shift", "shift opposite", REACH - 1
ROUNDS = ((SHIFT, SHIFT), (OPPOSITE, OPPOSITE), (1, 2), (SHIFT_OPPOSITE, SHIFT_OPPOSITE), (2, 1))
BOUNDS = 3 + 2 * len(ROUNDS)


def send_round(block, kinds):
    spans, cores = lax.axis_size("ctx"), lax.axis_size("head")
    pairs = []
    for s in range(spans):
        for core, kind in enumerate(kinds):
            if kind in (SHIFT, SHIFT_OPPOSITE):
                target = s + REACH
                if target >= spans or (kind == SHIFT_OPPOSITE and s % REACH >= REACH // 2):
                    continue
            else:
                target = s ^ kind
            pairs.append((s * cores + core, target * cores + core))
    return lax.ppermute(block, AXES, pairs)


def to_other_core(block):
    cores = lax.axis_size("head")
    return lax.ppermute(block, "head", [(h, cores - 1 - h) for h in range(cores)])


def doc_starts(lengths_ref, first, last):
    def one_doc(i, carry):
        start, lo_first, lo_last = carry
        start = start + lengths_ref[i]
        return start, jnp.where(start <= first, start, lo_first), jnp.where(start <= last, start, lo_last)

    zero = jnp.int32(0)
    _, lo_first, lo_last = lax.fori_loop(0, lengths_ref.shape[0], one_doc, (zero, zero, zero))
    return lo_first, lo_last


def doc_start_rows(lengths_ref, first_query, rows):
    pos = first_query + lax.broadcasted_iota(jnp.int32, (rows, rows), 0)

    def one_doc(i, carry):
        start, lo = carry
        start = start + lengths_ref[i]
        return start, jnp.where(start <= pos, start, lo)

    zero = jnp.zeros((rows, rows), jnp.int32)
    return lax.fori_loop(0, lengths_ref.shape[0], one_doc, (jnp.int32(0), zero))[1]


def block_of(at, size):
    return pl.ds(pl.multiple_of(at * size, size), size)


def positions(start, rows):
    return start + lax.broadcasted_iota(jnp.int32, (rows, rows), 1)


def softmax_step(scores, allowed, max_before):
    if allowed is not None:
        allowed = jnp.concatenate([allowed] * (scores.shape[0] // allowed.shape[0]), axis=0)
        scores = jnp.where(allowed, scores, NEVER)
    row_max = jnp.broadcast_to(jnp.max(scores, axis=1, keepdims=True), (scores.shape[0], HD))
    rescale = None
    if max_before is not None:
        row_max = jnp.maximum(max_before, row_max)
        rescale = jnp.exp2((max_before - row_max) * SCORE_SCALE)
    shift = jnp.concatenate([row_max] * (scores.shape[1] // HD), axis=1)
    return jnp.exp2((scores - shift) * SCORE_SCALE).astype(jnp.bfloat16), row_max, rescale


def scores_for(queries, keys):
    return lax.dot_general(queries, keys, (((1,), (1,)), ((), ())), preferred_element_type=jnp.float32)


def pipeline(kv_heads, ahead_ref, allowed, scores_of, values_of, before_of, store):
    def finish(g, part, scores):
        max_before, acc_before = before_of(g, part)
        weights, row_max, rescale = softmax_step(scores, allowed, max_before)
        values = values_of(g)
        widened = jnp.concatenate([values, jnp.ones_like(values)], axis=1)
        acc = jnp.dot(weights, widened, preferred_element_type=jnp.float32)
        if rescale is not None:
            acc = acc_before * jnp.concatenate([rescale] * 2, axis=1) + acc
        store(g, part, row_max, acc)

    ahead_ref[...] = scores_of(0, 0)
    step = 2 if kv_heads % 2 == 0 else 1

    def some_heads(i, _):
        scores = ahead_ref[...]
        for number in range(step * PARTS):
            if number + 1 < step * PARTS:
                later = scores_of(i * step + (number + 1) // PARTS, (number + 1) % PARTS)
            else:
                later = scores_of(jnp.minimum((i + 1) * step, kv_heads - 1), 0)
            finish(i * step + number // PARTS, number % PARTS, scores)
            scores = later
        ahead_ref[...] = scores
        return 0

    lax.fori_loop(0, kv_heads // step, some_heads, 0)


def pick_kernel(place_ref, q_ref, out_ref, sem):
    copy = pltpu.make_async_copy(q_ref.at[:, block_of(1 - place_ref[2], out_ref.shape[1])], out_ref, sem)
    copy.start()
    copy.wait()


def own_kernel(place_ref, *refs, side):
    if side == 0:
        lengths_ref, q_ref, kv_ref, *refs = refs
        queries_ref, max_ref, acc_ref, lows_ref, info_ref, ahead_ref, q_side_ref, sem = refs
        fetch = pltpu.make_async_copy(q_ref.at[:, block_of(place_ref[2], q_side_ref.shape[1])], q_side_ref, sem)
        fetch.start()
    else:
        q_ref, kv_ref, _, _, _, lows_ref, queries_ref, max_ref, acc_ref, ahead_ref = refs
        q_side_ref = q_ref
    rows, wide = q_side_ref.shape
    kv_heads = kv_ref.shape[3] // HD
    heads = wide // (kv_heads * PARTS * HD)
    half = place_ref[2]
    first, other = place_ref[side], place_ref[1 - side]
    query_pos = first + lax.broadcasted_iota(jnp.int32, (rows, rows), 0)
    if side == 0:
        for i in range(2):
            lows_ref[i] = doc_start_rows(lengths_ref, place_ref[i], rows)
            low, high = doc_starts(lengths_ref, place_ref[i], place_ref[i] + rows - 1)
            info_ref[BOUNDS + 2 * i], info_ref[BOUNDS + 2 * i + 1] = low, high
        for i in range(BOUNDS):
            info_ref[i] = place_ref[i]
    lows = lows_ref[side]
    key_pos = positions(first, rows)
    diagonal = (key_pos >= lows) & (key_pos <= query_pos)
    earlier = positions(other, rows) >= lows
    if side == 0:
        fetch.wait()

    def at(g, part):
        return block_of((side * kv_heads + g) * PARTS + part, heads * rows)

    def place_queries(i, _):
        q = q_side_ref[:, block_of(i, heads * HD)]
        queries_ref[block_of(side * kv_heads * PARTS + i, heads * rows), :] = jnp.concatenate(
            [q[:, h * HD : (h + 1) * HD] for h in range(heads)], axis=0
        )
        return 0

    lax.fori_loop(0, kv_heads * PARTS, place_queries, 0)

    def store(g, part, row_max, acc):
        max_ref[at(g, part), :] = row_max
        acc_ref[at(g, part), :] = acc

    def work(blocks, allowed):
        def of(i, g):
            return jnp.concatenate([kv_ref[block, i, :, block_of(g, HD)] for block in blocks], axis=0)

        pipeline(
            kv_heads,
            ahead_ref.at[:, : len(blocks) * rows],
            allowed,
            lambda g, part: scores_for(queries_ref[at(g, part), :], of(0, g)),
            lambda g: of(1, g),
            lambda g, part: (None, None),
            store,
        )

    pl.when(half == side)(lambda: work([side], diagonal))
    pl.when(half != side)(lambda: work([1 - side, side], jnp.concatenate([earlier, diagonal], axis=1)))


def span_steps(place_ref, lows_ref, kv_refs, queries_ref, ahead_ref, numbers, side, load, store):
    rows = kv_refs[0].shape[2]
    kv_heads = kv_refs[0].shape[3] // HD
    key_starts = [(place_ref[3 + 2 * number], place_ref[4 + 2 * number]) for number in numbers]
    lo_first, lo_last = place_ref[BOUNDS + 2 * side], place_ref[BOUNDS + 2 * side + 1]
    needed = [jnp.maximum(*starts) + rows > lo_first for starts in key_starts]

    def at(g, part):
        return block_of((side * kv_heads + g) * PARTS + part, ahead_ref.shape[0])

    def work(chosen, masked):
        def of(i, g):
            parts = [kv_refs[n][block, i, :, block_of(g, HD)] for n in chosen for block in range(2)]
            return jnp.concatenate(parts, axis=0)

        allowed = None
        if masked:
            lows = lows_ref[side]
            allowed = jnp.concatenate(
                [positions(start, rows) >= lows for n in chosen for start in key_starts[n]], axis=1
            )
        pipeline(
            kv_heads,
            ahead_ref.at[:, : 2 * rows * len(chosen)],
            allowed,
            lambda g, part: scores_for(queries_ref[at(g, part), :], of(0, g)),
            lambda g: of(1, g),
            lambda g, part: load(at(g, part)),
            lambda g, part, row_max, acc: store(g, part, at(g, part), row_max, acc),
        )

    if len(numbers) == 1:
        whole = jnp.minimum(*key_starts[0]) >= lo_last
        pl.when(whole)(lambda: work([0], False))
        pl.when(needed[0] & jnp.logical_not(whole))(lambda: work([0], True))
        return needed[0]
    pl.when(needed[0] & needed[1])(lambda: work([0, 1], True))
    pl.when(needed[0] & jnp.logical_not(needed[1]))(lambda: work([0], True))
    pl.when(needed[1] & jnp.logical_not(needed[0]))(lambda: work([1], True))
    return needed[0] | needed[1]


def span_kernel(place_ref, lows_ref, *refs, numbers):
    kv_refs, (queries_ref, _, _, max_ref, acc_ref, ahead_ref) = refs[: len(numbers)], refs[len(numbers) :]

    def load(at):
        return max_ref[at, :], acc_ref[at, :]

    def store(g, part, at, row_max, acc):
        max_ref[at, :] = row_max
        acc_ref[at, :] = acc

    def one_side(side, _):
        span_steps(place_ref, lows_ref, kv_refs, queries_ref, ahead_ref, numbers, side, load, store)
        return 0

    lax.fori_loop(0, 2, one_side, 0)


def last_kernel(place_ref, lows_ref, *refs, numbers, side):
    kv_refs, (queries_ref, max_ref, acc_ref, out_ref, ahead_ref) = refs[: len(numbers)], refs[len(numbers) :]
    rows = kv_refs[0].shape[2]
    kv_heads = kv_refs[0].shape[3] // HD
    chunk = ahead_ref.shape[0]
    heads = chunk // rows

    def load(at):
        return max_ref[at, :], acc_ref[at, :]

    def finish(g, part, at, row_max, acc):
        finished = (acc[:, :HD] * (1.0 / acc[:, HD:])).astype(out_ref.dtype)
        out_ref[:, block_of(g * PARTS + part, heads * HD)] = jnp.concatenate(
            [finished[h * rows : (h + 1) * rows] for h in range(heads)], axis=1
        )

    needed = span_steps(place_ref, lows_ref, kv_refs, queries_ref, ahead_ref, numbers, side, load, finish)

    @pl.when(jnp.logical_not(needed))
    def _():
        def one_head(g, _):
            for part in range(PARTS):
                finish(g, part, None, *load(block_of((side * kv_heads + g) * PARTS + part, chunk)))
            return 0

        lax.fori_loop(0, kv_heads, one_head, 0)


def join_kernel(place_ref, near_ref, far_ref, out_ref, sems):
    pieces = sems.shape[1]
    rows = far_ref.shape[0] // pieces
    copies = []
    for side, source in enumerate((near_ref, far_ref)):
        columns = block_of(place_ref[2] if side == 0 else 1 - place_ref[2], source.shape[1])
        for i in range(pieces):
            here = pl.ds(i * rows, rows)
            copies.append(pltpu.make_async_copy(source.at[here, :], out_ref.at[here, columns], sems.at[side, i]))
    for copy in copies:
        copy.start()
    for copy in copies:
        copy.wait()


def per_device(queries, keys, values, doc_lengths):
    rows, all_heads = queries.shape
    half_heads = all_heads // 2
    head_rows = (all_heads // HD) * rows
    half, span = lax.axis_index("head"), lax.axis_index("ctx")
    cores = lax.axis_size("head")
    place_in_group = lax.rem(span, REACH)

    nowhere = -2 * REACH

    def origin(kind):
        if kind == SHIFT:
            return span - REACH
        late = place_in_group >= REACH // 2
        from_place = place_in_group ^ (OPPOSITE if kind == SHIFT_OPPOSITE else kind)
        here = span - place_in_group + from_place
        if kind == SHIFT_OPPOSITE:
            return jnp.where(late, nowhere, here - REACH)
        if kind == OPPOSITE:
            return jnp.where(late, here, nowhere)
        return here - jnp.where(from_place > place_in_group, REACH, 0)

    parts = [(span * cores + half) * rows, (span * cores + 1 - half) * rows, half]
    for kinds in ROUNDS:
        start = jnp.where(half == 0, origin(kinds[0]), origin(kinds[1]))
        parts += [(start * cores + half) * rows, (start * cores + 1 - half) * rows]
    place = jnp.stack(parts).astype(jnp.int32)

    vmem = pl.BlockSpec(memory_space=pltpu.VMEM)
    smem = pl.BlockSpec(memory_space=pltpu.SMEM)
    anywhere = pl.BlockSpec(memory_space=pl.ANY)
    hbm = pl.BlockSpec(memory_space=pltpu.MemorySpace.HBM)
    placed_shape = jax.ShapeDtypeStruct((head_rows, HD), queries.dtype)
    max_shape = jax.ShapeDtypeStruct((head_rows, HD), jnp.float32)
    acc_shape = jax.ShapeDtypeStruct((head_rows, 2 * HD), jnp.float32)
    side_shape = jax.ShapeDtypeStruct((rows, half_heads), queries.dtype)
    common = dict(
        compiler_params=pltpu.CompilerParams(vmem_limit_bytes=24 * 1024 * 1024),
        cost_estimate=pl.CostEstimate(flops=0, bytes_accessed=0, transcendentals=0),
    )

    def heads_of(array, core):
        width = array.shape[1] // 2
        return lax.dynamic_slice_in_dim(array, core * width, width, 1)

    to_give = jnp.stack([heads_of(keys, 1 - half), heads_of(values, 1 - half)])
    given = to_other_core(to_give)
    given, queries = lax.optimization_barrier((given, queries))
    own = jnp.stack([jnp.stack([heads_of(keys, half), heads_of(values, half)]), given])
    arrived = [send_round(own, kinds) for kinds in ROUNDS[:2]]
    q_far = to_other_core(
        pl.pallas_call(
            pick_kernel,
            in_specs=[smem, hbm],
            out_specs=vmem,
            out_shape=side_shape,
            scratch_shapes=[pltpu.SemaphoreType.DMA],
            name="pick_queries",
            **common,
        )(place, queries)
    )

    chunk_heads = queries.shape[1] // keys.shape[1] // PARTS
    ahead = pltpu.VMEM((chunk_heads * rows, 4 * rows), jnp.float32)
    state_shapes = (placed_shape, max_shape, acc_shape)
    lows_shape = jax.ShapeDtypeStruct((2, rows, rows), jnp.int32)
    info_shape = jax.ShapeDtypeStruct((BOUNDS + 4,), jnp.int32)
    *state, lows, info = pl.pallas_call(
        functools.partial(own_kernel, side=0),
        in_specs=[smem, smem, hbm, vmem],
        out_specs=(vmem, vmem, vmem, vmem, smem),
        out_shape=state_shapes + (lows_shape, info_shape),
        scratch_shapes=[ahead, pltpu.VMEM((rows, half_heads), queries.dtype), pltpu.SemaphoreType.DMA],
        name="attend_own_near",
        **{**common, "cost_estimate": pl.CostEstimate(flops=10**11, bytes_accessed=0, transcendentals=0)},
    )(place, doc_lengths, queries, own)
    placed, row_max, acc = pl.pallas_call(
        functools.partial(own_kernel, side=1),
        in_specs=[smem] + [vmem] * 6,
        out_specs=(vmem, vmem, vmem),
        out_shape=state_shapes,
        input_output_aliases={3: 0, 4: 1, 5: 2},
        scratch_shapes=[ahead],
        name="attend_own_far",
        **common,
    )(info, q_far, own, *state, lows)

    def attend(kv, row_max, acc, number):
        return pl.pallas_call(
            functools.partial(span_kernel, numbers=tuple(range(number, number + len(kv)))),
            in_specs=[smem] + [vmem] * (len(kv) + 4),
            out_specs=(vmem, vmem),
            out_shape=(max_shape, acc_shape),
            input_output_aliases={len(kv) + 3: 0, len(kv) + 4: 1},
            scratch_shapes=[ahead],
            name="attend_spans",
            **common,
        )(info, lows, *kv, placed, row_max, acc)

    behind, acc = lax.optimization_barrier((arrived[0], acc))
    opposite, acc = lax.optimization_barrier((arrived[1], acc))

    def plane_round(number):
        sends = [jnp.where((place_in_group ^ kind) > place_in_group, own, behind) for kind in ROUNDS[number]]
        return jnp.where(half == 0, *sends)

    first = send_round(plane_round(2), ROUNDS[2])
    relayed = send_round(opposite, ROUNDS[3])
    row_max, acc = attend([behind, opposite], row_max, acc, 0)
    to_second, first, acc = lax.optimization_barrier((plane_round(4), first, acc))
    second = send_round(to_second, ROUNDS[4])
    row_max, acc = attend([first], row_max, acc, 2)

    last_args = (info, lows, relayed, second, placed, row_max, acc)
    def finish(side, name):
        return pl.pallas_call(
            functools.partial(last_kernel, numbers=(3, 4), side=side),
            in_specs=[smem] + [vmem] * 6,
            out_specs=vmem,
            out_shape=side_shape,
            scratch_shapes=[ahead],
            name=name,
            **common,
        )(*last_args)

    out_far = to_other_core(finish(1, "attend_last_far"))
    return pl.pallas_call(
        join_kernel,
        in_specs=[smem, vmem, vmem],
        out_specs=anywhere,
        out_shape=jax.ShapeDtypeStruct(queries.shape, queries.dtype),
        scratch_shapes=[pltpu.SemaphoreType.DMA((2, 8))],
        name="join_heads",
        **common,
    )(info, finish(0, "attend_last_near"), out_far)


def solution(mesh):
    placed = P(AXES, None)
    return jax.shard_map(
        per_device, mesh=mesh, in_specs=(placed, placed, placed, P()), out_specs=placed, check_vma=False
    )
```
